32 devices in a mesh: rows: 8 (over z, y), feat: 4 (over x, core).
Axes of the slice: x: 2, y: 2, z: 4, core: 2. Of those that a mesh axis runs over, the one named last changes fastest.
Arguments:
- raw_rows: float32 [16384, 100], P('rows', 'feat'), may hold values from -400 to 400
- enc_weight: bfloat16 [100, 512], replicated, may hold values from -0.625 to 0.625
- enc_bias: float32 [512], replicated, may hold values from -3 to 3
- label_table: bfloat16 [10, 512], replicated, may hold values from -5 to 5
- w_query: bfloat16 [512, 512], replicated, may hold values from -0.25 to 0.25
- b_query: float32 [512], replicated, may hold values from -2 to 2
- w_key: bfloat16 [512, 512], replicated, may hold values from -0.25 to 0.25
- w_value: bfloat16 [512, 512], replicated, may hold values from -0.25 to 0.25
- b_value: float32 [512], replicated, may hold values from -2 to 2
- w_out: bfloat16 [512, 512], replicated, may hold values from -1 to 1
- b_out: float32 [512], replicated, may hold values from -2 to 2
- gain_one: float32 [512], replicated, may hold values from 0.5 to 1.5
- shift_one: float32 [512], replicated, may hold values from -2 to 2
- w_in: bfloat16 [512, 1024], replicated, may hold values from -0.25 to 0.25
- b_in: float32 [1024], replicated, may hold values from -2 to 2
- w_back: bfloat16 [1024, 512], replicated, may hold values from -0.1875 to 0.1875
- b_back: float32 [512], replicated, may hold values from -2 to 2
- gain_two: float32 [512], replicated, may hold values from 0.5 to 1.5
- shift_two: float32 [512], replicated, may hold values from -2 to 2
- members: int32 [64, 1100], P(('rows', 'feat')), may hold values from 0 to 16383, as said below
- labels: int32 [64, 1000], P(('rows', 'feat')), may hold values from 0 to 9
- queries: int32 [64], P(('rows', 'feat')), may hold values from 1 to 100
- cotangent: float32 [64, 1100, 512], P(('rows', 'feat')), may hold values from -6 to 6
Outputs:
- layer_out: bfloat16 [64, 1100, 512], P(('rows', 'feat'))
- raw_grad: float32 [16384, 100], P('rows', 'feat')
- grad_enc_weight: float32 [100, 512], replicated
- grad_enc_bias: float32 [512], replicated
- grad_label_table: float32 [10, 512], replicated
- grad_w_query: float32 [512, 512], replicated
- grad_b_query: float32 [512], replicated
- grad_w_key: float32 [512, 512], replicated
- grad_w_value: float32 [512, 512], replicated
- grad_b_value: float32 [512], replicated
- grad_w_out: float32 [512, 512], replicated
- grad_b_out: float32 [512], replicated
- grad_gain_one: float32 [512], replicated
- grad_shift_one: float32 [512], replicated
- grad_w_in: float32 [512, 1024], replicated
- grad_b_in: float32 [1024], replicated
- grad_w_back: float32 [1024, 512], replicated
- grad_b_back: float32 [512], replicated
- grad_gain_two: float32 [512], replicated
- grad_shift_two: float32 [512], replicated
The draws below stay inside these ranges and needn't reach their ends.
Inputs may be any that keep to these rules, and one draw needn't show every extreme that they name: members[n, j] names a table row. Take the neighbourhoods in blocks of 2 in order, block b; every row named in block b has (row // 512) % 4 == b % 4; within one block at most 275 slots name rows of one group of 2048 consecutive rows, and some group is named exactly 275 times.
All inputs are finite; a program needn't handle non-finite values.
Results may differ from the reference program's by a relative error of at most 0.012.
Values may be sent and summed in bfloat16 or wider, within the bound.
No kernel may reach another device: no remote copies, remote signals or barrier semaphores. Data moves between devices by JAX's collectives and lax.ppermute only.
A program may use at most 192 MiB of HBM per device.

```python
import math
import jax
import jax.numpy as jnp
from jax import lax

F = 100
D = 512
HEADS = 4
FF = 1024
CLASSES = 10
CTX = 1000
QMAX = 100
NB_DEV = 2
TOK_DEV = 512
HEAD = 128
SLOTS = 1100
NBH = 64
TOKENS = 16384
CAP = 275
N_ROWS = 8
N_FEAT = 4
DEVICES = 32


def draw_raw_rows(key, part):
    key = jax.random.fold_in(key, 7)
    keys_row = jax.random.split(key, 4)
    position = jnp.arange(TOKENS, dtype=jnp.float32)[:, None] / TOKENS
    rising = 1.0 + 2.0 * position
    row_scale = jnp.exp(jax.random.uniform(keys_row[0], (TOKENS, 1), minval=0.0, maxval=math.log(4.0)))
    col_scale = jnp.exp(jax.random.uniform(keys_row[1], (1, F), minval=math.log(0.5), maxval=math.log(5.0)))
    col_shift = 2.0 * jnp.clip(jax.random.normal(keys_row[2], (1, F)), -3.0, 3.0)
    noise = jnp.clip(jax.random.normal(keys_row[3], (TOKENS, F)), -4.0, 4.0)
    return (col_shift + col_scale * rising * row_scale * noise).astype(jnp.float32)


def draw_members(key, part):
    key = jax.random.fold_in(key, 13)
    per_device = NB_DEV * SLOTS
    device_keys = jax.random.split(key, DEVICES)
    feat_slots = jnp.arange(DEVICES, dtype=jnp.int32) % N_FEAT

    def one_device(dev_key, feat_slot):
        order_key, row_key = jax.random.split(dev_key)
        src_order = jax.random.permutation(order_key, N_ROWS * CAP)[:per_device] // CAP
        local_row = jax.random.randint(row_key, (per_device,), 0, TOK_DEV)
        return ((src_order.astype(jnp.int32) * N_FEAT + feat_slot) * TOK_DEV + local_row).astype(jnp.int32)
    return jax.vmap(one_device)(device_keys, feat_slots).reshape(NBH, SLOTS)


def draw_cotangent(key, part):
    key = jax.random.fold_in(key, 19)
    keys_cot = jax.random.split(key, 2)
    offset_unit = jnp.clip(jax.random.normal(keys_cot[0], (1, 1, D)), -3.0, 3.0)
    noise = jnp.clip(jax.random.normal(keys_cot[1], (NBH, SLOTS, D)), -4.0, 4.0)
    offset = 0.5 * offset_unit
    return (offset + noise).astype(jnp.float32)


def set_ends(values, rng, least, largest):
    index_at = [jax.random.randint(jax.random.fold_in(rng, axis), (), 0, length) for axis, length in enumerate(values.shape)]
    main_axis = values.shape.index(max(values.shape))
    neighbour = index_at[:main_axis] + [(index_at[main_axis] + 1) % values.shape[main_axis]] + index_at[main_axis + 1:]
    return values.at[tuple(index_at)].set(least).at[tuple(neighbour)].set(largest)


def gaussian(own_key, shape, deviation, most, kind=jnp.bfloat16):
    values = deviation * jax.random.normal(own_key, shape, jnp.float32)
    return jnp.clip(values, min=-most, max=most).astype(kind)


def setup_inputs(seed: int = 0) -> dict:
    seeds = jax.random.split(jax.random.key(seed), 24)
    return {
        "raw_rows": draw_raw_rows(jax.random.fold_in(seeds[23], 71), 0),
        "enc_weight": gaussian(seeds[1], (F, D), F ** -0.5, 0.625),
        "enc_bias": gaussian(seeds[2], (D,), 0.5, 3.0, jnp.float32),
        "label_table": gaussian(seeds[3], (CLASSES, D), 1.0, 5.0),
        "w_query": gaussian(seeds[4], (D, D), D ** -0.5, 0.25),
        "b_query": gaussian(seeds[5], (D,), 0.3, 2.0, jnp.float32),
        "w_key": gaussian(seeds[6], (D, D), D ** -0.5, 0.25),
        "w_value": gaussian(seeds[7], (D, D), D ** -0.5, 0.25),
        "b_value": gaussian(seeds[8], (D,), 0.3, 2.0, jnp.float32),
        "w_out": gaussian(seeds[9], (D, D), (D // 16) ** -0.5, 1.0),
        "b_out": gaussian(seeds[10], (D,), 0.3, 2.0, jnp.float32),
        "gain_one": jnp.clip(1.0 + 0.1 * jax.random.normal(seeds[11], (D,), jnp.float32), 0.5, 1.5),
        "shift_one": gaussian(seeds[12], (D,), 0.3, 2.0, jnp.float32),
        "w_in": gaussian(seeds[13], (D, FF), D ** -0.5, 0.25),
        "b_in": gaussian(seeds[14], (FF,), 0.3, 2.0, jnp.float32),
        "w_back": gaussian(seeds[15], (FF, D), FF ** -0.5, 0.1875),
        "b_back": gaussian(seeds[16], (D,), 0.3, 2.0, jnp.float32),
        "gain_two": jnp.clip(1.0 + 0.1 * jax.random.normal(seeds[17], (D,), jnp.float32), 0.5, 1.5),
        "shift_two": gaussian(seeds[18], (D,), 0.3, 2.0, jnp.float32),
        "members": draw_members(jax.random.fold_in(seeds[23], 71), 0),
        "labels": set_ends(jax.random.randint(seeds[20], (NBH, CTX), 0, CLASSES), jax.random.fold_in(seeds[20], 1), 0, CLASSES - 1).astype(jnp.int32),
        "queries": set_ends(jax.random.randint(seeds[21], (NBH,), 1, QMAX + 1), jax.random.fold_in(seeds[21], 1), 1, QMAX).astype(jnp.int32),
        "cotangent": draw_cotangent(jax.random.fold_in(seeds[23], 71), 0),
    }


@jax.custom_vjp
def low(v):
    return lax.optimization_barrier(v.astype(jnp.bfloat16)).astype(jnp.float32)

@jax.custom_vjp
def low_back(v):
    return v

def low_keep(v):
    return (low(v), None)

def low_pass(kept, grad):
    return (grad,)

def back_keep(v):
    return (v, None)

def back_low(kept, grad):
    return (low(grad),)
low.defvjp(low_keep, low_pass)
low_back.defvjp(back_keep, back_low)
epsilon = 1e-05

def matmul_hi(left, right):
    return jnp.dot(left, right, preferred_element_type=jnp.float32, precision=lax.Precision.HIGHEST)

def norm_apply(values, gain, shift):
    centre = lax.optimization_barrier(jnp.mean(values, -1, keepdims=True))
    offset = values - centre
    second = lax.optimization_barrier(jnp.mean(offset * offset, -1, keepdims=True))
    return offset * lax.rsqrt(second + epsilon) * gain + shift

def layer_ref(stream, w_query, b_query, w_key, w_value, b_value, w_out, b_out, gain_one, shift_one, w_in, b_in, w_back, b_back, gain_two, shift_two):
    stream_low = low(stream)
    context = stream_low[:CTX]
    query_all = low_back(matmul_hi(stream_low, w_query) + b_query)
    keys_all = low_back(matmul_hi(context, w_key))
    values_all = low_back(matmul_hi(context, w_value) + b_value)
    query_low = low(query_all).reshape(SLOTS, HEADS, HEAD)
    keys_low = low(keys_all).reshape(CTX, HEADS, HEAD)
    values_low = low(values_all).reshape(CTX, HEADS, HEAD)
    scores = low_back(jnp.einsum('shd,chd->hsc', query_low, keys_low, precision=lax.Precision.HIGHEST) / math.sqrt(HEAD))
    prob_values = low(jax.nn.softmax(scores, axis=-1))
    mixed_heads = low_back(jnp.einsum('hsc,chd->shd', prob_values, values_low, precision=lax.Precision.HIGHEST).reshape(SLOTS, D))
    attended = low_back(matmul_hi(low(mixed_heads), w_out) + b_out)
    normed = norm_apply(stream + attended, gain_one, shift_one)
    hidden = low_back(matmul_hi(low(normed), w_in) + b_in)
    branch = low_back(matmul_hi(low(jax.nn.gelu(hidden)), w_back) + b_back)
    return norm_apply(normed + branch, gain_two, shift_two)

def reference(raw_rows, enc_weight, enc_bias, label_table, w_query, b_query, w_key, w_value, b_value, w_out, b_out, gain_one, shift_one, w_in, b_in, w_back, b_back, gain_two, shift_two, members, labels, queries, cotangent):
    floats = tuple((item.astype(jnp.float32) for item in (enc_weight, enc_bias, label_table, w_query, b_query, w_key, w_value, b_value, w_out, b_out, gain_one, shift_one, w_in, b_in, w_back, b_back, gain_two, shift_two)))
    live_mask = (jnp.arange(SLOTS, dtype=jnp.int32)[None, :] < (CTX + queries)[:, None]).astype(jnp.float32)
    label_hot = (labels[:, :, None] == jnp.arange(CLASSES, dtype=jnp.int32)[None, None, :]).astype(jnp.float32)
    flat_members = members.reshape(-1).astype(jnp.int32)

    def forward(raw, enc_w, enc_b, table, *layer_weights):
        col_mean = lax.optimization_barrier(jnp.mean(raw, 0))
        spread = lax.optimization_barrier(jnp.mean(raw * raw, 0)) - col_mean * col_mean
        standard = (raw - col_mean) * lax.rsqrt(spread + epsilon)
        embedded = matmul_hi(low(standard), enc_w) + enc_b
        slot_values = low_back(low(embedded[flat_members])).reshape(NBH, SLOTS, D)
        label_add = jnp.einsum('nci,id->ncd', label_hot, table, precision=lax.Precision.HIGHEST)
        stream_in = jnp.concatenate([slot_values[:, :CTX] + label_add, slot_values[:, CTX:]], 1)

        def one_block(item):
            stream, alive_rows = item
            return alive_rows[:, None] * layer_ref(stream, *layer_weights)
        return lax.map(jax.checkpoint(one_block), (stream_in, live_mask))
    result, pull_back = jax.vjp(forward, raw_rows, *floats)
    grads_all = pull_back(cotangent)
    return (result.astype(jnp.bfloat16), grads_all[0], grads_all[1], grads_all[2], grads_all[3], grads_all[4], grads_all[5], grads_all[6], grads_all[7], grads_all[8], grads_all[9], grads_all[10], grads_all[11], grads_all[12], grads_all[13], grads_all[14], grads_all[15], grads_all[16], grads_all[17], grads_all[18])
```

```python
import functools
import math

import jax
import jax.numpy as jnp
from jax import lax
from jax.experimental import pallas as pl
from jax.experimental.pallas import tpu as pltpu
from jax.sharding import PartitionSpec as P

HEADS = 4
LANES = 128
epsilon = 1e-05
CHUNKS = 32
VMEM_LIMIT = 60 * 1024 * 1024
f32 = jnp.float32
bf16 = jnp.bfloat16


def dot(left, right):
    return jnp.dot(left, right, preferred_element_type=f32)


def dot_nt(left, right):
    return lax.dot_general(left, right, (((1,), (1,)), ((), ())), preferred_element_type=f32)


def dot_tn(left, right):
    return lax.dot_general(left, right, (((0,), (0,)), ((), ())), preferred_element_type=f32)


def round_up(value, unit):
    return -(-value // unit) * unit


def row_chunks(span):
    for parts in (3, 2, 1):
        if span % (16 * parts) == 0:
            return parts
    return 1


def params(*names):
    return pltpu.CompilerParams(vmem_limit_bytes=VMEM_LIMIT, dimension_semantics=("arbitrary",) * len(names))


def embed(feats, w_feat, w_mark, b_enc):
    slots = (dot(feats, w_feat[...]) + b_enc[...]).astype(bf16)
    return slots.astype(f32) + dot(feats, w_mark[...])


def attend_kernel(span, ctx_len, ctx_pad, feat_total, classes, parts,
                  ids, groups, mark, w_feat, w_mark, b_enc, w_query, b_query, w_key, w_value, b_value,
                  feats_o, low_o, q_o, k_o, v_o, e_o, inv_o, mix_o, table, rows_f):
    block = pl.program_id(0)
    head = pl.program_id(1)
    pad = feats_o.shape[1]
    step = pad // parts

    @pl.when((head == 0) & (block == 0))
    def _():
        count, deep, own = groups.shape

        def unfold(g, _):
            piece = jnp.concatenate([groups[g].astype(f32), jnp.zeros((LANES - deep, own), f32)], 0)
            table[pl.ds(pl.multiple_of(g * own, own), own), :] = piece.T
            return 0

        lax.fori_loop(0, count, unfold, 0)

    @pl.when(head == 0)
    def _():
        rows_f[pad - 16:, :] = jnp.zeros((16, LANES), f32)

        def fetch(i, _):
            for u in range(10):
                at = i * 10 + u
                rows_f[pl.ds(at, 1), :] = table[pl.ds(ids[block, at], 1), :]
            return 0

        lax.fori_loop(0, span // 10, fetch, 0)
        for at in range(span // 10 * 10, span):
            rows_f[pl.ds(at, 1), :] = table[pl.ds(ids[block, at], 1), :]

        def project(c, _):
            rows = pl.ds(pl.multiple_of(c * step, 16), step)
            lane = lax.broadcasted_iota(jnp.int32, (step, LANES), 1)
            hot = (lane == mark[0, rows, :] + feat_total) | (lane == feat_total + classes)
            feats = jnp.where(lane < feat_total, rows_f[rows, :], hot.astype(f32)).astype(bf16)
            feats_o[0, rows, :] = feats
            low = embed(feats, w_feat, w_mark, b_enc).astype(bf16)
            low_o[0, rows, :] = low
            q_o[0, rows, :] = (dot(low, w_query[...]) + b_query[...]).astype(bf16)
            k_o[0, rows, :] = dot(low, w_key[...]).astype(bf16)
            v_o[0, rows, :] = (dot(low, w_value[...]) + b_value[...]).astype(bf16)
            return 0

        lax.fori_loop(0, parts, project, 0)

    width = q_o.shape[2] // HEADS
    factor = math.log2(math.e) / math.sqrt(width)
    cols = pl.ds(pl.multiple_of(head * width, LANES), width)
    keys = k_o[0, :ctx_pad, cols]
    vals = jnp.concatenate([v_o[0, :ctx_pad, cols], jnp.ones((ctx_pad, width), bf16)], 1)
    edge = ctx_len // LANES * LANES
    for c in range(parts):
        rows = slice(c * step, (c + 1) * step)
        scores = dot_nt(q_o[0, rows, cols], keys)
        head_part = scores[:, :edge]
        most = jnp.max(head_part, 1, keepdims=True)
        if edge < ctx_pad:
            lane = lax.broadcasted_iota(jnp.int32, (step, ctx_pad - edge), 1)
            tail_part = jnp.where(lane < ctx_len - edge, scores[:, edge:], -1e30)
            most = jnp.maximum(most, jnp.max(tail_part, 1, keepdims=True))
            e_o[0, 0, rows, edge:] = jnp.exp2((tail_part - most) * factor).astype(bf16)
        e_o[0, 0, rows, :edge] = jnp.exp2((head_part - most) * factor).astype(bf16)
        summed = dot(e_o[0, 0, rows, :], vals)
        inverse = 1.0 / summed[:, width:]
        inv_o[0, rows, cols] = inverse
        mix_o[0, rows, cols] = (summed[:, :width] * inverse).astype(bf16)


def norm_parts(values):
    centre = jnp.mean(values, -1, keepdims=True)
    offset = values - centre
    second = jnp.mean(offset * offset, -1, keepdims=True)
    root = lax.rsqrt(second + epsilon)
    return offset * root, root


def norm_back(grad, unit, root):
    return root * (grad - jnp.mean(grad, -1, keepdims=True) - unit * jnp.mean(grad * unit, -1, keepdims=True))


def middle_kernel(ctx_len,
                  place, queries, feats, mixed, inv, cot, w_feat, w_mark, b_enc, w_out, b_out, gain_one, shift_one, w_in, b_in,
                  w_back, b_back, gain_two, shift_two,
                  out_o, first_o, dox_o, grads_o, wide_o, narrow_o,
                  g_out, g_in, g_back, wide, narrow):
    block = pl.program_id(0)
    part = pl.program_id(1)
    step = feats.shape[1]
    width = mixed.shape[2] // HEADS

    @pl.when((block == 0) & (part == 0))
    def _():
        g_out[...] = jnp.zeros_like(g_out)
        g_in[...] = jnp.zeros_like(g_in)
        g_back[...] = jnp.zeros_like(g_back)
        wide[...] = jnp.zeros_like(wide)
        narrow[...] = jnp.zeros_like(narrow)

    mixed_low = mixed[0]
    stream = embed(feats[0], w_feat, w_mark, b_enc)
    unit_one, root_one = norm_parts(stream + dot(mixed_low, w_out[...]) + b_out[...])
    normed = unit_one * gain_one[...] + shift_one[...]
    normed_low = normed.astype(bf16)
    hidden = dot(normed_low, w_in[...]) + b_in[...]
    inner = math.sqrt(2.0 / math.pi)
    square = hidden * hidden
    curve = jnp.tanh(hidden * (inner + (inner * 0.044715) * square))
    half = 0.5 * curve + 0.5
    active_low = (hidden * half).astype(bf16)
    slope = half + (0.5 * hidden) * (1.0 - curve * curve) * (inner + (3.0 * inner * 0.044715) * square)
    branch = dot(active_low, w_back[...]) + b_back[...]
    unit_two, root_two = norm_parts(normed + branch)
    row = part * step + lax.broadcasted_iota(jnp.int32, (step, 1), 0)
    alive = row < ctx_len + queries[block]
    out_o[0] = jnp.where(alive, unit_two * gain_two[...] + shift_two[...], 0.0).astype(bf16)
    grad = jnp.where(alive, cot[0], 0.0)
    second = norm_back(grad * gain_two[...], unit_two, root_two)
    branch_low = second.astype(bf16)
    g_back[...] += dot_tn(active_low, branch_low)
    hidden_low = (slope * dot_nt(branch_low, w_back[...])).astype(bf16)
    g_in[...] += dot_tn(normed_low, hidden_low)
    grad_one = second + dot_nt(hidden_low, w_in[...])
    first = norm_back(grad_one * gain_one[...], unit_one, root_one)
    first_o[0] = first
    first_low = first.astype(bf16)
    g_out[...] += dot_tn(mixed_low, first_low)
    back = dot_nt(first_low, w_out[...]).astype(bf16).astype(f32) * inv[0]
    lane = lax.broadcasted_iota(jnp.int32, (step, width), 1)
    for head in range(HEADS):
        cols = slice(head * width, (head + 1) * width)
        scaled = back[:, cols].astype(bf16)
        shift = -jnp.sum(scaled.astype(f32) * mixed_low[:, cols].astype(f32), 1, keepdims=True)
        top = shift.astype(bf16).astype(f32)
        extra = jnp.where(lane == 0, top, jnp.where(lane == 1, shift - top, 0.0))
        dox_o[0, head, :, :width] = scaled
        dox_o[0, head, :, width:] = extra.astype(bf16)
    total = lambda v: jnp.sum(v, 0, keepdims=True)
    wide[0:1, :] += total(hidden_low.astype(f32))
    narrow[0:1, :] += total(first_low.astype(f32))
    narrow[1:2, :] += total(grad_one * unit_one)
    narrow[2:3, :] += total(grad_one)
    narrow[3:4, :] += total(branch_low.astype(f32))
    narrow[4:5, :] += total(grad * unit_two)
    narrow[5:6, :] += total(grad)

    @pl.when((block == pl.num_programs(0) - 1) & (part == pl.num_programs(1) - 1))
    def _():
        model = g_out.shape[1]

        def lay(p, _):
            at = pl.multiple_of((p ^ place[0]) * 16, 16)
            grads_o[p, 0:16, :] = g_out[pl.ds(at, 16), :].astype(bf16)
            for j in range(2):
                grads_o[p, 16 + 16 * j:32 + 16 * j, :] = g_in[pl.ds(at, 16), j * model:(j + 1) * model].astype(bf16)
            grads_o[p, 48:80, :] = g_back[pl.ds(pl.multiple_of(at * 2, 32), 32), :].astype(bf16)
            return 0

        lax.fori_loop(0, CHUNKS, lay, 0)
        wide_o[...] = wide[...]
        narrow_o[...] = narrow[...]


def scores_kernel(ctx_pad, parts,
                  place, e, q, k, v, dox, low, d_o, g_o, bias_o, ds, g_scr, bias_scr):
    block = pl.program_id(0)
    pad = q.shape[1]
    step = pad // parts
    width = q.shape[2]
    root = 1.0 / math.sqrt(width)
    keys = k[0, :ctx_pad, :]
    vals = jnp.concatenate([v[0, :ctx_pad, :], jnp.ones((ctx_pad, width), bf16)], 1)
    for c in range(parts):
        rows = slice(c * step, (c + 1) * step)
        d_probs = dot_nt(dox[0, 0, rows, :], vals)
        ds[rows, :] = e[0, 0, rows, :] * d_probs.astype(bf16)
        d_o[0, 0, rows, :width] = (dot(ds[rows, :], keys) * root).astype(bf16)
    d_o[0, 0, :ctx_pad, width:2 * width] = (dot_tn(ds[...], q[0]) * root).astype(bf16)
    d_o[0, 0, :ctx_pad, 2 * width:] = dot_tn(e[0, 0], dox[0, 0, :, :width]).astype(bf16)
    d_o[0, 0, ctx_pad:, width:] = jnp.zeros((pad - ctx_pad, 2 * width), bf16)
    grads = dot_tn(low[0], d_o[0, 0])
    sums = jnp.sum(d_o[0, 0].astype(f32), 0, keepdims=True)

    @pl.when(block == 0)
    def _():
        g_scr[...] = grads
        bias_scr[...] = jnp.broadcast_to(sums, bias_scr.shape)

    @pl.when(block > 0)
    def _():
        g_scr[...] += grads
        bias_scr[...] += jnp.broadcast_to(sums, bias_scr.shape)

    @pl.when(block == pl.num_programs(0) - 1)
    def _():
        def lay(p, _):
            at = pl.multiple_of((p ^ place[0]) * 16, 16)
            g_o[p] = g_scr[pl.ds(at, 16), :].astype(bf16)
            return 0

        lax.fori_loop(0, CHUNKS, lay, 0)
        bias_o[...] = bias_scr[...]


def attend(ids, groups, mark, w_feat, w_mark, b_enc, w_query, b_query, w_key, w_value, b_value, ctx_len, feat_total, classes):
    blocks, span = ids.shape
    pad = mark.shape[1]
    model = w_query.shape[0]
    ctx_pad = round_up(ctx_len, LANES)
    parts = row_chunks(pad)
    whole = lambda a: pl.BlockSpec(a.shape, lambda *_: (0,) * a.ndim)
    per = lambda w: pl.BlockSpec((1, pad, w), lambda b, h, *_: (b, 0, 0))
    kernel = functools.partial(attend_kernel, span, ctx_len, ctx_pad, feat_total, classes, parts)
    shape = lambda *s: jax.ShapeDtypeStruct(s, bf16)
    return pl.pallas_call(
        kernel,
        grid_spec=pltpu.PrefetchScalarGridSpec(
            num_scalar_prefetch=1,
            grid=(blocks, HEADS),
            in_specs=[whole(groups), per(1)] + [whole(a) for a in (w_feat, w_mark, b_enc, w_query, b_query, w_key, w_value, b_value)],
            out_specs=[per(LANES), per(model), per(model), per(model), per(model),
                       pl.BlockSpec((1, 1, pad, ctx_pad), lambda b, h, *_: (b, h, 0, 0)), per(model), per(model)],
            scratch_shapes=[pltpu.VMEM((groups.shape[0] * groups.shape[2], LANES), f32), pltpu.VMEM((pad, LANES), f32)],
        ),
        out_shape=[shape(blocks, pad, LANES), shape(blocks, pad, model), shape(blocks, pad, model), shape(blocks, pad, model),
                   shape(blocks, pad, model), shape(blocks, HEADS, pad, ctx_pad),
                   jax.ShapeDtypeStruct((blocks, pad, model), f32), shape(blocks, pad, model)],
        compiler_params=params(0, 0),
        name="attend",
    )(ids, groups, mark, w_feat, w_mark, b_enc, w_query, b_query, w_key, w_value, b_value)


def middle(place, queries, feats, mixed, inv, cot, weights, ctx_len):
    blocks, pad, model = mixed.shape
    span = cot.shape[1]
    parts = row_chunks(pad)
    step = pad // parts
    inner = weights[7].shape[1]
    whole = lambda a: pl.BlockSpec(a.shape, lambda *_: (0,) * a.ndim)
    full = lambda *s: pl.BlockSpec(s, lambda *_: (0,) * len(s))
    per = lambda w: pl.BlockSpec((1, step, w), lambda b, c, *_: (b, c, 0))
    grads = [(model, model), (model, inner), (inner, model)]
    return pl.pallas_call(
        functools.partial(middle_kernel, ctx_len),
        grid_spec=pltpu.PrefetchScalarGridSpec(
            num_scalar_prefetch=2,
            grid=(blocks, parts),
            in_specs=[per(LANES), per(model), per(model), per(model)] + [whole(a) for a in weights],
            out_specs=[per(model), per(model),
                       pl.BlockSpec((1, HEADS, step, 2 * model // HEADS), lambda b, c, *_: (b, 0, c, 0))]
            + [full(CHUNKS, 80, model), full(8, inner), full(8, model)],
            scratch_shapes=[pltpu.VMEM(s, f32) for s in grads] + [pltpu.VMEM((8, inner), f32), pltpu.VMEM((8, model), f32)],
        ),
        out_shape=[jax.ShapeDtypeStruct((blocks, span, model), bf16), jax.ShapeDtypeStruct((blocks, pad, model), f32),
                   jax.ShapeDtypeStruct((blocks, HEADS, pad, 2 * model // HEADS), bf16)]
        + [jax.ShapeDtypeStruct((CHUNKS, 80, model), bf16)]
        + [jax.ShapeDtypeStruct((8, inner), f32), jax.ShapeDtypeStruct((8, model), f32)],
        compiler_params=params(0, 0),
        name="middle",
    )(place, queries, feats, mixed, inv, cot, *weights)


def score_grads(place, head, e, q, k, v, dox, low):
    blocks, pad, model = q.shape
    ctx_pad = e.shape[3]
    width = model // HEADS
    parts = row_chunks(pad)
    col = pl.BlockSpec((1, pad, width), lambda b, *_: (b, 0, head))
    return pl.pallas_call(
        functools.partial(scores_kernel, ctx_pad, parts),
        grid_spec=pltpu.PrefetchScalarGridSpec(
            num_scalar_prefetch=1,
            grid=(blocks,),
            in_specs=[pl.BlockSpec((1, 1, pad, ctx_pad), lambda b, *_: (b, head, 0, 0)), col, col, col,
                      pl.BlockSpec((1, 1, pad, 2 * width), lambda b, *_: (b, head, 0, 0)),
                      pl.BlockSpec((1, pad, model), lambda b, *_: (b, 0, 0))],
            out_specs=[pl.BlockSpec((1, 1, pad, 3 * width), lambda b, *_: (b, 0, 0, 0)),
                       pl.BlockSpec((CHUNKS, 16, 3 * width), lambda b, *_: (0, 0, 0)),
                       pl.BlockSpec((8, 3 * width), lambda b, *_: (0, 0))],
            scratch_shapes=[pltpu.VMEM((pad, ctx_pad), bf16), pltpu.VMEM((model, 3 * width), f32), pltpu.VMEM((8, 3 * width), f32)],
        ),
        out_shape=[jax.ShapeDtypeStruct((blocks, 1, pad, 3 * width), bf16),
                   jax.ShapeDtypeStruct((CHUNKS, 16, 3 * width), bf16), jax.ShapeDtypeStruct((8, 3 * width), f32)],
        compiler_params=params(0),
        name="score_grads",
    )(place, e, q, k, v, dox, low)


def stream_kernel(feat_total, place, first, *refs):
    d_refs, refs = refs[:HEADS], refs[HEADS:]
    wts, feats, w_aug_t, narrow, wide = refs[:5]
    biases, refs = refs[5:5 + HEADS], refs[5 + HEADS:]
    rows_o, tail_o, aug, sums = refs
    block = pl.program_id(0)
    part = pl.program_id(1)
    model = first.shape[2]
    width = model // HEADS

    total = first[0]
    for head in range(HEADS):
        total = total + dot(d_refs[head][0, 0], wts[head])
    low = total.astype(bf16)

    @pl.when((block == 0) & (part == 0))
    def _():
        aug[...] = jnp.zeros_like(aug)
        sums[...] = jnp.zeros_like(sums)

    aug[:LANES, :] += dot_tn(feats[0], low)
    d_feats = dot(low, w_aug_t[...])
    rows_o[0] = d_feats
    sums[0:1, :] += jnp.sum(d_feats, 0, keepdims=True)
    sums[1:2, :] += jnp.sum(d_feats * feats[0].astype(f32), 0, keepdims=True)

    @pl.when((block == pl.num_programs(0) - 1) & (part == pl.num_programs(1) - 1))
    def _():
        aug[LANES:LANES + 6, :] = narrow[0:6, :]
        aug[LANES + 6:LANES + 7, :] = wide[0:1, :model]
        aug[LANES + 7:LANES + 8, :] = wide[0:1, model:]
        for head in range(HEADS):
            cols = slice(head * width, (head + 1) * width)
            aug[LANES + 8:LANES + 9, cols] = biases[head][0:1, :width]
            aug[LANES + 9:LANES + 10, cols] = biases[head][0:1, 2 * width:]
        for j in range(2):
            aug[LANES + 10:LANES + 11, j * LANES:(j + 1) * LANES] = sums[j:j + 1, :]
        half = model // 2

        def lay(p, _):
            at = p ^ place[0]
            rows = pl.ds(pl.multiple_of(at // 2 * 16, 16), 16)
            tail_o[p] = aug[rows, pl.ds(pl.multiple_of(at % 2 * half, half), half)].astype(bf16)
            return 0

        lax.fori_loop(0, CHUNKS, lay, 0)


def stream_grads(place, first, d_parts, wts, feats, w_aug_t, narrow, wide, biases, feat_total):
    blocks, pad, model = first.shape
    parts = row_chunks(pad)
    step = pad // parts
    per = lambda w: pl.BlockSpec((1, step, w), lambda b, c, *_: (b, c, 0))
    d_spec = pl.BlockSpec((1, 1, step, d_parts[0].shape[3]), lambda b, c, *_: (b, 0, c, 0))
    whole = lambda a: pl.BlockSpec(a.shape, lambda *_: (0,) * a.ndim)
    return pl.pallas_call(
        functools.partial(stream_kernel, feat_total),
        grid_spec=pltpu.PrefetchScalarGridSpec(
            num_scalar_prefetch=1,
            grid=(blocks, parts),
            in_specs=[per(model)] + [d_spec] * HEADS + [whole(wts), per(LANES), whole(w_aug_t), whole(narrow), whole(wide)]
            + [whole(b) for b in biases],
            out_specs=[per(LANES), pl.BlockSpec((CHUNKS, 16, model // 2), lambda *_: (0, 0, 0))],
            scratch_shapes=[pltpu.VMEM((2 * LANES, model), f32), pltpu.VMEM((8, LANES), f32)],
        ),
        out_shape=[jax.ShapeDtypeStruct((blocks, pad, LANES), f32), jax.ShapeDtypeStruct((CHUNKS, 16, model // 2), bf16)],
        compiler_params=params(0, 0),
        name="stream_grads",
    )(place, first, *d_parts, wts, feats, w_aug_t, narrow, wide, *biases)


def spread_kernel(span, own, ids, rows, out_o, *tables):
    blocks = rows.shape[0]
    count = out_o.shape[0]
    deep = out_o.shape[1]
    for table in tables:
        table[...] = jnp.zeros_like(table)
    each = len(tables) // blocks if len(tables) > 1 else 1
    run = span // each
    unit = next(u for u in (10, 5, 2, 1) if run % u == 0)

    def add(i, _):
        for u in range(unit):
            for t in range(blocks * each):
                block, at = t // each, t % each * run + i * unit + u
                table = tables[t % len(tables)]
                spot = pl.ds(ids[block, at], 1)
                table[spot, :] += rows[block, pl.ds(at, 1), :]
        return 0

    lax.fori_loop(0, run // unit, add, 0)

    def fold(g, _):
        spot = pl.ds(pl.multiple_of(g * own, own), own)
        total = tables[0][spot, :]
        for table in tables[1:]:
            total = total + table[spot, :]
        out_o[g] = total.T[:deep].astype(bf16)
        return 0

    lax.fori_loop(0, count, fold, 0)


def spread(ids, rows, count, deep, own):
    span = ids.shape[1]
    tables = 4 if count <= 8 and span % 2 == 0 else 1
    return pl.pallas_call(
        functools.partial(spread_kernel, span, own),
        grid_spec=pltpu.PrefetchScalarGridSpec(
            num_scalar_prefetch=1,
            grid=(1,),
            in_specs=[pl.BlockSpec(rows.shape, lambda *_: (0, 0, 0))],
            out_specs=pl.BlockSpec((count, deep, own), lambda *_: (0, 0, 0)),
            scratch_shapes=[pltpu.VMEM((count * own, LANES), f32)] * tables,
        ),
        out_shape=jax.ShapeDtypeStruct((count, deep, own), bf16),
        compiler_params=params(0),
        name="spread",
    )(ids, rows)


def finish_kernel(place, grads, out_o, in_o, back_o):
    step = pl.program_id(0)
    model = out_o.shape[1]
    for u in range(out_o.shape[0] // 16):
        p = (step * (out_o.shape[0] // 16) + u) ^ place[0]
        rows = slice(u * 16, (u + 1) * 16)
        out_o[rows, :] = grads[p, 0:16, :].astype(f32)
        for j in range(2):
            in_o[rows, j * model:(j + 1) * model] = grads[p, 16 + 16 * j:32 + 16 * j, :].astype(f32)
        back_o[u * 32:(u + 1) * 32, :] = grads[p, 48:80, :].astype(f32)


def finish(place, grads):
    model = grads.shape[2]
    steps = 8
    shapes = [(model, model), (model, 2 * model), (2 * model, model)]
    return pl.pallas_call(
        finish_kernel,
        grid_spec=pltpu.PrefetchScalarGridSpec(
            num_scalar_prefetch=1,
            grid=(steps,),
            in_specs=[pl.BlockSpec(grads.shape, lambda *_: (0, 0, 0))],
            out_specs=[pl.BlockSpec((s[0] // steps, s[1]), lambda i, *_: (i, 0)) for s in shapes],
        ),
        out_shape=[jax.ShapeDtypeStruct(s, f32) for s in shapes],
        compiler_params=params(0),
        name="finish",
    )(place, grads)


def finish_tail_kernel(place, heads, tail, q_o, k_o, v_o, aug_o):
    step = pl.program_id(0)
    model = q_o.shape[1]
    width = model // HEADS
    half = model // 2
    for u in range(q_o.shape[0] // 16):
        p = (step * (q_o.shape[0] // 16) + u) ^ place[0]
        rows = slice(u * 16, (u + 1) * 16)
        for head in range(HEADS):
            cols = slice(head * width, (head + 1) * width)
            for j, ref in enumerate((q_o, k_o, v_o)):
                at = (head * 3 + j) * width
                ref[rows, cols] = heads[p, :, at:at + width].astype(f32)
        row = pl.ds(pl.multiple_of(u // 2 * 16, 16), 16)
        aug_o[row, (u % 2) * half:(u % 2 + 1) * half] = tail[p].astype(f32)


def finish_tail(place, heads, tail):
    model = tail.shape[2] * 2
    steps = 8
    shapes = [(model, model)] * 3 + [(2 * LANES, model)]
    return pl.pallas_call(
        finish_tail_kernel,
        grid_spec=pltpu.PrefetchScalarGridSpec(
            num_scalar_prefetch=1,
            grid=(steps,),
            in_specs=[pl.BlockSpec(heads.shape, lambda *_: (0, 0, 0)), pl.BlockSpec(tail.shape, lambda *_: (0, 0, 0))],
            out_specs=[pl.BlockSpec((s[0] // steps, s[1]), lambda i, *_: (i, 0)) for s in shapes],
        ),
        out_shape=[jax.ShapeDtypeStruct(s, f32) for s in shapes],
        compiler_params=params(0),
        name="finish_tail",
    )(place, heads, tail)


def swap(value, axis, bit):
    size = lax.axis_size(axis)
    return lax.ppermute(value, axis, [(i, i ^ bit) for i in range(size)])


def axis_bits(axis):
    return [(axis, 1 << b) for b in range(lax.axis_size(axis).bit_length() - 1)]


def sum_over(value, bits):
    for axis, bit in bits:
        value = value + swap(value, axis, bit)
    return value


def reduce_chunks(value, bits):
    split = CHUNKS.bit_length() - 1
    total = value
    for axis, bit in bits[:split]:
        half = total.shape[0] // 2
        came = swap(total[half:].astype(bf16), axis, bit)
        total = total[:half].astype(f32) + came.astype(f32)
    for axis, bit in bits[split:]:
        low = total.astype(bf16)
        total = low.astype(f32) + swap(low, axis, bit).astype(f32)
    return total.astype(bf16)


def gather_chunks(value, bits):
    for axis, bit in reversed(bits[:CHUNKS.bit_length() - 1]):
        value = jnp.concatenate([value, swap(value, axis, bit)], 0)
    return value


def body(
    raw_rows, enc_weight, enc_bias, label_table, w_query, b_query, w_key, w_value, b_value, w_out, b_out,
    gain_one, shift_one, w_in, b_in, w_back, b_back, gain_two, shift_two, members, labels, queries, cotangent,
):
    row_count = lax.axis_size("rows")
    feat_count = lax.axis_size("feat")
    row_index = lax.axis_index("rows")
    feat_index = lax.axis_index("feat")
    local_rows, col_width = raw_rows.shape
    own_rows = local_rows // feat_count
    feat_total = col_width * feat_count
    model = enc_weight.shape[1]
    classes = label_table.shape[0]
    blocks, span = members.shape
    ctx_len = labels.shape[1]
    pad = round_up(span, 16)
    row_total = float(local_rows * row_count)
    row_bits = axis_bits("rows")
    bits = axis_bits("feat") + row_bits
    place = jnp.int32(0)
    for at, (axis, bit) in enumerate(bits[:CHUNKS.bit_length() - 1]):
        has = (lax.axis_index(axis) // bit) % 2
        place = place + has * (CHUNKS >> (at + 1))
    place = place.reshape(1).astype(jnp.int32)
    row = lambda a: a.reshape(1, -1)

    columns = raw_rows.T
    sums = jnp.stack([jnp.sum(columns, 1), jnp.sum(columns * columns, 1)])
    sums = sum_over(sums, row_bits)
    col_mean = sums[0] / row_total
    factor = lax.rsqrt(sums[1] / row_total - col_mean * col_mean + epsilon)
    standard = ((columns - col_mean[:, None]) * factor[:, None]).astype(bf16)
    standard = standard.reshape(col_width, feat_count, own_rows).transpose(1, 0, 2)
    owned = lax.all_to_all(standard, "feat", split_axis=0, concat_axis=0, tiled=True).reshape(1, feat_total, own_rows)
    groups = owned
    for axis, bit in reversed(row_bits):
        groups = jnp.concatenate([groups, swap(groups, axis, bit)], 0)
    source = (members // local_rows) ^ row_index
    spot = jnp.zeros_like(source)
    for at in range(len(row_bits)):
        spot = spot + ((source >> at) & 1) * (row_count >> (at + 1))
    ids = spot * own_rows + members % own_rows

    w_feat = jnp.pad(enc_weight, ((0, LANES - feat_total), (0, 0)))
    w_mark = jnp.pad(label_table, ((feat_total, LANES - feat_total - classes), (0, 0)))
    b_enc = row(enc_bias)
    mark = jnp.pad(labels, ((0, 0), (0, pad - ctx_len)), constant_values=-2 * LANES)[:, :, None]
    feats, low, qry, key, val, expo, inv, mixed = attend(
        ids, groups, mark, w_feat, w_mark, b_enc, w_query, row(b_query), w_key, w_value, row(b_value), ctx_len, feat_total, classes)
    weights = (w_feat, w_mark, b_enc, w_out, row(b_out), row(gain_one), row(shift_one), w_in, row(b_in), w_back, row(b_back),
               row(gain_two), row(shift_two))
    layer_out, first, dox, grads, wide, narrow = middle(place, queries, feats, mixed, inv, cotangent, weights, ctx_len)
    grads = gather_chunks(reduce_chunks(grads, bits), bits)
    g_out, g_in, g_back = finish(place, grads)

    width = model // HEADS
    parts, heads, biases = [], [], []
    for head in range(HEADS):
        part, head_grads, bias = score_grads(place, head, expo, qry, key, val, dox, low)
        parts.append(part)
        heads.append(head_grads)
        biases.append(bias)
    cut = lambda w: w.T.reshape(HEADS, width, model)
    wts = jnp.concatenate([cut(w_query), cut(w_key), cut(w_value)], 1)
    d_rows, tail = stream_grads(place, first, parts, wts, feats, w_feat.T, narrow, wide, biases, feat_total)
    both = jnp.concatenate(heads + [tail], 2)
    both = gather_chunks(reduce_chunks(both, bits), bits)
    g_query, g_key, g_value, aug = finish_tail(place, both[:, :, :3 * model], both[:, :, 3 * model:])

    d_table = spread(ids, d_rows, row_count, feat_total, own_rows)
    d_table = d_table.astype(f32)
    for axis, bit in row_bits:
        half = d_table.shape[0] // 2
        d_table = d_table[:half] + swap(d_table[half:].astype(bf16), axis, bit).astype(f32)
    d_own = d_table.astype(bf16).reshape(feat_count, col_width, own_rows)
    d_columns = lax.all_to_all(d_own, "feat", split_axis=0, concat_axis=0, tiled=True)
    d_columns = d_columns.transpose(1, 0, 2).reshape(col_width, local_rows).astype(f32)
    smalls = aug[LANES:]
    stats = smalls[10, :2 * LANES].reshape(2, LANES)
    stats = lax.dynamic_slice_in_dim(stats, feat_index * col_width, col_width, 1)
    d_spread = -0.5 * (stats[1] / factor) * factor * factor * factor
    d_mean = -factor * stats[0] - 2.0 * d_spread * col_mean
    raw_grad = factor[:, None] * d_columns + (d_mean[:, None] + 2.0 * d_spread[:, None] * columns) / row_total
    return (
        layer_out, raw_grad.T, aug[:feat_total], aug[feat_total + classes], aug[feat_total:feat_total + classes],
        g_query, smalls[8], g_key, g_value, smalls[9], g_out, smalls[0], smalls[1], smalls[2], g_in,
        smalls[6:8].reshape(-1), g_back, smalls[3], smalls[4], smalls[5],
    )


def solution(mesh):
    both = ("rows", "feat")
    placed = (P("rows", "feat"),) + (P(),) * 18 + (P(both, None), P(both, None), P(both), P(both, None, None))
    results = (P(both, None, None), P("rows", "feat")) + (P(),) * 18
    return jax.shard_map(body, mesh=mesh, in_specs=placed, out_specs=results, check_vma=False)
```

```python
import functools
import math

import jax
import jax.numpy as jnp
from jax import lax
from jax.experimental import pallas as pl
from jax.experimental.pallas import tpu as pltpu
from jax.sharding import PartitionSpec as P

HEADS = 4
LANES = 128
epsilon = 1e-05
CHUNKS = 32
VMEM_LIMIT = 60 * 1024 * 1024
f32 = jnp.float32
bf16 = jnp.bfloat16


def dot(left, right):
    return jnp.dot(left, right, preferred_element_type=f32)


def dot_nt(left, right):
    return lax.dot_general(left, right, (((1,), (1,)), ((), ())), preferred_element_type=f32)


def dot_tn(left, right):
    return lax.dot_general(left, right, (((0,), (0,)), ((), ())), preferred_element_type=f32)


def round_up(value, unit):
    return -(-value // unit) * unit


def row_chunks(span):
    for parts in (3, 2, 1):
        if span % (16 * parts) == 0:
            return parts
    return 1


def cost(gigaflops, megabytes):
    return pl.CostEstimate(flops=int(gigaflops * 1e9), bytes_accessed=int(megabytes * 1e6), transcendentals=0)


def params(*names):
    return pltpu.CompilerParams(vmem_limit_bytes=VMEM_LIMIT, dimension_semantics=("arbitrary",) * len(names))


def fetch_kernel(span, feat_total, classes, ids, near, far, mark, feats_o, table, rows_f):
    count, deep, own = near.shape
    blocks, pad, _ = feats_o.shape
    unit = next(u for u in (20, 10, 5, 2, 1) if span % u == 0)

    for half, ref in enumerate((near, far)):
        def unfold(g, _):
            piece = jnp.concatenate([ref[g].astype(f32), jnp.zeros((LANES - deep, own), f32)], 0).T
            at = half * count + g
            table[pl.ds(pl.multiple_of(at * own, own), own), :] = piece
            return 0

        lax.fori_loop(0, count, unfold, 0)
    rows_f[pad - 16:, :] = jnp.zeros((16, LANES), f32)
    for block in range(blocks):
        def fetch(i, _):
            for u in range(unit):
                at = i * unit + u
                rows_f[pl.ds(at, 1), :] = table[pl.ds(ids[block * span + at], 1), :]
            return 0

        lax.fori_loop(0, span // unit, fetch, 0)
        lane = lax.broadcasted_iota(jnp.int32, (pad, LANES), 1)
        hot = (lane == mark[block] + feat_total) | (lane == feat_total + classes)
        feats_o[block] = jnp.where(lane < feat_total, rows_f[...], hot.astype(f32)).astype(bf16)


def fetch(ids, near, far, mark, feat_total, classes):
    blocks, pad, _ = mark.shape
    full = lambda *s: pl.BlockSpec(s, lambda *_: (0,) * len(s), pipeline_mode=pl.Buffered(1))
    return pl.pallas_call(
        functools.partial(fetch_kernel, ids.shape[0] // blocks, feat_total, classes),
        grid_spec=pltpu.PrefetchScalarGridSpec(
            num_scalar_prefetch=1,
            grid=(1,),
            in_specs=[full(*near.shape), full(*far.shape), full(*mark.shape)],
            out_specs=pl.BlockSpec((blocks, pad, LANES), lambda *_: (0, 0, 0)),
            scratch_shapes=[pltpu.VMEM((2 * near.shape[0] * near.shape[2], LANES), f32), pltpu.VMEM((pad, LANES), f32)],
        ),
        out_shape=jax.ShapeDtypeStruct((blocks, pad, LANES), bf16),
        compiler_params=params(0),
        cost_estimate=cost(6, 1),
        name="fetch",
    )(ids, near, far, mark)


def embed(feats, w_feat, w_mark, b_enc):
    slots = (dot(feats, w_feat[...]) + b_enc[...]).astype(bf16)
    return slots.astype(f32) + dot(feats, w_mark[...])


def norm_parts(values):
    centre = jnp.mean(values, -1, keepdims=True)
    offset = values - centre
    second = jnp.mean(offset * offset, -1, keepdims=True)
    root = lax.rsqrt(second + epsilon)
    return offset * root, root


def norm_back(grad, unit, root):
    return root * (grad - jnp.mean(grad, -1, keepdims=True) - unit * jnp.mean(grad * unit, -1, keepdims=True))


def forward_kernel(blocks, ctx_len, ctx_pad, parts,
                   place, queries, feats, cot, w_feat, w_mark, b_enc, w_qkv, b_qkv, w_out, b_out, gain_one, shift_one,
                   w_in, b_in, w_back, b_back, gain_two, shift_two, w_feat_t,
                   low_o, qkv_o, e_o, out_o, rows_o, back_o, shift_o, keep_o, give_o, aug_o,
                   mixed, inv, out_f, act_s, norm_s, d_hid_s, d_bra_s, d_att_s, g_out, g_in, g_back, wide, narrow):
    tick = pl.program_id(0)
    pad = low_o.shape[1]
    model = back_o.shape[2]
    step = pad // parts
    width = model // HEADS

    @pl.when(tick < blocks * HEADS)
    def _():
        block = tick // HEADS
        head = tick % HEADS

        @pl.when(head == 0)
        def _():
            def project(c, _):
                rows = pl.ds(pl.multiple_of(c * step, 16), step)
                low = embed(feats[block, rows, :], w_feat, w_mark, b_enc).astype(bf16)
                low_o[0, rows, :model] = low
                low_o[0, rows, model:] = feats[block, rows, :]
                made = (dot(low, w_qkv[...]) + b_qkv[...]).astype(bf16)
                for h in range(HEADS):
                    qkv_o[0, h, rows, :] = made[:, h * 3 * width:(h + 1) * 3 * width]
                return 0

            lax.fori_loop(0, parts, project, 0)

        factor = math.log2(math.e) / math.sqrt(width)
        keys = qkv_o[0, head, :ctx_pad, width:2 * width]
        vals = jnp.concatenate([qkv_o[0, head, :ctx_pad, 2 * width:], jnp.ones((ctx_pad, width), bf16)], 1)
        edge = ctx_len // LANES * LANES
        cols = pl.ds(pl.multiple_of(head * width, LANES), width)
        spans = [slice(c * step, (c + 1) * step) for c in range(parts)]

        def score(c):
            return dot_nt(qkv_o[0, head, spans[c], :width], keys)

        def weigh(c, scores):
            front = scores[:, :edge]
            most = jnp.max(front, 1, keepdims=True)
            if edge < ctx_pad:
                lane = lax.broadcasted_iota(jnp.int32, (step, ctx_pad - edge), 1)
                rear = jnp.where(lane < ctx_len - edge, scores[:, edge:], -1e30)
                most = jnp.maximum(most, jnp.max(rear, 1, keepdims=True))
                e_o[0, 0, spans[c], edge:] = jnp.exp2((rear - most) * factor).astype(bf16)
            e_o[0, 0, spans[c], :edge] = jnp.exp2((front - most) * factor).astype(bf16)

        def mix(c):
            summed = dot(e_o[0, 0, spans[c], :], vals)
            inverse = 1.0 / summed[:, width:]
            lane = lax.broadcasted_iota(jnp.int32, (step, LANES), 1)
            inv[block, spans[c], :] = jnp.where(lane == head, inverse[:, :LANES], inv[block, spans[c], :])
            mixed[block, spans[c], cols] = (summed[:, :width] * inverse).astype(bf16)

        ready = score(0)
        for c in range(parts):
            coming = score(c + 1) if c + 1 < parts else None
            weigh(c, ready)
            mix(c)
            ready = coming

    @pl.when(tick >= blocks * HEADS)
    def _():
        part = tick - blocks * HEADS

        @pl.when(part == 0)
        def _():
            for ref in (g_out, g_in, g_back, wide, narrow):
                ref[...] = jnp.zeros_like(ref)

        tiles = model // LANES
        rows = pl.ds(pl.multiple_of(part * step, 16), step)
        total = lambda v: jnp.sum(v, 0, keepdims=True)
        wide_t, narrow_t = [], [[] for _ in range(6)]

        def flow(block):
            here = slice(block * step, (block + 1) * step)
            mixed_low = mixed[block, rows, :]
            reached = embed(feats[block, rows, :], w_feat, w_mark, b_enc) + dot(mixed_low, w_out[...])
            yield
            unit_one, root_one = norm_parts(reached + b_out[...])
            normed = unit_one * gain_one[...] + shift_one[...]
            norm_s[here, :] = normed.astype(bf16)
            yield
            hidden = dot(norm_s[here, :], w_in[...])
            yield
            hidden = hidden + b_in[...]
            slant = math.sqrt(2.0 / math.pi)
            square = hidden * hidden
            half = 0.5 * jnp.tanh(hidden * (slant + (slant * 0.044715) * square)) + 0.5
            active = hidden * half
            act_s[here, :] = active.astype(bf16)
            slope = half + active * (1.0 - half) * (2.0 * slant + (6.0 * slant * 0.044715) * square)
            yield
            branch = dot(act_s[here, :], w_back[...])
            yield
            unit_two, root_two = norm_parts(normed + (branch + b_back[...]))
            row = part * step + lax.broadcasted_iota(jnp.int32, (step, 1), 0)
            alive = row < ctx_len + queries[block]
            result = jnp.where(alive, unit_two * gain_two[...] + shift_two[...], 0.0)
            given = []
            for j in range(tiles):
                lanes = pl.ds(j * blocks + block, step, stride=tiles * blocks)
                out_f[lanes, :] = result[:, j * LANES:(j + 1) * LANES]
                given.append(cot[lanes, :])
            grad = jnp.where(alive, jnp.concatenate(given, 1), 0.0)
            second = norm_back(grad * gain_two[...], unit_two, root_two)
            d_bra_s[here, :] = second.astype(bf16)
            narrow_t[3].append(total(d_bra_s[here, :].astype(f32)))
            narrow_t[4].append(total(grad * unit_two))
            narrow_t[5].append(total(grad))
            yield
            d_act = dot_nt(d_bra_s[here, :], w_back[...])
            yield
            d_hid = (slope * d_act).astype(bf16)
            d_hid_s[here, :] = d_hid
            wide_t.append(total(d_hid.astype(f32)))
            yield
            d_norm = dot_nt(d_hid_s[here, :], w_in[...])
            yield
            grad_one = second + d_norm
            narrow_t[1].append(total(grad_one * unit_one))
            narrow_t[2].append(total(grad_one))
            first = norm_back(grad_one * gain_one[...], unit_one, root_one)
            d_att_s[here, :] = first.astype(bf16)
            narrow_t[0].append(total(d_att_s[here, :].astype(f32)))
            yield
            back = dot_nt(d_att_s[here, :], w_out[...])
            rows_o[block] = dot(d_att_s[here, :], w_feat_t[...])
            yield
            back = back.astype(bf16).astype(f32)
            lane = lax.broadcasted_iota(jnp.int32, (step, LANES), 1)
            shifts = jnp.zeros((step, LANES), f32)
            for h in range(HEADS):
                cols = slice(h * width, (h + 1) * width)
                scaled = (back[:, cols] * inv[block, rows, h:h + 1]).astype(bf16)
                back_o[block, :, cols] = scaled
                moved = jnp.sum(scaled.astype(f32) * mixed_low[:, cols].astype(f32), 1, keepdims=True)
                shifts = jnp.where(lane == h, -moved, shifts)
            shift_o[block] = shifts
            yield

        flows = [flow(block) for block in range(blocks)]
        for item in flows:
            next(item)
        for turn in range(6):
            for item in flows:
                next(item)
                next(item, None)
            if turn == 2:
                g_back[...] += dot_tn(act_s[...], d_bra_s[...])
            if turn == 3:
                g_in[...] += dot_tn(norm_s[...], d_hid_s[...])
            if turn == 4:
                both = jnp.concatenate([jnp.concatenate([mixed[block, rows, :], feats[block, rows, :]], 1) for block in range(blocks)], 0)
                g_out[...] += dot_tn(both, d_att_s[...])
        out_o[...] = out_f[...].astype(bf16)
        wide[0:1, :] += sum(wide_t[1:], wide_t[0])
        for at in range(6):
            narrow[at:at + 1, :] += sum(narrow_t[at][1:], narrow_t[at][0])

        @pl.when(part == parts - 1)
        def _():
            def lay(start, ref, p, _):
                at = pl.multiple_of((p ^ place[0]) * 16, 16)
                ref[p - start, 0:16, :] = g_out[pl.ds(at, 16), :].astype(bf16)
                for j in range(2):
                    ref[p - start, 16 + 16 * j:32 + 16 * j, :] = g_in[pl.ds(at, 16), j * model:(j + 1) * model].astype(bf16)
                ref[p - start, 48:80, :] = g_back[pl.ds(pl.multiple_of(at * 2, 32), 32), :].astype(bf16)
                return 0

            for start, ref in ((0, keep_o), (CHUNKS // 2, give_o)):
                lax.fori_loop(start, start + CHUNKS // 2, functools.partial(lay, start, ref), 0)
            aug_o[:LANES, :] = g_out[model:, :]
            aug_o[LANES:, :] = jnp.zeros((LANES, model), f32)
            aug_o[LANES:LANES + 6, :] = narrow[0:6, :]
            for j in range(2):
                aug_o[LANES + 6 + j:LANES + 7 + j, :] = wide[0:1, j * model:(j + 1) * model]


def forward(place, queries, feats, cot, weights, ctx_len):
    blocks, pad, _ = feats.shape
    model = weights[3].shape[0]
    inner = weights[9].shape[1]
    width = model // HEADS
    ctx_pad = round_up(ctx_len, LANES)
    parts = row_chunks(pad)
    step = pad // parts
    early = blocks * HEADS
    flat = blocks * model // LANES
    attending = lambda t: jnp.minimum(t, early - 1)
    later = lambda t: jnp.maximum(t - early, 0)
    once = lambda a: pl.BlockSpec(a.shape, lambda *_: (0,) * a.ndim, pipeline_mode=pl.Buffered(1))
    full = lambda *s: pl.BlockSpec(s, lambda *_: (0,) * len(s))
    rowed = lambda w: pl.BlockSpec((blocks, step, w), lambda t, *_: (0, later(t), 0))
    shape = jax.ShapeDtypeStruct
    return pl.pallas_call(
        functools.partial(forward_kernel, blocks, ctx_len, ctx_pad, parts),
        grid_spec=pltpu.PrefetchScalarGridSpec(
            num_scalar_prefetch=2,
            grid=(early + parts,),
            in_specs=[once(feats), pl.BlockSpec((step * flat, LANES), lambda t, *_: (later(t), 0))] + [once(a) for a in weights],
            out_specs=[
                pl.BlockSpec((1, pad, model + LANES), lambda t, *_: (attending(t) // HEADS, 0, 0)),
                pl.BlockSpec((1, HEADS, pad, 3 * width), lambda t, *_: (attending(t) // HEADS, 0, 0, 0)),
                pl.BlockSpec((1, 1, pad, ctx_pad), lambda t, *_: (attending(t) // HEADS, attending(t) % HEADS, 0, 0)),
                pl.BlockSpec((step * flat, LANES), lambda t, *_: (later(t), 0)),
                rowed(LANES), rowed(model), rowed(LANES),
                full(CHUNKS // 2, 80, model), full(CHUNKS // 2, 80, model), full(2 * LANES, model)],
            scratch_shapes=[
                pltpu.VMEM((blocks, pad, model), bf16), pltpu.VMEM((blocks, pad, LANES), f32), pltpu.VMEM((step * flat, LANES), f32),
                pltpu.VMEM((blocks * step, inner), bf16), pltpu.VMEM((blocks * step, model), bf16),
                pltpu.VMEM((blocks * step, inner), bf16), pltpu.VMEM((blocks * step, model), bf16),
                pltpu.VMEM((blocks * step, model), bf16), pltpu.VMEM((model + LANES, model), f32), pltpu.VMEM((model, inner), f32),
                pltpu.VMEM((inner, model), f32), pltpu.VMEM((8, inner), f32), pltpu.VMEM((8, model), f32)],
        ),
        out_shape=[
            shape((blocks, pad, model + LANES), bf16), shape((blocks, HEADS, pad, 3 * width), bf16),
            shape((blocks, HEADS, pad, ctx_pad), bf16), shape(cot.shape, bf16), shape((blocks, pad, LANES), f32),
            shape((blocks, pad, model), bf16), shape((blocks, pad, LANES), f32), shape((CHUNKS // 2, 80, model), bf16),
            shape((CHUNKS // 2, 80, model), bf16), shape((2 * LANES, model), f32)],
        compiler_params=params(0),
        cost_estimate=cost(60, 1),
        name="forward",
    )(place, queries, feats, cot, *weights)


def scores_kernel(head, ctx_pad, parts, place, e, qkv, back, shift, low, w_head, w_rows, d_rows, aug, *refs):
    last = head == HEADS - 1
    done, refs = (refs[:head], refs[head:]) if last else ((), refs)
    if last:
        keep_o, give_o, rows_o, ds, dox, d_all, g_scr, aug_s = refs
    else:
        g_o, rows_o, aug_o, ds, dox, d_all, g_scr, aug_s = refs
    block = pl.program_id(0)
    pad = back.shape[1]
    model = aug.shape[1]
    step = pad // parts
    width = back.shape[2]
    root = 1.0 / math.sqrt(width)
    keys = qkv[0, 0, :ctx_pad, width:2 * width]
    vals = jnp.concatenate([qkv[0, 0, :ctx_pad, 2 * width:], jnp.ones((ctx_pad, width), bf16)], 1)
    lane = lax.broadcasted_iota(jnp.int32, (pad, width), 1)
    moved = shift[0, :, head:head + 1]
    top = moved.astype(bf16).astype(f32)
    dox[:, :width] = back[0]
    dox[:, width:] = jnp.where(lane == 0, top, jnp.where(lane == 1, moved - top, 0.0)).astype(bf16)
    spans = [slice(c * step, (c + 1) * step) for c in range(parts)]

    def score(c):
        return dot_nt(dox[spans[c], :], vals)

    ready = score(0)
    for c in range(parts):
        coming = score(c + 1) if c + 1 < parts else None
        ds[spans[c], :] = e[0, 0, spans[c], :] * ready.astype(bf16)
        d_all[spans[c], :width] = (dot(ds[spans[c], :], keys) * root).astype(bf16)
        ready = coming
    d_all[:ctx_pad, 2 * width:] = dot_tn(back[0], e[0, 0]).T.astype(bf16)
    d_all[:ctx_pad, width:2 * width] = (dot_tn(qkv[0, 0, :, :width], ds[...]) * root).T.astype(bf16)
    d_all[ctx_pad:, width:] = jnp.zeros((pad - ctx_pad, 2 * width), bf16)
    grads = dot_tn(low[0], d_all[...])
    sums = jnp.sum(d_all[...].astype(f32), 0, keepdims=True)
    pair = dot(d_all[...], w_rows[0])
    rows_o[0] = d_rows[0] + (pair[:, :LANES] + pair[:, LANES:])
    cols = slice(head * width, (head + 1) * width)

    @pl.when(block == 0)
    def _():
        g_scr[...] = grads
        aug_s[...] = aug[...]

    @pl.when(block > 0)
    def _():
        g_scr[...] += grads

    aug_s[LANES + 8:LANES + 9, cols] += sums[:, :width]
    aug_s[LANES + 9:LANES + 10, cols] += sums[:, 2 * width:]

    @pl.when(block == pl.num_programs(0) - 1)
    def _():
        feat_part = g_scr[model:, :]
        high = feat_part.astype(bf16)
        both = jnp.concatenate([high, (feat_part - high.astype(f32)).astype(bf16)], 0)
        fitted = dot(both, w_head[0])
        aug_s[:LANES, :] += fitted[:LANES] + fitted[LANES:]
        half = model // 2

        def lay(start, ref, p, _):
            at = p ^ place[0]
            rows = pl.ds(pl.multiple_of(at * 16, 16), 16)
            if not last:
                ref[p - start] = g_scr[rows, :].astype(bf16)
                return 0
            for h in range(head):
                ref[p - start, :, h * 3 * width:(h + 1) * 3 * width] = done[h][p]
            ref[p - start, :, head * 3 * width:3 * model] = g_scr[rows, :].astype(bf16)
            spot = pl.ds(pl.multiple_of(at // 2 * 16, 16), 16)
            ref[p - start, :, 3 * model:] = aug_s[spot, pl.ds(pl.multiple_of(at % 2 * half, half), half)].astype(bf16)
            return 0

        if last:
            for start, ref in ((0, keep_o), (CHUNKS // 2, give_o)):
                lax.fori_loop(start, start + CHUNKS // 2, functools.partial(lay, start, ref), 0)
        else:
            lax.fori_loop(0, CHUNKS, functools.partial(lay, 0, g_o), 0)
            aug_o[...] = aug_s[...]


def score_grads(place, head, e, qkv, back, shift, low, w_head, w_rows, d_rows, aug, done):
    blocks, pad, model = back.shape
    ctx_pad = e.shape[3]
    width = model // HEADS
    parts = row_chunks(pad)
    last = head == HEADS - 1
    full = lambda *s: pl.BlockSpec(s, lambda *_: (0,) * len(s))
    rowed = pl.BlockSpec((1, pad, LANES), lambda b, *_: (b, 0, 0))
    shape = jax.ShapeDtypeStruct
    ends = [(CHUNKS // 2, 16, 3 * model + model // 2)] * 2 if last else [(CHUNKS, 16, 3 * width)]
    out_specs = [full(*s) for s in ends] + [rowed]
    out_shape = [shape(s, bf16) for s in ends] + [shape((blocks, pad, LANES), f32)]
    if not last:
        out_specs.append(full(2 * LANES, model))
        out_shape.append(shape((2 * LANES, model), f32))
    return pl.pallas_call(
        functools.partial(scores_kernel, head, ctx_pad, parts),
        grid_spec=pltpu.PrefetchScalarGridSpec(
            num_scalar_prefetch=1,
            grid=(blocks,),
            in_specs=[pl.BlockSpec((1, 1, pad, ctx_pad), lambda b, *_: (b, head, 0, 0)),
                      pl.BlockSpec((1, 1, pad, 3 * width), lambda b, *_: (b, head, 0, 0)),
                      pl.BlockSpec((1, pad, width), lambda b, *_: (b, 0, head)),
                      rowed,
                      pl.BlockSpec((1, pad, model + LANES), lambda b, *_: (b, 0, 0)),
                      pl.BlockSpec((1, 3 * width, model), lambda b, *_: (head, 0, 0)),
                      pl.BlockSpec((1, 3 * width, 2 * LANES), lambda b, *_: (head, 0, 0)),
                      rowed, full(2 * LANES, model)] + [full(*d.shape) for d in done if last],
            out_specs=out_specs,
            scratch_shapes=[pltpu.VMEM((pad, ctx_pad), bf16), pltpu.VMEM((pad, 2 * width), bf16), pltpu.VMEM((pad, 3 * width), bf16),
                            pltpu.VMEM((model + LANES, 3 * width), f32), pltpu.VMEM((2 * LANES, model), f32)],
        ),
        out_shape=out_shape,
        compiler_params=params(0),
        cost_estimate=cost(10, 1),
        name="score_grads",
    )(place, e, qkv, back, shift, low, w_head, w_rows, d_rows, aug, *(done if last else ()))


def spread_kernel(span, own, ids, rows, out_o, *tables):
    blocks = rows.shape[0]
    count, feats, col_width, _ = out_o.shape
    for table in tables:
        table[...] = jnp.zeros_like(table)
    each = len(tables) // blocks if len(tables) > 1 else 1
    run = span // each
    unit = next(u for u in (10, 5, 2, 1) if run % u == 0)

    def add(i, _):
        for u in range(unit):
            for t in range(blocks * each):
                block, at = t // each, t % each * run + i * unit + u
                table = tables[t % len(tables)]
                spot = pl.ds(ids[block * span + at], 1)
                table[spot, :] += rows[block, pl.ds(at, 1), :]
        return 0

    lax.fori_loop(0, run // unit, add, 0)

    def fold(g, _):
        spot = pl.ds(pl.multiple_of(g * own, own), own)
        total = tables[0][spot, :]
        for table in tables[1:]:
            total = total + table[spot, :]
        total = total.T
        for f in range(feats):
            at = f * (col_width + 1)
            out_o[g, f] = total[at:at + col_width].astype(bf16)
        return 0

    lax.fori_loop(0, count, fold, 0)


def spread(ids, rows, count, feats, col_width, own):
    span = ids.shape[0] // rows.shape[0]
    tables = 4 if count <= 8 and span % 2 == 0 else 1
    return pl.pallas_call(
        functools.partial(spread_kernel, span, own),
        grid_spec=pltpu.PrefetchScalarGridSpec(
            num_scalar_prefetch=1,
            grid=(1,),
            in_specs=[pl.BlockSpec(rows.shape, lambda *_: (0, 0, 0))],
            out_specs=pl.BlockSpec((count, feats, col_width, own), lambda *_: (0, 0, 0, 0)),
            scratch_shapes=[pltpu.VMEM((count * own, LANES), f32)] * tables,
        ),
        out_shape=jax.ShapeDtypeStruct((count, feats, col_width, own), bf16),
        compiler_params=params(0),
        cost_estimate=cost(7, 1),
        name="spread",
    )(ids, rows)


def chosen(p, near, far):
    half = CHUNKS // 2
    at = p % half
    return lambda *spot: jnp.where(p < half, near[(at, *spot)].astype(f32), far[(at, *spot)].astype(f32))


def finish_kernel(place, near, far, out_o, in_o, back_o):
    step = pl.program_id(0)
    model = out_o.shape[1]
    each = out_o.shape[0] // 16
    for u in range(each):
        take = chosen((step * each + u) ^ place[0], near, far)
        rows = slice(u * 16, (u + 1) * 16)
        out_o[rows, :] = take(slice(0, 16))
        for j in range(2):
            in_o[rows, j * model:(j + 1) * model] = take(slice(16 + 16 * j, 32 + 16 * j))
        back_o[u * 32:(u + 1) * 32, :] = take(slice(48, 80))


def finish(place, near, far):
    model = near.shape[2]
    steps = 8
    shapes = [(model, model), (model, 2 * model), (2 * model, model)]
    return pl.pallas_call(
        finish_kernel,
        grid_spec=pltpu.PrefetchScalarGridSpec(
            num_scalar_prefetch=1,
            grid=(steps,),
            in_specs=[pl.BlockSpec(a.shape, lambda *_: (0, 0, 0)) for a in (near, far)],
            out_specs=[pl.BlockSpec((s[0] // steps, s[1]), lambda i, *_: (i, 0)) for s in shapes],
        ),
        out_shape=[jax.ShapeDtypeStruct(s, f32) for s in shapes],
        compiler_params=params(0),
        cost_estimate=cost(5, 1),
        name="finish",
    )(place, near, far)


def finish_tail_kernel(col_width, classes, place, near, far, q_o, k_o, v_o, enc_o, bias_o, mark_o, wide_o, *refs):
    lines, aug = refs[:-1], refs[-1]
    step = pl.program_id(0)
    model = q_o.shape[1]
    width = model // HEADS
    half = model // 2
    each = q_o.shape[0] // 16
    for u in range(each):
        take = chosen((step * each + u) ^ place[0], near, far)
        rows = slice(u * 16, (u + 1) * 16)
        for head in range(HEADS):
            cols = slice(head * width, (head + 1) * width)
            for j, ref in enumerate((q_o, k_o, v_o)):
                at = (head * 3 + j) * width
                ref[rows, cols] = take(slice(None), slice(at, at + width))

    @pl.when(step == 0)
    def _():
        for c in range(CHUNKS):
            take = chosen(c ^ place[0], near, far)
            aug[c // 2 * 16:c // 2 * 16 + 16, c % 2 * half:(c % 2 + 1) * half] = take(slice(None), slice(3 * model, None))
        feats = enc_o.shape[0] // col_width
        for f in range(feats):
            enc_o[f * col_width:(f + 1) * col_width, :] = aug[f * (col_width + 1):f * (col_width + 1) + col_width, :]
        at = feats * (col_width + 1)
        mark_o[...] = aug[at:at + classes, :]
        bias_o[...] = aug[at + classes:at + classes + 1, :]
        for j in range(2):
            wide_o[:, j * model:(j + 1) * model] = aug[LANES + 6 + j:LANES + 7 + j, :]
        for line, row in zip(lines, (0, 1, 2, 3, 4, 5, 8, 9)):
            line[...] = aug[LANES + row:LANES + row + 1, :]


def finish_tail(place, near, far, model, feat_total, col_width, classes):
    steps = 8
    shapes = [(model, model)] * 3
    singles = [(feat_total, model), (1, model), (classes, model), (1, 2 * model)] + [(1, model)] * 8
    full = lambda *s: pl.BlockSpec(s, lambda *_: (0,) * len(s))
    return pl.pallas_call(
        functools.partial(finish_tail_kernel, col_width, classes),
        grid_spec=pltpu.PrefetchScalarGridSpec(
            num_scalar_prefetch=1,
            grid=(steps,),
            in_specs=[full(*a.shape) for a in (near, far)],
            out_specs=[pl.BlockSpec((s[0] // steps, s[1]), lambda i, *_: (i, 0)) for s in shapes] + [full(*s) for s in singles],
            scratch_shapes=[pltpu.VMEM((2 * LANES, model), f32)],
        ),
        out_shape=[jax.ShapeDtypeStruct(s, f32) for s in shapes + singles],
        compiler_params=params(0),
        cost_estimate=cost(5, 1),
        name="finish_tail",
    )(place, near, far)


SLOTS = (0, 1, 0, 1, 1)
SPAN = 64.0


def swap(value, axis, bit):
    size = lax.axis_size(axis)
    return lax.ppermute(value, axis, [(i, i ^ bit) for i in range(size)])


def rounded(value):
    return lax.reduce_precision(value, 8, 7)


def exchange(value, axis):
    return lax.all_to_all(value, axis, split_axis=0, concat_axis=0, tiled=True)


def chunk_steps(keep, give, bits):
    split = CHUNKS.bit_length() - 1
    for at, (axis, bit) in enumerate(bits):
        came = swap(give, axis, bit)
        if at + 1 < split:
            half = keep.shape[0] // 2
            give = (keep[half:].astype(f32) + came[half:].astype(f32)).astype(bf16)
            keep = keep[:half].astype(f32) + came[:half].astype(f32)
        else:
            give = keep = (keep.astype(f32) + came.astype(f32)).astype(bf16)
        fixed = yield give
        if fixed is not None:
            give = fixed
    for axis, bit in reversed(bits[1:split]):
        keep = jnp.concatenate([keep, swap(keep, axis, bit)], 0)
        yield keep
    yield keep, swap(keep, *bits[0])


def body(
    raw_rows, enc_weight, enc_bias, label_table, w_query, b_query, w_key, w_value, b_value, w_out, b_out,
    gain_one, shift_one, w_in, b_in, w_back, b_back, gain_two, shift_two, members, labels, queries, cotangent,
):
    row_count = lax.axis_size("rows")
    feat_count = lax.axis_size("feat")
    row_index = lax.axis_index("rows")
    feat_index = lax.axis_index("feat")
    local_rows, col_width = raw_rows.shape
    own_rows = local_rows // feat_count
    feat_total = col_width * feat_count
    feat_span = feat_total + feat_count
    model = enc_weight.shape[1]
    width = model // HEADS
    classes = label_table.shape[0]
    blocks, span = members.shape
    ctx_len = labels.shape[1]
    pad = round_up(span, 16)
    row_total = float(local_rows * row_count)
    bits = [(axis, 1 << b) for axis in ("feat", "rows") for b in range(lax.axis_size(axis).bit_length() - 1)]
    place = jnp.int32(0)
    for at, (axis, bit) in enumerate(bits[:CHUNKS.bit_length() - 1]):
        place = place + lax.axis_index(axis) // bit % 2 * (CHUNKS >> (at + 1))
    place = place.reshape(1).astype(jnp.int32)
    row = lambda a: a.reshape(1, -1)

    columns = raw_rows.T
    origin = rounded(jnp.mean(columns, 1, keepdims=True))
    moved = columns - origin
    sums = [origin[:, 0]]
    for value, scales in ((jnp.mean(moved, 1), (1.0, 1024.0, 1048576.0)), (jnp.mean(moved * moved, 1), (0.0625, 64.0, 65536.0))):
        for scale in scales:
            top = lax.reduce_precision(value * scale, 5, 10)
            sums.append(top)
            value = value - top / scale
    moved = moved * SPAN
    notes = jnp.pad(jnp.stack(sums), ((0, 1), (0, 32 - col_width))).reshape(1, 1, 2 * LANES)
    notes = jnp.broadcast_to(jnp.pad(notes, ((0, 0), (0, 0), (0, own_rows - 2 * LANES))), (feat_count, 1, own_rows))
    moved = moved.reshape(col_width, feat_count, own_rows).transpose(1, 0, 2)
    sent = jnp.concatenate([moved, notes], 1).astype(jnp.float16)
    owned = exchange(sent, "feat").reshape(1, feat_span, own_rows)
    near = jnp.concatenate([owned] + [swap(owned, "rows", bits) for bits in (2, 4, 6)], 0)
    for bit in range(3, row_count.bit_length() - 1):
        near = jnp.concatenate([near, swap(near, "rows", 1 << bit)], 0)
    far = swap(near, "rows", 1)
    groups = jnp.concatenate([near[:, col_width::col_width + 1, :2 * LANES], far[:, col_width::col_width + 1, :2 * LANES]], 0)
    notes = groups.astype(f32).reshape(row_count, feat_count, 8, 32)[:, :, :, :col_width]
    origins = notes[:, :, 0]
    first_means = notes[:, :, 1] + notes[:, :, 2] / 1024.0 + notes[:, :, 3] / 1048576.0
    square_means = notes[:, :, 4] * 16.0 + notes[:, :, 5] / 64.0 + notes[:, :, 6] / 65536.0
    col_mean = jnp.mean(origins + first_means, 0)
    apart = origins - col_mean
    factor = lax.rsqrt(jnp.mean(square_means + apart * (2.0 * first_means + apart), 0) + epsilon)
    wider = lambda v: jnp.pad(v, ((0, 0), (0, 0), (0, 1))).reshape(v.shape[0], feat_span, 1)
    apart, slope = wider(apart), wider(factor[None])
    standard = lambda part, off: ((part.astype(f32) * (1.0 / SPAN) + off) * slope).astype(bf16)
    near, far = standard(near, apart[:row_count // 2]), standard(far, apart[row_count // 2:])
    source = members // local_rows
    ids_back = (source * own_rows + members % own_rows).reshape(-1)
    source = source ^ row_index
    source = ((source >> 1) & 3) + 4 * (source >> 3) + (source & 1) * (row_count // 2)
    ids = (source * own_rows + members % own_rows).reshape(-1)

    spaced = jnp.pad(enc_weight.reshape(feat_count, col_width, model), ((0, 0), (0, 1), (0, 0))).reshape(feat_span, model)
    w_feat = jnp.pad(spaced, ((0, LANES - feat_span), (0, 0)))
    w_mark = jnp.pad(label_table, ((feat_span, LANES - feat_span - classes), (0, 0)))
    b_enc = row(enc_bias)
    mark = jnp.pad(labels, ((0, 0), (0, pad - ctx_len)), constant_values=-2 * LANES)[:, :, None]
    cut = lambda w: w.reshape(model, HEADS, 1, width)
    w_qkv = jnp.concatenate([cut(w_query), cut(w_key), cut(w_value)], 2).reshape(model, 3 * model)
    edge = lambda b: b.reshape(1, HEADS, 1, width)
    b_qkv = jnp.concatenate([edge(b_query), edge(jnp.zeros_like(b_query)), edge(b_value)], 2).reshape(1, 3 * model)
    w_heads = w_qkv.T.reshape(HEADS, 3 * width, model)
    w_feat_t = w_feat.T
    w_rows = jnp.einsum("hkd,df->hkf", w_heads, w_feat_t, preferred_element_type=f32)
    high = rounded(w_rows)
    w_rows = jnp.concatenate([high, w_rows - high], 2).astype(bf16)
    tiles = model // LANES
    flat = cotangent.transpose(1, 0, 2).reshape(span, blocks, tiles, LANES).transpose(0, 2, 1, 3).reshape(-1, LANES)

    feats = fetch(ids, near, far, mark, feat_span, classes)
    weights = (w_feat, w_mark, b_enc, w_qkv, b_qkv, w_out, row(b_out), row(gain_one), row(shift_one), w_in, row(b_in),
               w_back, row(b_back), row(gain_two), row(shift_two), w_feat_t)
    low, qkv, expo, layer_out, d_rows, back, shift, keep, give, aug = forward(place, queries, feats, flat, weights, ctx_len)
    layer_out = layer_out.reshape(span, tiles, blocks, LANES).transpose(0, 2, 1, 3).reshape(span, blocks, model).transpose(1, 0, 2)

    steps = chunk_steps(keep, give, bits)
    done = []
    for head in range(HEADS):
        for _ in range(SLOTS[head]):
            held, back = lax.optimization_barrier((next(steps), back))
        made = score_grads(place, head, expo, qkv, back, shift, low, w_heads, w_rows, d_rows, aug, done)
        if head < HEADS - 1:
            head_grads, d_rows, aug = made
            done.append(head_grads)
        else:
            keep, give, d_rows = made
    tail = chunk_steps(keep, give, bits)
    for _ in range(SLOTS[HEADS]):
        held, d_rows = lax.optimization_barrier((next(steps), d_rows))

    d_table = spread(ids_back, d_rows, row_count, feat_count, col_width, own_rows)
    held, d_table = lax.optimization_barrier((next(tail), d_table))
    tail.send(held)
    d_table = exchange(d_table.reshape(row_count * feat_count, col_width, own_rows), ("rows", "feat"))
    d_columns = jnp.sum(d_table.reshape(row_count, feat_count, col_width, own_rows).astype(f32), 0)
    d_columns = d_columns.transpose(1, 0, 2).reshape(col_width, local_rows)
    for ends in tail:
        pass
    (g_query, g_key, g_value, g_enc, g_enc_bias, g_table, g_b_in, g_b_out, g_gain_one, g_shift_one, g_b_back, g_gain_two,
     g_shift_two, g_b_query, g_b_value) = finish_tail(place, *ends, model, feat_total, col_width, classes)
    for ends in steps:
        pass
    g_out, g_in, g_back = finish(place, *ends)

    at = feat_index * col_width
    weight = lax.dynamic_slice_in_dim(enc_weight, at, col_width, 0).astype(f32)
    stat_one = jnp.sum(weight * g_enc_bias, 1)
    stat_two = jnp.sum(weight * lax.dynamic_slice_in_dim(g_enc, at, col_width, 0), 1)
    col_mean = lax.dynamic_slice_in_dim(col_mean, feat_index, 1, 0)[0]
    factor = lax.dynamic_slice_in_dim(factor, feat_index, 1, 0)[0]
    d_spread = -0.5 * stat_two * factor * factor
    d_mean = -factor * stat_one - 2.0 * d_spread * col_mean
    raw_grad = factor[:, None] * d_columns + (d_mean[:, None] + 2.0 * d_spread[:, None] * columns) / row_total
    flatten = lambda a: a.reshape(-1)
    return (
        layer_out, raw_grad.T, g_enc, flatten(g_enc_bias), g_table, g_query, flatten(g_b_query), g_key, g_value,
        flatten(g_b_value), g_out, flatten(g_b_out), flatten(g_gain_one), flatten(g_shift_one), g_in, flatten(g_b_in), g_back,
        flatten(g_b_back), flatten(g_gain_two), flatten(g_shift_two),
    )


def solution(mesh):
    both = ("rows", "feat")
    placed = (P("rows", "feat"),) + (P(),) * 18 + (P(both, None), P(both, None), P(both), P(both, None, None))
    results = (P(both, None, None), P("rows", "feat")) + (P(),) * 18
    return jax.shard_map(body, mesh=mesh, in_specs=placed, out_specs=results, check_vma=False)
```

```python
import functools
import math

import jax
import jax.numpy as jnp
from jax import lax
from jax.experimental import pallas as pl
from jax.experimental.pallas import tpu as pltpu
from jax.sharding import PartitionSpec as P

HEADS = 4
LANES = 128
epsilon = 1e-05
CHUNKS = 32
SMALLS = 120
SPAN = 64.0
VMEM_LIMIT = 60 * 1024 * 1024
f32 = jnp.float32
bf16 = jnp.bfloat16


def dot(left, right):
    return jnp.dot(left, right, preferred_element_type=f32)


def dot_nt(left, right):
    return lax.dot_general(left, right, (((1,), (1,)), ((), ())), preferred_element_type=f32)


def dot_tn(left, right):
    return lax.dot_general(left, right, (((0,), (0,)), ((), ())), preferred_element_type=f32)


def round_up(value, unit):
    return -(-value // unit) * unit


def row_chunks(span):
    for parts in (3, 2, 1):
        if span % (16 * parts) == 0:
            return parts
    return 1


def cost(gigaflops, megabytes):
    return pl.CostEstimate(flops=int(gigaflops * 1e9), bytes_accessed=int(megabytes * 1e6), transcendentals=0)


def params(*names, room=VMEM_LIMIT):
    room = min(room, VMEM_LIMIT)
    return pltpu.CompilerParams(vmem_limit_bytes=room, dimension_semantics=("arbitrary",) * len(names))


def fetch_kernel(span, feats, classes, ids, near, far, labels, feats_o, stats_o, table, rows_f, notes, origins):
    count, deep, own = near.shape
    each = deep // feats
    blocks, pad, _ = feats_o.shape
    unit = next(u for u in (50, 20, 10, 5, 2, 1) if span % u == 0)
    total = 2 * count
    lane = lax.broadcasted_iota(jnp.int32, (total, LANES), 1)
    mean_row, factor_row, origin_rows = 0.0, 0.0, 0.0
    for f in range(feats):
        for half, ref in enumerate((near, far)):
            def collect(g, _):
                notes[pl.ds(half * count + g, 1), :] = ref[g, (f + 1) * each - 1:(f + 1) * each, :2 * LANES]
                return 0

            lax.fori_loop(0, count, collect, 0)
        start, other = notes[:, :LANES], notes[:, LANES:]
        back = lambda v, by: pltpu.roll(v, LANES - by, 1)
        place = lambda v: pltpu.roll(jnp.where(lane < each - 1, v, 0.0), f * each, 1) if f else jnp.where(lane < each - 1, v, 0.0)
        first = back(start, 32) + back(start, 64) * (1.0 / 1024.0) + back(start, 96) * (1.0 / 1048576.0)
        square = other * 16.0 + back(other, 32) * (1.0 / 64.0) + back(other, 64) * (1.0 / 65536.0)
        middle_of = jnp.sum(start + first, 0, keepdims=True) * (1.0 / total)
        apart = start - middle_of
        spread_of = jnp.sum(square + apart * (2.0 * first + apart), 0, keepdims=True) * (1.0 / total)
        spread_of = jnp.where(lane[:1] < each - 1, spread_of, 1.0)
        full = lambda v: jnp.broadcast_to(v, (total, LANES))
        mean_row = mean_row + place(full(middle_of))
        factor_row = factor_row + place(full(lax.rsqrt(spread_of + epsilon)))
        origin_rows = origin_rows + place(start)
    origins[...] = origin_rows
    stats_o[0:1, :] = mean_row[0:1]
    stats_o[1:2, :] = factor_row[0:1]

    for half, ref in enumerate((near, far)):
        def unfold(g, _):
            piece = jnp.concatenate([ref[g], jnp.zeros((LANES - deep, own), f32)], 0).T
            at = half * count + g
            table[pl.ds(pl.multiple_of(at * own, own), own), :] = piece * (1.0 / SPAN) + origins[pl.ds(at, 1), :]
            return 0

        lax.fori_loop(0, count, unfold, 0)
    rows_f[pad - 16:, :] = jnp.zeros((16, LANES), f32)
    kind = lax.broadcasted_iota(jnp.int32, (16, pad), 0)
    pick = (lax.broadcasted_iota(jnp.int32, (16, LANES), 0) + deep == lax.broadcasted_iota(jnp.int32, (16, LANES), 1))
    pick = pick.astype(f32).astype(bf16)
    lane = lax.broadcasted_iota(jnp.int32, (pad, LANES), 1)
    for block in range(blocks):
        def fetch(i, _):
            for u in range(unit):
                at = i * unit + u
                rows_f[pl.ds(at, 1), :] = table[pl.ds(ids[block * span + at], 1), :]
            return 0

        lax.fori_loop(0, span // unit, fetch, 0)
        hot = ((kind == labels[block:block + 1, :]) | (kind == classes)).astype(f32).astype(bf16)
        scaled = (rows_f[...] - mean_row[0:1]) * factor_row[0:1]
        feats_o[block] = jnp.where(lane < deep, scaled, dot_tn(hot, pick)).astype(bf16)


def fetch(ids, near, far, labels, feats, classes):
    blocks, pad = labels.shape
    whole = lambda *s: pl.BlockSpec(s, lambda *_: (0,) * len(s), pipeline_mode=pl.Buffered(1))
    full = lambda *s: pl.BlockSpec(s, lambda *_: (0,) * len(s))
    total = 2 * near.shape[0]
    return pl.pallas_call(
        functools.partial(fetch_kernel, ids.shape[0] // blocks, feats, classes),
        grid_spec=pltpu.PrefetchScalarGridSpec(
            num_scalar_prefetch=1,
            grid=(1,),
            in_specs=[whole(*near.shape), whole(*far.shape), whole(*labels.shape)],
            out_specs=[full(blocks, pad, LANES), full(8, LANES)],
            scratch_shapes=[pltpu.VMEM((total * near.shape[2], LANES), f32), pltpu.VMEM((pad, LANES), f32),
                            pltpu.VMEM((total, 2 * LANES), f32), pltpu.VMEM((total, LANES), f32)],
        ),
        out_shape=[jax.ShapeDtypeStruct((blocks, pad, LANES), bf16), jax.ShapeDtypeStruct((8, LANES), f32)],
        compiler_params=params(0, room=(12 << 20) + 16 * total * near.shape[2] * LANES),
        cost_estimate=cost(6, 1),
        name="fetch",
    )(ids, near, far, labels)


def embed(feats, w_embed, b_enc):
    both = dot(feats, w_embed[...])
    model = both.shape[1] // 2
    slots = (both[:, :model] + b_enc[...]).astype(bf16)
    return slots.astype(f32) + both[:, model:]


def norm_parts(values):
    centre = jnp.mean(values, -1, keepdims=True)
    offset = values - centre
    second = jnp.mean(offset * offset, -1, keepdims=True)
    root = lax.rsqrt(second + epsilon)
    return offset * root, root


def norm_back(grad, unit, root):
    return root * (grad - jnp.mean(grad, -1, keepdims=True) - unit * jnp.mean(grad * unit, -1, keepdims=True))


def forward_kernel(blocks, ctx_len, ctx_pad, parts,
                   place, queries, feats, cot, w_embed, b_enc, w_qkv, b_qkv, w_out, b_out, gain_one, shift_one,
                   w_in, b_in, w_back, b_back, gain_two, shift_two, w_out_t,
                   qkv_o, e_o, out_o, rows_o, back_o, shift_o, keep_o, give_o, aug_o,
                   mixed, inv, out_f, act_s, norm_s, d_hid_s, d_bra_s, d_att_s, g_out, g_in, g_back, wide, narrow):
    tick = pl.program_id(0)
    pad = qkv_o.shape[2]
    model = back_o.shape[2]
    step = pad // parts
    width = model // HEADS

    @pl.when(tick < blocks * HEADS)
    def _():
        block = tick // HEADS
        head = tick % HEADS

        @pl.when(head == 0)
        def _():
            def project(c, _):
                rows = pl.ds(pl.multiple_of(c * step, 16), step)
                low = embed(feats[block, rows, :], w_embed, b_enc).astype(bf16)
                made = (dot(low, w_qkv[...]) + b_qkv[...]).astype(bf16)
                for h in range(HEADS):
                    qkv_o[0, h, rows, :] = made[:, h * 3 * width:(h + 1) * 3 * width]
                return 0

            lax.fori_loop(0, parts, project, 0)

        factor = math.log2(math.e) / math.sqrt(width)
        keys = qkv_o[0, head, :ctx_pad, width:2 * width]
        vals = jnp.concatenate([qkv_o[0, head, :ctx_pad, 2 * width:], jnp.ones((ctx_pad, width), bf16)], 1)
        edge = ctx_len // LANES * LANES
        cols = pl.ds(pl.multiple_of(head * width, LANES), width)
        spans = [slice(c * step, (c + 1) * step) for c in range(parts)]

        def score(c):
            return dot_nt(qkv_o[0, head, spans[c], :width], keys)

        def weigh(c, scores):
            front = scores[:, :edge]
            most = jnp.max(front, 1, keepdims=True)
            if edge < ctx_pad:
                lane = lax.broadcasted_iota(jnp.int32, (step, ctx_pad - edge), 1)
                rear = jnp.where(lane < ctx_len - edge, scores[:, edge:], -1e30)
                most = jnp.maximum(most, jnp.max(rear, 1, keepdims=True))
                e_o[0, 0, spans[c], edge:] = jnp.exp2((rear - most) * factor).astype(bf16)
            e_o[0, 0, spans[c], :edge] = jnp.exp2((front - most) * factor).astype(bf16)

        def mix(c):
            summed = dot(e_o[0, 0, spans[c], :], vals)
            inverse = 1.0 / summed[:, width:]
            lane = lax.broadcasted_iota(jnp.int32, (step, LANES), 1)
            inv[block, spans[c], :] = jnp.where(lane == head, inverse[:, :LANES], inv[block, spans[c], :])
            mixed[block, spans[c], cols] = (summed[:, :width] * inverse).astype(bf16)

        ready = score(0)
        for c in range(parts):
            coming = score(c + 1) if c + 1 < parts else None
            weigh(c, ready)
            mix(c)
            ready = coming

    @pl.when(tick >= blocks * HEADS)
    def _():
        part = tick - blocks * HEADS

        @pl.when(part == 0)
        def _():
            for ref in (g_out, g_in, g_back, wide, narrow):
                ref[...] = jnp.zeros_like(ref)

        tiles = model // LANES
        rows = pl.ds(pl.multiple_of(part * step, 16), step)
        total = lambda v: jnp.sum(v, 0, keepdims=True)
        wide_t, narrow_t = [], [[] for _ in range(6)]

        def flow(block):
            here = slice(block * step, (block + 1) * step)
            mixed_low = mixed[block, rows, :]
            reached = embed(feats[block, rows, :], w_embed, b_enc) + dot(mixed_low, w_out[...])
            yield
            unit_one, root_one = norm_parts(reached + b_out[...])
            normed = unit_one * gain_one[...] + shift_one[...]
            norm_s[here, :] = normed.astype(bf16)
            yield
            hidden = dot(norm_s[here, :], w_in[...])
            yield
            hidden = hidden + b_in[...]
            slant = math.sqrt(2.0 / math.pi)
            square = hidden * hidden
            half = 0.5 * jnp.tanh(hidden * (slant + (slant * 0.044715) * square)) + 0.5
            active = hidden * half
            act_s[here, :] = active.astype(bf16)
            slope = half + active * (1.0 - half) * (2.0 * slant + (6.0 * slant * 0.044715) * square)
            yield
            branch = dot(act_s[here, :], w_back[...])
            yield
            unit_two, root_two = norm_parts(normed + (branch + b_back[...]))
            row = part * step + lax.broadcasted_iota(jnp.int32, (step, 1), 0)
            alive = row < ctx_len + queries[block]
            result = jnp.where(alive, unit_two * gain_two[...] + shift_two[...], 0.0)
            given = []
            for j in range(tiles):
                lanes = pl.ds(j * blocks + block, step, stride=tiles * blocks)
                out_f[lanes, :] = result[:, j * LANES:(j + 1) * LANES]
                given.append(cot[lanes, :])
            grad = jnp.where(alive, jnp.concatenate(given, 1), 0.0)
            second = norm_back(grad * gain_two[...], unit_two, root_two)
            d_bra_s[here, :] = second.astype(bf16)
            narrow_t[3].append(total(d_bra_s[here, :].astype(f32)))
            narrow_t[4].append(total(grad * unit_two))
            narrow_t[5].append(total(grad))
            yield
            d_act = dot_nt(d_bra_s[here, :], w_back[...])
            yield
            d_hid = (slope * d_act).astype(bf16)
            d_hid_s[here, :] = d_hid
            wide_t.append(total(d_hid.astype(f32)))
            yield
            d_norm = dot_nt(d_hid_s[here, :], w_in[...])
            yield
            grad_one = second + d_norm
            narrow_t[1].append(total(grad_one * unit_one))
            narrow_t[2].append(total(grad_one))
            first = norm_back(grad_one * gain_one[...], unit_one, root_one)
            d_att_s[here, :] = first.astype(bf16)
            narrow_t[0].append(total(d_att_s[here, :].astype(f32)))
            yield
            both = dot(d_att_s[here, :], w_out_t[...])
            yield
            rows_o[block] = both[:, model:]
            back = both[:, :model].astype(bf16).astype(f32)
            lane = lax.broadcasted_iota(jnp.int32, (step, LANES), 1)
            shifts = jnp.zeros((step, LANES), f32)
            for h in range(HEADS):
                cols = slice(h * width, (h + 1) * width)
                scaled = (back[:, cols] * inv[block, rows, h:h + 1]).astype(bf16)
                back_o[block, :, cols] = scaled
                moved = jnp.sum(scaled.astype(f32) * mixed_low[:, cols].astype(f32), 1, keepdims=True)
                shifts = jnp.where(lane == h, -moved, shifts)
            shift_o[block] = shifts
            yield

        flows = [flow(block) for block in range(blocks)]
        for item in flows:
            next(item)
        for turn in range(6):
            for item in flows:
                next(item)
                next(item, None)
            if turn == 2:
                g_back[...] += dot_tn(act_s[...], d_bra_s[...])
            if turn == 3:
                g_in[...] += dot_tn(norm_s[...], d_hid_s[...])
            if turn == 4:
                both = jnp.concatenate([jnp.concatenate([mixed[block, rows, :], feats[block, rows, :]], 1) for block in range(blocks)], 0)
                g_out[...] += dot_tn(both, d_att_s[...])
        out_o[...] = out_f[...].astype(bf16)
        wide[0:1, :] += sum(wide_t[1:], wide_t[0])
        for at in range(6):
            narrow[at:at + 1, :] += sum(narrow_t[at][1:], narrow_t[at][0])

        @pl.when(part == parts - 1)
        def _():
            def lay(start, ref, p, _):
                at = pl.multiple_of((p ^ place[0]) * 16, 16)
                other = pl.multiple_of((p ^ place[1]) * 32, 32)
                ref[p - start, 0:16, :] = g_out[pl.ds(at, 16), :].astype(bf16)
                for j in range(2):
                    ref[p - start, 16 + 16 * j:32 + 16 * j, :] = g_in[pl.ds(at, 16), j * model:(j + 1) * model].astype(bf16)
                ref[p - start, 48:80, :] = g_back[pl.ds(other, 32), :].astype(bf16)
                return 0

            for start, ref in ((0, keep_o), (CHUNKS // 2, give_o)):
                lax.fori_loop(start, start + CHUNKS // 2, functools.partial(lay, start, ref), 0)
            aug_o[...] = g_out[model:, :]
            aug_o[SMALLS:SMALLS + 6, :] = narrow[0:6, :]
            for j in range(2):
                aug_o[SMALLS + 6 + j:SMALLS + 7 + j, :] = wide[0:1, j * model:(j + 1) * model]


def forward(place, queries, feats, cot, weights, ctx_len):
    blocks, pad, _ = feats.shape
    model = weights[2].shape[0]
    inner = weights[8].shape[1]
    width = model // HEADS
    ctx_pad = round_up(ctx_len, LANES)
    parts = row_chunks(pad)
    step = pad // parts
    early = blocks * HEADS
    flat = blocks * model // LANES
    attending = lambda t: jnp.minimum(t, early - 1)
    later = lambda t: jnp.maximum(t - early, 0)
    once = lambda a: pl.BlockSpec(a.shape, lambda *_: (0,) * a.ndim, pipeline_mode=pl.Buffered(1))
    full = lambda *s: pl.BlockSpec(s, lambda *_: (0,) * len(s))
    rowed = lambda w: pl.BlockSpec((blocks, step, w), lambda t, *_: (0, later(t), 0))
    shape = jax.ShapeDtypeStruct
    return pl.pallas_call(
        functools.partial(forward_kernel, blocks, ctx_len, ctx_pad, parts),
        grid_spec=pltpu.PrefetchScalarGridSpec(
            num_scalar_prefetch=2,
            grid=(early + parts,),
            in_specs=[once(feats), pl.BlockSpec((step * flat, LANES), lambda t, *_: (later(t), 0))] + [once(a) for a in weights],
            out_specs=[
                pl.BlockSpec((1, HEADS, pad, 3 * width), lambda t, *_: (attending(t) // HEADS, 0, 0, 0)),
                pl.BlockSpec((1, 1, pad, ctx_pad), lambda t, *_: (attending(t) // HEADS, attending(t) % HEADS, 0, 0)),
                pl.BlockSpec((step * flat, LANES), lambda t, *_: (later(t), 0)),
                rowed(LANES), rowed(model), rowed(LANES),
                full(CHUNKS // 2, 80, model), full(CHUNKS // 2, 80, model), full(LANES, model)],
            scratch_shapes=[
                pltpu.VMEM((blocks, pad, model), bf16), pltpu.VMEM((blocks, pad, LANES), f32), pltpu.VMEM((step * flat, LANES), f32),
                pltpu.VMEM((blocks * step, inner), bf16), pltpu.VMEM((blocks * step, model), bf16),
                pltpu.VMEM((blocks * step, inner), bf16), pltpu.VMEM((blocks * step, model), bf16),
                pltpu.VMEM((blocks * step, model), bf16), pltpu.VMEM((model + LANES, model), f32), pltpu.VMEM((model, inner), f32),
                pltpu.VMEM((inner, model), f32), pltpu.VMEM((8, inner), f32), pltpu.VMEM((8, model), f32)],
        ),
        out_shape=[
            shape((blocks, HEADS, pad, 3 * width), bf16),
            shape((blocks, HEADS, pad, ctx_pad), bf16), shape(cot.shape, bf16), shape((blocks, pad, LANES), f32),
            shape((blocks, pad, model), bf16), shape((blocks, pad, LANES), f32), shape((CHUNKS // 2, 80, model), bf16),
            shape((CHUNKS // 2, 80, model), bf16), shape((LANES, model), f32)],
        compiler_params=params(0),
        cost_estimate=cost(60, 1),
        name="forward",
    )(place, queries, feats, cot, *weights)


def scores_kernel(start, last, ctx_pad, parts, place, e, qkv, back, shift, feats, w_rows, d_rows, *refs):
    block = pl.program_id(0)
    at = pl.program_id(1)
    count = pl.num_programs(1)
    base = start if last else 0
    if last:
        early, (first, keep_o, give_o, rows_o, ds, dox, d_all, fit) = refs[:-8], refs[-8:]
    else:
        early_o, rows_o, ds, dox, d_all, fit = refs
    pad = back.shape[1]
    step = pad // parts
    width = back.shape[2]
    root = 1.0 / math.sqrt(width)
    keys = qkv[0, 0, :ctx_pad, width:2 * width]
    vals = jnp.concatenate([qkv[0, 0, :ctx_pad, 2 * width:], jnp.ones((ctx_pad, width), bf16)], 1)
    lane = lax.broadcasted_iota(jnp.int32, (pad, width), 1)
    moved = jnp.sum(jnp.where(lane == start + at, shift[0], 0.0), 1, keepdims=True)
    top = moved.astype(bf16).astype(f32)
    dox[:, :width] = back[0]
    dox[:, width:] = jnp.where(lane == 0, top, jnp.where(lane == 1, moved - top, 0.0)).astype(bf16)
    spans = [slice(c * step, (c + 1) * step) for c in range(parts)]

    def score(c):
        return dot_nt(dox[spans[c], :], vals)

    ready = score(0)
    for c in range(parts):
        coming = score(c + 1) if c + 1 < parts else None
        ds[spans[c], :] = e[0, 0, spans[c], :] * ready.astype(bf16)
        d_all[spans[c], :width] = (dot(ds[spans[c], :], keys) * root).astype(bf16)
        ready = coming
    d_all[:ctx_pad, 2 * width:] = dot_tn(back[0], e[0, 0]).T.astype(bf16)
    d_all[:ctx_pad, width:2 * width] = (dot_tn(qkv[0, 0, :, :width], ds[...]) * root).T.astype(bf16)
    d_all[ctx_pad:, width:] = jnp.zeros((pad - ctx_pad, 2 * width), bf16)
    fitted = dot_tn(feats[0], d_all[...])
    pair = dot(d_all[...], w_rows[0])
    made = pair[:, :LANES] + pair[:, LANES:]

    @pl.when(at == 0)
    def _():
        rows_o[0] = d_rows[0] + made

    @pl.when(at > 0)
    def _():
        rows_o[0] += made

    @pl.when(block == 0)
    def _():
        fit[base + at] = fitted

    @pl.when(block > 0)
    def _():
        fit[base + at] += fitted

    @pl.when((block == pl.num_programs(0) - 1) & (at == count - 1))
    def _():
        if not last:
            early_o[...] = fit[...]
        else:
            filled = 0
            for ref in early:
                fit[filled:filled + ref.shape[0]] = ref[...]
                filled += ref.shape[0]
            for turn, ref in enumerate((keep_o, give_o)):
                def lay(p, _):
                    chunk = (turn * (CHUNKS // 2) + p) ^ place[2]
                    rows = pl.ds(pl.multiple_of(chunk // HEADS * 16, 16), 16)
                    head = chunk % HEADS
                    ref[p, :, :3 * width] = fit[head, rows, :].astype(bf16)
                    ref[p, :, 3 * width:] = first[rows, pl.ds(pl.multiple_of(head * width, LANES), width)].astype(bf16)
                    return 0

                lax.fori_loop(0, CHUNKS // 2, lay, 0)


def score_grads(place, start, count, e, qkv, back, shift, feats, w_rows, d_rows, early, first):
    blocks, pad, model = back.shape
    ctx_pad = e.shape[3]
    width = model // HEADS
    parts = row_chunks(pad)
    full = lambda *s: pl.BlockSpec(s, lambda *_: (0,) * len(s))
    rowed = pl.BlockSpec((1, pad, LANES), lambda b, h, *_: (b, 0, 0))
    shape = jax.ShapeDtypeStruct
    last = start + count == HEADS
    late = (*early, first) if last else ()
    ends = [shape((CHUNKS // 2, 16, 4 * width), bf16)] * 2 if last else [shape((count, LANES, 3 * width), f32)]
    return pl.pallas_call(
        functools.partial(scores_kernel, start, last, ctx_pad, parts),
        grid_spec=pltpu.PrefetchScalarGridSpec(
            num_scalar_prefetch=1,
            grid=(blocks, count),
            in_specs=[pl.BlockSpec((1, 1, pad, ctx_pad), lambda b, h, *_: (b, start + h, 0, 0)),
                      pl.BlockSpec((1, 1, pad, 3 * width), lambda b, h, *_: (b, start + h, 0, 0)),
                      pl.BlockSpec((1, pad, width), lambda b, h, *_: (b, 0, start + h)),
                      rowed, rowed,
                      pl.BlockSpec((1, 3 * width, 2 * LANES), lambda b, h, *_: (start + h, 0, 0)),
                      rowed] + [full(*a.shape) for a in late],
            out_specs=[full(*end.shape) for end in ends] + [rowed],
            scratch_shapes=[pltpu.VMEM((pad, ctx_pad), bf16), pltpu.VMEM((pad, 2 * width), bf16), pltpu.VMEM((pad, 3 * width), bf16),
                            pltpu.VMEM((HEADS if last else count, LANES, 3 * width), f32)],
        ),
        out_shape=ends + [shape((blocks, pad, LANES), f32)],
        compiler_params=params(0, 0, room=36 << 20),
        cost_estimate=cost(8 * count, 1),
        name="score_grads",
    )(place, e, qkv, back, shift, feats, w_rows, d_rows, *late)


def spread_kernel(span, own, ids, rows, near_o, far_o, *tables):
    blocks = rows.shape[0]
    count, feats, col_width, _ = near_o.shape
    for table in tables:
        table[...] = jnp.zeros_like(table)
    each = len(tables) // blocks if len(tables) > 1 else 1
    run = span // each
    unit = next(u for u in (10, 5, 2, 1) if run % u == 0)

    def add(i, _):
        for u in range(unit):
            for t in range(blocks * each):
                block, at = t // each, t % each * run + i * unit + u
                table = tables[t % len(tables)]
                spot = pl.ds(ids[block * span + at], 1)
                table[spot, :] += rows[block, pl.ds(at, 1), :]
        return 0

    lax.fori_loop(0, run // unit, add, 0)

    def fold(start, out_o, g, _):
        spot = pl.ds(pl.multiple_of((start + g) * own, own), own)
        total = tables[0][spot, :]
        for table in tables[1:]:
            total = total + table[spot, :]
        total = total.T
        for f in range(feats):
            at = f * (col_width + 1)
            out_o[g, f] = total[at:at + col_width].astype(bf16)
        return 0

    for start, out_o in ((0, near_o), (count, far_o)):
        lax.fori_loop(0, count, functools.partial(fold, start, out_o), 0)


def spread(ids, rows, count, feats, col_width, own):
    span = ids.shape[0] // rows.shape[0]
    tables = 4 if count <= 8 and span % 2 == 0 else 1
    return pl.pallas_call(
        functools.partial(spread_kernel, span, own),
        grid_spec=pltpu.PrefetchScalarGridSpec(
            num_scalar_prefetch=1,
            grid=(1,),
            in_specs=[pl.BlockSpec(rows.shape, lambda *_: (0, 0, 0))],
            out_specs=[pl.BlockSpec((count // 2, feats, col_width, own), lambda *_: (0, 0, 0, 0))] * 2,
            scratch_shapes=[pltpu.VMEM((count * own, LANES), f32)] * tables,
        ),
        out_shape=[jax.ShapeDtypeStruct((count // 2, feats, col_width, own), bf16)] * 2,
        compiler_params=params(0, room=(12 << 20) + 16 * count * own * LANES),
        cost_estimate=cost(7, 1),
        name="spread",
    )(ids, rows)


def chosen(p, near, far):
    half = CHUNKS // 2
    at = p % half
    return lambda *spot: jnp.where(p < half, near[(at, *spot)].astype(f32), far[(at, *spot)].astype(f32))


def finish_kernel(place, near, far, near_q, far_q, out_o, in_o, back_o):
    step = pl.program_id(0)
    model = out_o.shape[1]
    each = out_o.shape[0] // 16
    for u in range(each):
        take = chosen((step * each + u) ^ place[0], near, far)
        rows = slice(u * 16, (u + 1) * 16)
        out_o[rows, :] = take(slice(0, 16))
        for j in range(2):
            in_o[rows, j * model:(j + 1) * model] = take(slice(16 + 16 * j, 32 + 16 * j))
        take = chosen((step * each + u) ^ place[1], near_q, far_q)
        back_o[u * 32:(u + 1) * 32, :] = take(slice(None))


def finish(place, *ends):
    model = ends[0].shape[2]
    steps = 4
    shapes = [(model, model), (model, 2 * model), (2 * model, model)]
    return pl.pallas_call(
        finish_kernel,
        grid_spec=pltpu.PrefetchScalarGridSpec(
            num_scalar_prefetch=1,
            grid=(steps,),
            in_specs=[pl.BlockSpec(a.shape, lambda *_: (0, 0, 0)) for a in ends],
            out_specs=[pl.BlockSpec((s[0] // steps, s[1]), lambda i, *_: (i, 0)) for s in shapes],
        ),
        out_shape=[jax.ShapeDtypeStruct(s, f32) for s in shapes],
        compiler_params=params(0, room=16 << 20),
        cost_estimate=cost(5, 1),
        name="finish",
    )(place, *ends)


def finish_tail_kernel(col_width, classes, place, near, far, w_heads, w_all, q_o, k_o, v_o, enc_o, bias_o, mark_o, b_query_o, b_value_o,
                       wide_o, *refs):
    lines, (fit, aug) = refs[:-2], refs[-2:]
    model = q_o.shape[1]
    width = model // HEADS
    for c in range(CHUNKS):
        rows = slice(c // HEADS * 16, c // HEADS * 16 + 16)
        head = c % HEADS
        take = chosen(c ^ place[2], near, far)
        fit[head, rows, :] = take(slice(None), slice(0, 3 * width)).astype(bf16)
        aug[rows, head * width:(head + 1) * width] = take(slice(None), slice(3 * width, None))
    feats = enc_o.shape[0] // col_width
    ones = feats * (col_width + 1) + classes
    for row in range(6):
        lines[row][...] = aug[SMALLS + row:SMALLS + row + 1, :]
    for j in range(2):
        wide_o[:, j * model:(j + 1) * model] = aug[SMALLS + 6 + j:SMALLS + 7 + j, :]
    kind = lax.broadcasted_iota(jnp.int32, (LANES, 3 * width), 0)
    total = aug[...]
    for head in range(HEADS):
        cols = slice(head * width, (head + 1) * width)
        part = fit[head]
        total = total + dot(part, w_heads[head])
        line = part[ones:ones + 1, :].astype(f32)
        b_query_o[:, cols] = line[:, :width]
        b_value_o[:, cols] = line[:, 2 * width:]
        spread_line = jnp.where((kind > ones) & (kind < ones + 3), line, part.astype(f32)).astype(bf16)
        made = dot_tn(w_all[...], spread_line)
        for j, ref in enumerate((q_o, k_o, v_o)):
            ref[:, cols] = made[:, j * width:(j + 1) * width]
    aug[...] = total
    for f in range(feats):
        enc_o[f * col_width:(f + 1) * col_width, :] = aug[f * (col_width + 1):f * (col_width + 1) + col_width, :]
    mark_o[...] = aug[ones - classes:ones, :]
    bias_o[...] = aug[ones:ones + 1, :]


def finish_tail(place, near, far, w_heads, w_all, feat_total, col_width, classes):
    model = w_all.shape[1]
    width = model // HEADS
    shapes = [(model, model)] * 3 + [(feat_total, model), (1, model), (classes, model), (1, model), (1, model), (1, 2 * model)]
    shapes = shapes + [(1, model)] * 6
    full = lambda *s: pl.BlockSpec(s, lambda *_: (0,) * len(s))
    return pl.pallas_call(
        functools.partial(finish_tail_kernel, col_width, classes),
        grid_spec=pltpu.PrefetchScalarGridSpec(
            num_scalar_prefetch=1,
            grid=(1,),
            in_specs=[full(*a.shape) for a in (near, far, w_heads, w_all)],
            out_specs=[full(*s) for s in shapes],
            scratch_shapes=[pltpu.VMEM((HEADS, LANES, 3 * width), bf16), pltpu.VMEM((LANES, model), f32)],
        ),
        out_shape=[jax.ShapeDtypeStruct(s, f32) for s in shapes],
        compiler_params=params(0, room=20 << 20),
        cost_estimate=cost(5, 1),
        name="finish_tail",
    )(place, near, far, w_heads, w_all)


CALLS = ((0, 2), (2, 2))


def swap(value, axis, bit):
    size = lax.axis_size(axis)
    return lax.ppermute(value, axis, [(i, i ^ bit) for i in range(size)])


def rounded(value):
    return lax.reduce_precision(value, 8, 7)


def exchange(value, axis):
    return lax.all_to_all(value, axis, split_axis=0, concat_axis=0, tiled=True)


def added(*values):
    return sum((value.astype(f32) for value in values[1:]), values[0].astype(f32))


def reduce_chunks(keep, give, cut):
    over_core, over_x, over_y = ("feat", 1), ("feat", 2), ("rows", 1)
    came = swap(give, *over_core)
    half = keep.shape[0] // 2
    both = []
    for rows, first, then in ((slice(None, cut), over_x, over_y), (slice(cut, None), over_y, over_x)):
        mine, theirs = added(keep[:half, rows], came[:half, rows]), added(keep[half:, rows], came[half:, rows]).astype(bf16)
        both.append((mine, theirs, first, then))
    yield both[0][1]
    half = half // 2
    last = []
    for mine, theirs, first, then in both:
        came = swap(theirs, *first)
        last.append((added(mine[:half], came[:half]), added(mine[half:], came[half:]).astype(bf16), then))
    yield last[0][1]
    total = jnp.concatenate([added(mine, swap(theirs, *then)) for mine, theirs, then in last], 1).astype(bf16)
    yield total
    own = added(total[0], *[swap(total[at], "rows", 2 * at) for at in range(1, half)]).astype(bf16)
    for bit in range(3, lax.axis_size("rows").bit_length() - 1):
        own = added(own, swap(own, "rows", 1 << bit)).astype(bf16)
    yield own


def gather_chunks(own, cut):
    over_core, over_x, over_y = ("feat", 1), ("feat", 2), ("rows", 1)
    own = jnp.stack([own] + [swap(own, "rows", 2 * at) for at in range(1, 4)])
    parts = []
    for rows, first, then in ((slice(None, cut), over_x, over_y), (slice(cut, None), over_y, over_x)):
        part = own[:, rows]
        parts.append((jnp.concatenate([part, swap(part, *then)], 0), first))
    near = [jnp.concatenate([part, swap(part, *first)], 0) for part, first in parts]
    return near[0], swap(near[0], *over_core), near[1], swap(near[1], *over_core)


def tail_first(keep, give):
    half = keep.shape[0] // 2
    came = swap(give, "feat", 1)
    return added(keep[:half], came[:half]), added(keep[half:], came[half:]).astype(bf16)


def body(
    raw_rows, enc_weight, enc_bias, label_table, w_query, b_query, w_key, w_value, b_value, w_out, b_out,
    gain_one, shift_one, w_in, b_in, w_back, b_back, gain_two, shift_two, members, labels, queries, cotangent,
):
    row_count = lax.axis_size("rows")
    feat_count = lax.axis_size("feat")
    row_index = lax.axis_index("rows")
    feat_index = lax.axis_index("feat")
    local_rows, col_width = raw_rows.shape
    own_rows = local_rows // feat_count
    feat_total = col_width * feat_count
    feat_span = feat_total + feat_count
    model = enc_weight.shape[1]
    width = model // HEADS
    classes = label_table.shape[0]
    blocks, span = members.shape
    ctx_len = labels.shape[1]
    pad = round_up(span, 16)
    row_total = float(local_rows * row_count)
    core, over, up, along = feat_index % 2, feat_index // 2, row_index % 2, row_index // 2 % 4
    place = jnp.stack([core * 16 + over * 8 + up * 4 + along, core * 16 + up * 8 + over * 4 + along, core * 16 + over * 8])
    place = place.astype(jnp.int32)
    row = lambda a: a.reshape(1, -1)

    columns = raw_rows.T
    origin = rounded(jnp.mean(columns, 1, keepdims=True))
    moved = columns - origin
    sums = [origin[:, 0]]
    for value, scales in ((jnp.mean(moved, 1), (1.0, 1024.0, 1048576.0)), (jnp.mean(moved * moved, 1), (0.0625, 64.0, 65536.0))):
        for scale in scales:
            top = lax.reduce_precision(value * scale, 5, 10)
            sums.append(top)
            value = value - top / scale
    moved = moved * SPAN
    notes = jnp.pad(jnp.stack(sums), ((0, 1), (0, 32 - col_width))).reshape(1, 1, 2 * LANES)
    notes = jnp.broadcast_to(jnp.pad(notes, ((0, 0), (0, 0), (0, own_rows - 2 * LANES))), (feat_count, 1, own_rows))
    moved = moved.reshape(col_width, feat_count, own_rows).transpose(1, 0, 2)
    sent = jnp.concatenate([moved, notes], 1).astype(jnp.float16)
    owned = exchange(sent, "feat").reshape(1, feat_span, own_rows)
    near = jnp.concatenate([owned] + [swap(owned, "rows", bits) for bits in (2, 4, 6)], 0)
    for bit in range(3, row_count.bit_length() - 1):
        near = jnp.concatenate([near, swap(near, "rows", 1 << bit)], 0)
    far = swap(near, "rows", 1)
    source = members // local_rows
    source = source ^ row_index
    source = ((source >> 1) & 3) + 4 * (source >> 3) + (source & 1) * (row_count // 2)
    ids = (source * own_rows + members % own_rows).reshape(-1)

    spaced = jnp.pad(enc_weight.reshape(feat_count, col_width, model), ((0, 0), (0, 1), (0, 0))).reshape(feat_span, model)
    w_feat = jnp.pad(spaced, ((0, LANES - feat_span), (0, 0)))
    w_mark = jnp.pad(label_table, ((feat_span, LANES - feat_span - classes), (0, 0)))
    b_enc = row(enc_bias)
    w_embed = jnp.concatenate([w_feat, w_mark], 1)
    terms, left = [], enc_bias
    for _ in range(3):
        terms.append(rounded(left))
        left = left - terms[-1]
    ones = feat_span + classes
    w_all = (w_feat + w_mark).at[ones:ones + 3].set(jnp.stack(terms).astype(bf16))
    marks = jnp.pad(labels, ((0, 0), (0, pad - ctx_len)), constant_values=-1)
    cut = lambda w: w.reshape(model, HEADS, 1, width)
    w_qkv = jnp.concatenate([cut(w_query), cut(w_key), cut(w_value)], 2).reshape(model, 3 * model)
    edge = lambda b: b.reshape(1, HEADS, 1, width)
    b_qkv = jnp.concatenate([edge(b_query), edge(jnp.zeros_like(b_query)), edge(b_value)], 2).reshape(1, 3 * model)
    w_heads = w_qkv.T.reshape(HEADS, 3 * width, model)
    w_feat_t = w_feat.T
    w_rows = jnp.einsum("hkd,df->hkf", w_heads, w_feat_t, preferred_element_type=f32)
    high = rounded(w_rows)
    w_rows = jnp.concatenate([high, w_rows - high], 2).astype(bf16)
    tiles = model // LANES
    flat = cotangent.transpose(1, 0, 2).reshape(span, blocks, tiles, LANES).transpose(0, 2, 1, 3).reshape(-1, LANES)

    feats, stats = fetch(ids, near.astype(f32), far.astype(f32), marks, feat_count, classes)
    stats = lax.dynamic_slice_in_dim(stats, feat_index * (col_width + 1), col_width, 1)
    col_mean, factor = stats[0], stats[1]
    w_out_t = jnp.concatenate([w_out.T, w_feat_t], 1)
    weights = (w_embed, b_enc, w_qkv, b_qkv, w_out, row(b_out), row(gain_one), row(shift_one), w_in, row(b_in),
               w_back, row(b_back), row(gain_two), row(shift_two), w_out_t)
    qkv, expo, layer_out, d_rows, back, shift, keep, give, first = forward(place, queries, feats, flat, weights, ctx_len)
    layer_out = layer_out.reshape(span, tiles, blocks, LANES).transpose(0, 2, 1, 3).reshape(span, blocks, model).transpose(1, 0, 2)

    steps = reduce_chunks(keep, give, 48)
    early = []
    for start, count in CALLS:
        held, back = lax.optimization_barrier((next(steps), back))
        *made, d_rows = score_grads(place, start, count, expo, qkv, back, shift, feats, w_rows, d_rows, early, first)
        early.append(made[0])
    held, d_rows = lax.optimization_barrier((next(steps), d_rows))
    near, far = spread(ids, d_rows, row_count, feat_count, col_width, own_rows)
    own, (keep, give) = next(steps), tail_first(*made)
    give, near, far = lax.optimization_barrier((give, near, far))
    total = added(keep, swap(give, "feat", 2)).astype(bf16)
    d_table = added(near, swap(far, "rows", 1))
    total = added(total, swap(total, "rows", 1)).astype(bf16)
    total, d_table = lax.optimization_barrier((total, d_table))
    for bit in range(row_count.bit_length() - 2, 2, -1):
        half = d_table.shape[0] // 2
        d_table = added(d_table[:half], swap(d_table[half:].astype(bf16), "rows", 1 << bit))
        total = added(total, swap(total, "rows", 1 << bit)).astype(bf16)
    d_low = d_table.astype(bf16)
    d_own = added(d_table[0], *[swap(d_low[at], "rows", 2 * at) for at in range(1, 4)]).astype(bf16)
    for bit in (2, 4):
        total = added(total, swap(total, "rows", bit)).astype(bf16)
    t_near = jnp.concatenate([total, swap(total, "feat", 2)], 0)
    t_far = swap(t_near, "feat", 1)
    d_columns = exchange(d_own, "feat").astype(f32)
    d_columns = d_columns.transpose(1, 0, 2).reshape(col_width, local_rows)
    (g_query, g_key, g_value, g_enc, g_enc_bias, g_table, g_b_query, g_b_value, g_b_in, g_b_out, g_gain_one, g_shift_one,
     g_b_back, g_gain_two, g_shift_two) = finish_tail(place, t_near, t_far, w_heads, w_all, feat_total, col_width, classes)
    ends = gather_chunks(own, 48)
    g_out, g_in, g_back = finish(place, *ends)

    at = feat_index * col_width
    weight = lax.dynamic_slice_in_dim(enc_weight, at, col_width, 0).astype(f32)
    stat_one = jnp.sum(weight * g_enc_bias, 1)
    stat_two = jnp.sum(weight * lax.dynamic_slice_in_dim(g_enc, at, col_width, 0), 1)
    d_spread = -0.5 * stat_two * factor * factor
    d_mean = -factor * stat_one - 2.0 * d_spread * col_mean
    raw_grad = factor[:, None] * d_columns + (d_mean[:, None] + 2.0 * d_spread[:, None] * columns) / row_total
    flatten = lambda a: a.reshape(-1)
    return (
        layer_out, raw_grad.T, g_enc, flatten(g_enc_bias), g_table, g_query, flatten(g_b_query), g_key, g_value,
        flatten(g_b_value), g_out, flatten(g_b_out), flatten(g_gain_one), flatten(g_shift_one), g_in, flatten(g_b_in), g_back,
        flatten(g_b_back), flatten(g_gain_two), flatten(g_shift_two),
    )


def solution(mesh):
    both = ("rows", "feat")
    placed = (P("rows", "feat"),) + (P(),) * 18 + (P(both, None), P(both, None), P(both), P(both, None, None))
    results = (P(both, None, None), P("rows", "feat")) + (P(),) * 18
    return jax.shard_map(body, mesh=mesh, in_specs=placed, out_specs=results, check_vma=False)
```

```python
import functools
import math

import jax
import jax.numpy as jnp
from jax import lax
from jax.experimental import pallas as pl
from jax.experimental.pallas import tpu as pltpu
from jax.sharding import PartitionSpec as P

HEADS = 4
LANES = 128
epsilon = 1e-05
CHUNKS = 32
SMALLS = 120
SPAN = 64.0
VMEM_LIMIT = 54 * 1024 * 1024
f32 = jnp.float32
bf16 = jnp.bfloat16


def dot(left, right):
    return jnp.dot(left, right, preferred_element_type=f32)


def dot_nt(left, right):
    return lax.dot_general(left, right, (((1,), (1,)), ((), ())), preferred_element_type=f32)


def dot_tn(left, right):
    return lax.dot_general(left, right, (((0,), (0,)), ((), ())), preferred_element_type=f32)


def round_up(value, unit):
    return -(-value // unit) * unit


def row_chunks(span):
    for parts in (3, 2, 1):
        if span % (16 * parts) == 0:
            return parts
    return 1


def cost(gigaflops, megabytes):
    return pl.CostEstimate(flops=int(gigaflops * 1e9), bytes_accessed=int(megabytes * 1e6), transcendentals=0)


def params(*names, room=VMEM_LIMIT):
    room = min(room, VMEM_LIMIT)
    return pltpu.CompilerParams(vmem_limit_bytes=room, dimension_semantics=("arbitrary",) * len(names))


def fetch_kernel(span, feats, classes, ids, near, far, labels, feats_o, stats_o, table, rows_f, notes, origins):
    count, deep, own = near.shape
    each = deep // feats
    blocks, pad, _ = feats_o.shape
    unit = next(u for u in (50, 20, 10, 5, 2, 1) if span % u == 0)
    total = 2 * count
    lane = lax.broadcasted_iota(jnp.int32, (total, LANES), 1)
    mean_row, factor_row, origin_rows = 0.0, 0.0, 0.0
    for f in range(feats):
        for half, ref in enumerate((near, far)):
            def collect(g, _):
                notes[pl.ds(half * count + g, 1), :] = ref[g, (f + 1) * each - 1:(f + 1) * each, :2 * LANES]
                return 0

            lax.fori_loop(0, count, collect, 0)
        start, other = notes[:, :LANES], notes[:, LANES:]
        back = lambda v, by: pltpu.roll(v, LANES - by, 1)
        place = lambda v: pltpu.roll(jnp.where(lane < each - 1, v, 0.0), f * each, 1) if f else jnp.where(lane < each - 1, v, 0.0)
        first = back(start, 32) + back(start, 64) * (1.0 / 1024.0) + back(start, 96) * (1.0 / 1048576.0)
        square = other * 16.0 + back(other, 32) * (1.0 / 64.0) + back(other, 64) * (1.0 / 65536.0)
        middle_of = jnp.sum(start + first, 0, keepdims=True) * (1.0 / total)
        apart = start - middle_of
        spread_of = jnp.sum(square + apart * (2.0 * first + apart), 0, keepdims=True) * (1.0 / total)
        spread_of = jnp.where(lane[:1] < each - 1, spread_of, 1.0)
        full = lambda v: jnp.broadcast_to(v, (total, LANES))
        mean_row = mean_row + place(full(middle_of))
        factor_row = factor_row + place(full(lax.rsqrt(spread_of + epsilon)))
        origin_rows = origin_rows + place(start)
    origins[...] = origin_rows
    stats_o[0:1, :] = mean_row[0:1]
    stats_o[1:2, :] = factor_row[0:1]

    for half, ref in enumerate((near, far)):
        def unfold(g, _):
            piece = jnp.concatenate([ref[g], jnp.zeros((LANES - deep, own), f32)], 0).T
            at = half * count + g
            table[pl.ds(pl.multiple_of(at * own, own), own), :] = piece * (1.0 / SPAN) + origins[pl.ds(at, 1), :]
            return 0

        lax.fori_loop(0, count, unfold, 0)
    rows_f[pad - 16:, :] = jnp.zeros((16, LANES), f32)
    kind = lax.broadcasted_iota(jnp.int32, (16, pad), 0)
    pick = (lax.broadcasted_iota(jnp.int32, (16, LANES), 0) + deep == lax.broadcasted_iota(jnp.int32, (16, LANES), 1))
    pick = pick.astype(f32).astype(bf16)
    lane = lax.broadcasted_iota(jnp.int32, (pad, LANES), 1)
    for block in range(blocks):
        def fetch(i, _):
            for u in range(unit):
                at = i * unit + u
                rows_f[pl.ds(at, 1), :] = table[pl.ds(ids[block * span + at], 1), :]
            return 0

        lax.fori_loop(0, span // unit, fetch, 0)
        hot = ((kind == labels[block:block + 1, :]) | (kind == classes)).astype(f32).astype(bf16)
        scaled = (rows_f[...] - mean_row[0:1]) * factor_row[0:1]
        feats_o[block] = jnp.where(lane < deep, scaled, dot_tn(hot, pick)).astype(bf16)


def fetch(ids, near, far, labels, feats, classes):
    blocks, pad = labels.shape
    whole = lambda *s: pl.BlockSpec(s, lambda *_: (0,) * len(s), pipeline_mode=pl.Buffered(1))
    full = lambda *s: pl.BlockSpec(s, lambda *_: (0,) * len(s))
    total = 2 * near.shape[0]
    return pl.pallas_call(
        functools.partial(fetch_kernel, ids.shape[0] // blocks, feats, classes),
        grid_spec=pltpu.PrefetchScalarGridSpec(
            num_scalar_prefetch=1,
            grid=(1,),
            in_specs=[whole(*near.shape), whole(*far.shape), whole(*labels.shape)],
            out_specs=[full(blocks, pad, LANES), full(8, LANES)],
            scratch_shapes=[pltpu.VMEM((total * near.shape[2], LANES), f32), pltpu.VMEM((pad, LANES), f32),
                            pltpu.VMEM((total, 2 * LANES), f32), pltpu.VMEM((total, LANES), f32)],
        ),
        out_shape=[jax.ShapeDtypeStruct((blocks, pad, LANES), bf16), jax.ShapeDtypeStruct((8, LANES), f32)],
        compiler_params=params(0, room=(12 << 20) + 16 * total * near.shape[2] * LANES),
        cost_estimate=cost(6, 1),
        name="fetch",
    )(ids, near, far, labels)


def embed(feats, w_embed, b_enc):
    both = dot(feats, w_embed[...])
    model = both.shape[1] // 2
    slots = (both[:, :model] + b_enc[...]).astype(bf16)
    return slots.astype(f32) + both[:, model:]


def norm_parts(values):
    centre = jnp.mean(values, -1, keepdims=True)
    offset = values - centre
    second = jnp.mean(offset * offset, -1, keepdims=True)
    root = lax.rsqrt(second + epsilon)
    return offset * root, root


def norm_back(grad, unit, root):
    return root * (grad - jnp.mean(grad, -1, keepdims=True) - unit * jnp.mean(grad * unit, -1, keepdims=True))


def forward_kernel(blocks, ctx_len, ctx_pad, parts,
                   place, queries, feats, cot, w_embed, b_enc, w_qkv, b_qkv, w_out, b_out, gain_one, shift_one,
                   w_in, b_in, w_back, b_back, gain_two, shift_two, w_out_t,
                   qkv_o, e_o, out_o, rows_o, back_o, keep_o, give_o, aug_o,
                   mixed, inv, out_f, act_s, norm_s, d_hid_s, d_bra_s, d_att_s, g_out, g_in, g_back, wide, narrow):
    tick = pl.program_id(0)
    pad = qkv_o.shape[2]
    model = back_o.shape[2]
    step = pad // parts
    width = model // HEADS

    @pl.when(tick < blocks * HEADS)
    def _():
        block = tick // HEADS
        head = tick % HEADS

        @pl.when(head == 0)
        def _():
            def project(c):
                rows = slice(c * step, (c + 1) * step)
                low = embed(feats[block, rows, :], w_embed, b_enc).astype(bf16)
                made = (dot(low, w_qkv[...]) + b_qkv[...]).astype(bf16)
                for h in range(HEADS):
                    qkv_o[0, h, rows, :] = made[:, h * 3 * width:(h + 1) * 3 * width]

            for c in range(parts):
                project(c)

        factor = math.log2(math.e) / math.sqrt(width)
        keys = qkv_o[0, head, :ctx_pad, width:2 * width]
        vals = jnp.concatenate([qkv_o[0, head, :ctx_pad, 2 * width:], jnp.ones((ctx_pad, width), bf16)], 1)
        edge = ctx_len // LANES * LANES
        cols = pl.ds(pl.multiple_of(head * width, LANES), width)
        spans = [slice(c * step, (c + 1) * step) for c in range(parts)]

        def score(c):
            return dot_nt(qkv_o[0, head, spans[c], :width], keys)

        def weigh(c, scores):
            front = scores[:, :edge]
            most = jnp.max(front, 1, keepdims=True)
            if edge < ctx_pad:
                lane = lax.broadcasted_iota(jnp.int32, (step, ctx_pad - edge), 1)
                rear = jnp.where(lane < ctx_len - edge, scores[:, edge:], -1e30)
                most = jnp.maximum(most, jnp.max(rear, 1, keepdims=True))
                e_o[0, 0, spans[c], edge:] = jnp.exp2((rear - most) * factor).astype(bf16)
            e_o[0, 0, spans[c], :edge] = jnp.exp2((front - most) * factor).astype(bf16)

        ready = score(0)
        for c in range(parts):
            coming = score(c + 1) if c + 1 < parts else None
            weigh(c, ready)
            ready = coming
        summed = dot(e_o[0, 0], vals)
        inverse = 1.0 / summed[:, width:]
        lane = lax.broadcasted_iota(jnp.int32, (pad, LANES), 1)
        inv[block] = jnp.where(lane == head, inverse[:, :LANES], inv[block])
        mixed[block, :, cols] = (summed[:, :width] * inverse).astype(bf16)

    @pl.when(tick >= blocks * HEADS)
    def _():
        part = tick - blocks * HEADS

        @pl.when(part == 0)
        def _():
            for ref in (g_out, g_in, g_back, wide, narrow):
                ref[...] = jnp.zeros_like(ref)

        tiles = model // LANES
        rows = pl.ds(pl.multiple_of(part * step, 16), step)
        total = lambda v: jnp.sum(v, 0, keepdims=True)
        wide_t, narrow_t = [], [[] for _ in range(6)]

        def flow(block):
            here = slice(block * step, (block + 1) * step)
            mixed_low = mixed[block, rows, :]
            reached = embed(feats[block, rows, :], w_embed, b_enc) + dot(mixed_low, w_out[...])
            yield
            unit_one, root_one = norm_parts(reached + b_out[...])
            normed = unit_one * gain_one[...] + shift_one[...]
            norm_s[here, :] = normed.astype(bf16)
            yield
            hidden = dot(norm_s[here, :], w_in[...])
            yield
            hidden = hidden + b_in[...]
            slant = math.sqrt(2.0 / math.pi)
            square = hidden * hidden
            half = 0.5 * jnp.tanh(hidden * (slant + (slant * 0.044715) * square)) + 0.5
            active = hidden * half
            act_s[here, :] = active.astype(bf16)
            slope = half + active * (1.0 - half) * (2.0 * slant + (6.0 * slant * 0.044715) * square)
            yield
            branch = dot(act_s[here, :], w_back[...])
            yield
            unit_two, root_two = norm_parts(normed + (branch + b_back[...]))
            row = part * step + lax.broadcasted_iota(jnp.int32, (step, 1), 0)
            alive = row < ctx_len + queries[block]
            result = jnp.where(alive, unit_two * gain_two[...] + shift_two[...], 0.0)
            given = []
            for j in range(tiles):
                lanes = pl.ds(j * blocks + block, step, stride=tiles * blocks)
                out_f[lanes, :] = result[:, j * LANES:(j + 1) * LANES]
                given.append(cot[lanes, :])
            grad = jnp.where(alive, jnp.concatenate(given, 1), 0.0)
            second = norm_back(grad * gain_two[...], unit_two, root_two)
            d_bra_s[here, :] = second.astype(bf16)
            narrow_t[3].append(total(d_bra_s[here, :].astype(f32)))
            narrow_t[4].append(total(grad * unit_two))
            narrow_t[5].append(total(grad))
            yield
            d_act = dot_nt(d_bra_s[here, :], w_back[...])
            yield
            d_hid = (slope * d_act).astype(bf16)
            d_hid_s[here, :] = d_hid
            wide_t.append(total(d_hid.astype(f32)))
            yield
            d_norm = dot_nt(d_hid_s[here, :], w_in[...])
            yield
            grad_one = second + d_norm
            narrow_t[1].append(total(grad_one * unit_one))
            narrow_t[2].append(total(grad_one))
            first = norm_back(grad_one * gain_one[...], unit_one, root_one)
            d_att_s[here, :] = first.astype(bf16)
            narrow_t[0].append(total(d_att_s[here, :].astype(f32)))
            yield
            both = dot(d_att_s[here, :], w_out_t[...])
            yield
            row_part = both[:, model:]
            back = both[:, :model].astype(bf16).astype(f32)
            lane = lax.broadcasted_iota(jnp.int32, (step, LANES), 1)
            shifts = jnp.zeros((step, LANES), f32)
            for h in range(HEADS):
                cols = slice(h * width, (h + 1) * width)
                scaled = (back[:, cols] * inv[block, rows, h:h + 1]).astype(bf16)
                back_o[block, :, cols] = scaled
                moved = jnp.sum(scaled.astype(f32) * mixed_low[:, cols].astype(f32), 1, keepdims=True)
                shifts = jnp.where(lane == SMALLS + h, -moved, shifts)
            rows_o[block] = row_part + shifts
            yield

        flows = [flow(block) for block in range(blocks)]
        for item in flows:
            next(item)
        for turn in range(6):
            for item in flows:
                next(item)
                next(item, None)
            if turn == 2:
                g_back[...] += dot_tn(act_s[...], d_bra_s[...])
            if turn == 3:
                g_in[...] += dot_tn(norm_s[...], d_hid_s[...])
            if turn == 4:
                both = jnp.concatenate([jnp.concatenate([mixed[block, rows, :], feats[block, rows, :]], 1) for block in range(blocks)], 0)
                g_out[...] += dot_tn(both, d_att_s[...])
        out_o[...] = out_f[...].astype(bf16)
        wide[0:1, :] += sum(wide_t[1:], wide_t[0])
        for at in range(6):
            narrow[at:at + 1, :] += sum(narrow_t[at][1:], narrow_t[at][0])

        @pl.when(part == parts - 1)
        def _():
            def lay(start, ref, p, _):
                at = pl.multiple_of((p ^ place[0]) * 16, 16)
                other = pl.multiple_of((p ^ place[1]) * 32, 32)
                ref[p - start, 0:16, :] = g_out[pl.ds(at, 16), :].astype(bf16)
                for j in range(2):
                    ref[p - start, 16 + 16 * j:32 + 16 * j, :] = g_in[pl.ds(at, 16), j * model:(j + 1) * model].astype(bf16)
                ref[p - start, 48:80, :] = g_back[pl.ds(other, 32), :].astype(bf16)
                return 0

            for start, ref in ((0, keep_o), (CHUNKS // 2, give_o)):
                lax.fori_loop(start, start + CHUNKS // 2, functools.partial(lay, start, ref), 0)
            aug_o[...] = g_out[model:, :]
            aug_o[SMALLS:SMALLS + 6, :] = narrow[0:6, :]
            for j in range(2):
                aug_o[SMALLS + 6 + j:SMALLS + 7 + j, :] = wide[0:1, j * model:(j + 1) * model]


def forward(place, queries, feats, cot, weights, ctx_len):
    blocks, pad, _ = feats.shape
    model = weights[2].shape[0]
    inner = weights[8].shape[1]
    width = model // HEADS
    ctx_pad = round_up(ctx_len, LANES)
    parts = row_chunks(pad)
    step = pad // parts
    early = blocks * HEADS
    flat = blocks * model // LANES
    attending = lambda t: jnp.minimum(t, early - 1)
    later = lambda t: jnp.maximum(t - early, 0)
    once = lambda a: pl.BlockSpec(a.shape, lambda *_: (0,) * a.ndim, pipeline_mode=pl.Buffered(1))
    full = lambda *s: pl.BlockSpec(s, lambda *_: (0,) * len(s))
    rowed = lambda w: pl.BlockSpec((blocks, step, w), lambda t, *_: (0, later(t), 0))
    shape = jax.ShapeDtypeStruct
    return pl.pallas_call(
        functools.partial(forward_kernel, blocks, ctx_len, ctx_pad, parts),
        grid_spec=pltpu.PrefetchScalarGridSpec(
            num_scalar_prefetch=2,
            grid=(early + parts,),
            in_specs=[once(feats), pl.BlockSpec((step * flat, LANES), lambda t, *_: (later(t), 0))] + [once(a) for a in weights],
            out_specs=[
                pl.BlockSpec((1, HEADS, pad, 3 * width), lambda t, *_: (attending(t) // HEADS, 0, 0, 0)),
                pl.BlockSpec((1, 1, pad, ctx_pad), lambda t, *_: (attending(t) // HEADS, attending(t) % HEADS, 0, 0)),
                pl.BlockSpec((step * flat, LANES), lambda t, *_: (later(t), 0)),
                rowed(LANES), rowed(model),
                full(CHUNKS // 2, 80, model), full(CHUNKS // 2, 80, model), full(LANES, model)],
            scratch_shapes=[
                pltpu.VMEM((blocks, pad, model), bf16), pltpu.VMEM((blocks, pad, LANES), f32), pltpu.VMEM((step * flat, LANES), f32),
                pltpu.VMEM((blocks * step, inner), bf16), pltpu.VMEM((blocks * step, model), bf16),
                pltpu.VMEM((blocks * step, inner), bf16), pltpu.VMEM((blocks * step, model), bf16),
                pltpu.VMEM((blocks * step, model), bf16), pltpu.VMEM((model + LANES, model), f32), pltpu.VMEM((model, inner), f32),
                pltpu.VMEM((inner, model), f32), pltpu.VMEM((8, inner), f32), pltpu.VMEM((8, model), f32)],
        ),
        out_shape=[
            shape((blocks, HEADS, pad, 3 * width), bf16),
            shape((blocks, HEADS, pad, ctx_pad), bf16), shape(cot.shape, bf16), shape((blocks, pad, LANES), f32),
            shape((blocks, pad, model), bf16), shape((CHUNKS // 2, 80, model), bf16),
            shape((CHUNKS // 2, 80, model), bf16), shape((LANES, model), f32)],
        compiler_params=params(0),
        cost_estimate=cost(60, 1),
        name="forward",
    )(place, queries, feats, cot, *weights)


def scores_kernel(start, last, ctx_pad, parts, place, e, qkv, back, feats, w_rows, d_rows, *refs):
    block = pl.program_id(0)
    at = pl.program_id(1)
    count = pl.num_programs(1)
    base = start if last else 0
    if last:
        early, (first, keep_o, give_o, rows_o, ds, dox, d_all, fit) = refs[:-8], refs[-8:]
    else:
        early_o, rows_o, ds, dox, d_all, fit = refs
    pad = back.shape[1]
    step = pad // parts
    width = back.shape[2]
    root = 1.0 / math.sqrt(width)
    keys = qkv[0, 0, :ctx_pad, width:2 * width]
    vals = jnp.concatenate([qkv[0, 0, :ctx_pad, 2 * width:], jnp.ones((ctx_pad, width), bf16)], 1)
    lane = lax.broadcasted_iota(jnp.int32, (pad, width), 1)
    moved = jnp.sum(jnp.where(lane == SMALLS + start + at, d_rows[0], 0.0), 1, keepdims=True)
    top = moved.astype(bf16).astype(f32)
    dox[:, :width] = back[0]
    dox[:, width:] = jnp.where(lane == 0, top, jnp.where(lane == 1, moved - top, 0.0)).astype(bf16)
    spans = [slice(c * step, (c + 1) * step) for c in range(parts)]

    def score(c):
        return dot_nt(dox[spans[c], :], vals)

    ready = score(0)
    for c in range(parts):
        coming = score(c + 1) if c + 1 < parts else None
        ds[spans[c], :] = e[0, 0, spans[c], :] * ready.astype(bf16)
        d_all[spans[c], :width] = (dot(ds[spans[c], :], keys) * root).astype(bf16)
        ready = coming
    d_all[:ctx_pad, 2 * width:] = dot_tn(back[0], e[0, 0]).T.astype(bf16)
    d_all[:ctx_pad, width:2 * width] = (dot_tn(qkv[0, 0, :, :width], ds[...]) * root).T.astype(bf16)
    d_all[ctx_pad:, width:] = jnp.zeros((pad - ctx_pad, 2 * width), bf16)
    fitted = dot_tn(feats[0], d_all[...])
    pair = dot(d_all[...], w_rows[0])
    made = pair[:, :LANES] + pair[:, LANES:]

    @pl.when(at == 0)
    def _():
        rows_o[0] = d_rows[0] + made

    @pl.when(at > 0)
    def _():
        rows_o[0] += made

    @pl.when(block == 0)
    def _():
        fit[base + at] = fitted

    @pl.when(block > 0)
    def _():
        fit[base + at] += fitted

    @pl.when((block == pl.num_programs(0) - 1) & (at == count - 1))
    def _():
        if not last:
            early_o[...] = fit[...]
        else:
            filled = 0
            for ref in early:
                fit[filled:filled + ref.shape[0]] = ref[...]
                filled += ref.shape[0]
            for turn, ref in enumerate((keep_o, give_o)):
                def lay(p, _):
                    chunk = (turn * (CHUNKS // 2) + p) ^ place[2]
                    rows = pl.ds(pl.multiple_of(chunk // HEADS * 16, 16), 16)
                    head = chunk % HEADS
                    ref[p, :, :3 * width] = fit[head, rows, :].astype(bf16)
                    ref[p, :, 3 * width:] = first[rows, pl.ds(pl.multiple_of(head * width, LANES), width)].astype(bf16)
                    return 0

                lax.fori_loop(0, CHUNKS // 2, lay, 0)


def score_grads(place, start, count, e, qkv, back, feats, w_rows, d_rows, early, first):
    blocks, pad, model = back.shape
    ctx_pad = e.shape[3]
    width = model // HEADS
    parts = row_chunks(pad)
    full = lambda *s: pl.BlockSpec(s, lambda *_: (0,) * len(s))
    rowed = pl.BlockSpec((1, pad, LANES), lambda b, h, *_: (b, 0, 0))
    shape = jax.ShapeDtypeStruct
    last = start + count == HEADS
    late = (*early, first) if last else ()
    ends = [shape((CHUNKS // 2, 16, 4 * width), bf16)] * 2 if last else [shape((count, LANES, 3 * width), f32)]
    return pl.pallas_call(
        functools.partial(scores_kernel, start, last, ctx_pad, parts),
        grid_spec=pltpu.PrefetchScalarGridSpec(
            num_scalar_prefetch=1,
            grid=(blocks, count),
            in_specs=[pl.BlockSpec((1, 1, pad, ctx_pad), lambda b, h, *_: (b, start + h, 0, 0)),
                      pl.BlockSpec((1, 1, pad, 3 * width), lambda b, h, *_: (b, start + h, 0, 0)),
                      pl.BlockSpec((1, pad, width), lambda b, h, *_: (b, 0, start + h)),
                      rowed,
                      pl.BlockSpec((1, 3 * width, 2 * LANES), lambda b, h, *_: (start + h, 0, 0)),
                      rowed] + [full(*a.shape) for a in late],
            out_specs=[full(*end.shape) for end in ends] + [rowed],
            scratch_shapes=[pltpu.VMEM((pad, ctx_pad), bf16), pltpu.VMEM((pad, 2 * width), bf16), pltpu.VMEM((pad, 3 * width), bf16),
                            pltpu.VMEM((HEADS if last else count, LANES, 3 * width), f32)],
        ),
        out_shape=ends + [shape((blocks, pad, LANES), f32)],
        compiler_params=params(0, 0, room=36 << 20),
        cost_estimate=cost(8 * count, 1),
        name="score_grads",
    )(place, e, qkv, back, feats, w_rows, d_rows, *late)


def spread_kernel(span, own, ids, rows, near_o, far_o, *tables):
    blocks = rows.shape[0]
    count, feats, col_width, _ = near_o.shape
    for table in tables:
        table[...] = jnp.zeros_like(table)
    each = len(tables) // blocks if len(tables) > 1 else 1
    run = span // each
    unit = next(u for u in (10, 5, 2, 1) if run % u == 0)

    def add(i, _):
        for u in range(unit):
            for t in range(blocks * each):
                block, at = t // each, t % each * run + i * unit + u
                table = tables[t % len(tables)]
                spot = pl.ds(ids[block * span + at], 1)
                table[spot, :] += rows[block, pl.ds(at, 1), :]
        return 0

    lax.fori_loop(0, run // unit, add, 0)

    def fold(start, out_o, g, _):
        spot = pl.ds(pl.multiple_of((start + g) * own, own), own)
        total = tables[0][spot, :]
        for table in tables[1:]:
            total = total + table[spot, :]
        total = total.T
        for f in range(feats):
            at = f * (col_width + 1)
            out_o[g, f] = total[at:at + col_width].astype(bf16)
        return 0

    for start, out_o in ((0, near_o), (count, far_o)):
        lax.fori_loop(0, count, functools.partial(fold, start, out_o), 0)


def spread(ids, rows, count, feats, col_width, own):
    span = ids.shape[0] // rows.shape[0]
    tables = 4 if count <= 8 and span % 2 == 0 else 1
    return pl.pallas_call(
        functools.partial(spread_kernel, span, own),
        grid_spec=pltpu.PrefetchScalarGridSpec(
            num_scalar_prefetch=1,
            grid=(1,),
            in_specs=[pl.BlockSpec(rows.shape, lambda *_: (0, 0, 0))],
            out_specs=[pl.BlockSpec((count // 2, feats, col_width, own), lambda *_: (0, 0, 0, 0))] * 2,
            scratch_shapes=[pltpu.VMEM((count * own, LANES), f32)] * tables,
        ),
        out_shape=[jax.ShapeDtypeStruct((count // 2, feats, col_width, own), bf16)] * 2,
        compiler_params=params(0, room=(12 << 20) + 16 * count * own * LANES),
        cost_estimate=cost(7, 1),
        name="spread",
    )(ids, rows)


def chosen(p, near, far):
    half = CHUNKS // 2
    at = p % half
    return lambda *spot: jnp.where(p < half, near[(at, *spot)].astype(f32), far[(at, *spot)].astype(f32))


def finish_kernel(place, near, far, near_q, far_q, out_o, in_o, back_o):
    step = pl.program_id(0)
    model = out_o.shape[1]
    each = out_o.shape[0] // 16
    for u in range(each):
        take = chosen((step * each + u) ^ place[0], near, far)
        rows = slice(u * 16, (u + 1) * 16)
        out_o[rows, :] = take(slice(0, 16))
        for j in range(2):
            in_o[rows, j * model:(j + 1) * model] = take(slice(16 + 16 * j, 32 + 16 * j))
        take = chosen((step * each + u) ^ place[1], near_q, far_q)
        back_o[u * 32:(u + 1) * 32, :] = take(slice(None))


def finish(place, *ends):
    model = ends[0].shape[2]
    steps = 4
    shapes = [(model, model), (model, 2 * model), (2 * model, model)]
    return pl.pallas_call(
        finish_kernel,
        grid_spec=pltpu.PrefetchScalarGridSpec(
            num_scalar_prefetch=1,
            grid=(steps,),
            in_specs=[pl.BlockSpec(a.shape, lambda *_: (0, 0, 0)) for a in ends],
            out_specs=[pl.BlockSpec((s[0] // steps, s[1]), lambda i, *_: (i, 0)) for s in shapes],
        ),
        out_shape=[jax.ShapeDtypeStruct(s, f32) for s in shapes],
        compiler_params=params(0, room=16 << 20),
        cost_estimate=cost(5, 1),
        name="finish",
    )(place, *ends)


def finish_tail_kernel(col_width, classes, place, near, far, w_heads, w_all, q_o, k_o, v_o, enc_o, bias_o, mark_o, b_query_o, b_value_o,
                       wide_o, *refs):
    lines, (fit, aug) = refs[:-2], refs[-2:]
    model = q_o.shape[1]
    width = model // HEADS
    for c in range(CHUNKS):
        rows = slice(c // HEADS * 16, c // HEADS * 16 + 16)
        head = c % HEADS
        take = chosen(c ^ place[2], near, far)
        fit[head, rows, :] = take(slice(None), slice(0, 3 * width)).astype(bf16)
        aug[rows, head * width:(head + 1) * width] = take(slice(None), slice(3 * width, None))
    feats = enc_o.shape[0] // col_width
    ones = feats * (col_width + 1) + classes
    for row in range(6):
        lines[row][...] = aug[SMALLS + row:SMALLS + row + 1, :]
    for j in range(2):
        wide_o[:, j * model:(j + 1) * model] = aug[SMALLS + 6 + j:SMALLS + 7 + j, :]
    kind = lax.broadcasted_iota(jnp.int32, (LANES, 3 * width), 0)
    total = aug[...]
    for head in range(HEADS):
        cols = slice(head * width, (head + 1) * width)
        part = fit[head]
        total = total + dot(part, w_heads[head])
        line = part[ones:ones + 1, :].astype(f32)
        b_query_o[:, cols] = line[:, :width]
        b_value_o[:, cols] = line[:, 2 * width:]
        spread_line = jnp.where((kind > ones) & (kind < ones + 3), line, part.astype(f32)).astype(bf16)
        made = dot_tn(w_all[...], spread_line)
        for j, ref in enumerate((q_o, k_o, v_o)):
            ref[:, cols] = made[:, j * width:(j + 1) * width]
    aug[...] = total
    for f in range(feats):
        enc_o[f * col_width:(f + 1) * col_width, :] = aug[f * (col_width + 1):f * (col_width + 1) + col_width, :]
    mark_o[...] = aug[ones - classes:ones, :]
    bias_o[...] = aug[ones:ones + 1, :]


def finish_tail(place, near, far, w_heads, w_all, feat_total, col_width, classes):
    model = w_all.shape[1]
    width = model // HEADS
    shapes = [(model, model)] * 3 + [(feat_total, model), (1, model), (classes, model), (1, model), (1, model), (1, 2 * model)]
    shapes = shapes + [(1, model)] * 6
    full = lambda *s: pl.BlockSpec(s, lambda *_: (0,) * len(s))
    return pl.pallas_call(
        functools.partial(finish_tail_kernel, col_width, classes),
        grid_spec=pltpu.PrefetchScalarGridSpec(
            num_scalar_prefetch=1,
            grid=(1,),
            in_specs=[full(*a.shape) for a in (near, far, w_heads, w_all)],
            out_specs=[full(*s) for s in shapes],
            scratch_shapes=[pltpu.VMEM((HEADS, LANES, 3 * width), bf16), pltpu.VMEM((LANES, model), f32)],
        ),
        out_shape=[jax.ShapeDtypeStruct(s, f32) for s in shapes],
        compiler_params=params(0, room=20 << 20),
        cost_estimate=cost(5, 1),
        name="finish_tail",
    )(place, near, far, w_heads, w_all)


CALLS = ((0, 2), (2, 2))


def swap(value, axis, bit):
    size = lax.axis_size(axis)
    return lax.ppermute(value, axis, [(i, i ^ bit) for i in range(size)])


def rounded(value):
    return lax.reduce_precision(value, 8, 7)


def exchange(value, axis):
    return lax.all_to_all(value, axis, split_axis=0, concat_axis=0, tiled=True)


def added(*values):
    return sum((value.astype(f32) for value in values[1:]), values[0].astype(f32))


def reduce_chunks(keep, give, cut):
    over_core, over_x, over_y = ("feat", 1), ("feat", 2), ("rows", 1)
    came = swap(give, *over_core)
    half = keep.shape[0] // 2
    both = []
    for rows, first, then in ((slice(None, cut), over_x, over_y), (slice(cut, None), over_y, over_x)):
        mine, theirs = added(keep[:half, rows], came[:half, rows]), added(keep[half:, rows], came[half:, rows]).astype(bf16)
        both.append((mine, theirs, first, then))
    yield both[0][1]
    half = half // 2
    last = []
    for mine, theirs, first, then in both:
        came = swap(theirs, *first)
        last.append((added(mine[:half], came[:half]), added(mine[half:], came[half:]).astype(bf16), then))
    yield last[0][1]
    total = jnp.concatenate([added(mine, swap(theirs, *then)) for mine, theirs, then in last], 1).astype(bf16)
    yield total
    own = added(total[0], *[swap(total[at], "rows", 2 * at) for at in range(1, half)]).astype(bf16)
    for bit in range(3, lax.axis_size("rows").bit_length() - 1):
        own = added(own, swap(own, "rows", 1 << bit)).astype(bf16)
    yield own


def gather_chunks(own, cut):
    over_core, over_x, over_y = ("feat", 1), ("feat", 2), ("rows", 1)
    own = jnp.stack([own] + [swap(own, "rows", 2 * at) for at in range(1, 4)])
    parts = []
    for rows, first, then in ((slice(None, cut), over_x, over_y), (slice(cut, None), over_y, over_x)):
        part = own[:, rows]
        parts.append((jnp.concatenate([part, swap(part, *then)], 0), first))
    near = [jnp.concatenate([part, swap(part, *first)], 0) for part, first in parts]
    return near[0], swap(near[0], *over_core), near[1], swap(near[1], *over_core)


def tail_first(keep, give):
    half = keep.shape[0] // 2
    came = swap(give, "feat", 1)
    return added(keep[:half], came[:half]), added(keep[half:], came[half:]).astype(bf16)


def body(
    raw_rows, enc_weight, enc_bias, label_table, w_query, b_query, w_key, w_value, b_value, w_out, b_out,
    gain_one, shift_one, w_in, b_in, w_back, b_back, gain_two, shift_two, members, labels, queries, cotangent,
):
    row_count = lax.axis_size("rows")
    feat_count = lax.axis_size("feat")
    row_index = lax.axis_index("rows")
    feat_index = lax.axis_index("feat")
    local_rows, col_width = raw_rows.shape
    own_rows = local_rows // feat_count
    feat_total = col_width * feat_count
    feat_span = feat_total + feat_count
    model = enc_weight.shape[1]
    width = model // HEADS
    classes = label_table.shape[0]
    blocks, span = members.shape
    ctx_len = labels.shape[1]
    pad = round_up(span, 16)
    row_total = float(local_rows * row_count)
    core, over, up, along = feat_index % 2, feat_index // 2, row_index % 2, row_index // 2 % 4
    place = jnp.stack([core * 16 + over * 8 + up * 4 + along, core * 16 + up * 8 + over * 4 + along, core * 16 + over * 8])
    place = place.astype(jnp.int32)
    row = lambda a: a.reshape(1, -1)

    columns = raw_rows.T
    origin = rounded(jnp.mean(columns, 1, keepdims=True))
    moved = columns - origin
    sums = [origin[:, 0]]
    for value, scales in ((jnp.mean(moved, 1), (1.0, 1024.0, 1048576.0)), (jnp.mean(moved * moved, 1), (0.0625, 64.0, 65536.0))):
        for scale in scales:
            top = lax.reduce_precision(value * scale, 5, 10)
            sums.append(top)
            value = value - top / scale
    moved = moved * SPAN
    notes = jnp.pad(jnp.stack(sums), ((0, 1), (0, 32 - col_width))).reshape(1, 1, 2 * LANES)
    notes = jnp.broadcast_to(jnp.pad(notes, ((0, 0), (0, 0), (0, own_rows - 2 * LANES))), (feat_count, 1, own_rows))
    moved = moved.reshape(col_width, feat_count, own_rows).transpose(1, 0, 2)
    sent = jnp.concatenate([moved, notes], 1).astype(jnp.float16)
    owned = exchange(sent, "feat").reshape(1, feat_span, own_rows)
    near = jnp.concatenate([owned] + [swap(owned, "rows", bits) for bits in (2, 4, 6)], 0)
    for bit in range(3, row_count.bit_length() - 1):
        near = jnp.concatenate([near, swap(near, "rows", 1 << bit)], 0)
    far = swap(near, "rows", 1)
    source = members // local_rows
    source = source ^ row_index
    source = ((source >> 1) & 3) + 4 * (source >> 3) + (source & 1) * (row_count // 2)
    ids = (source * own_rows + members % own_rows).reshape(-1)

    spaced = jnp.pad(enc_weight.reshape(feat_count, col_width, model), ((0, 0), (0, 1), (0, 0))).reshape(feat_span, model)
    w_feat = jnp.pad(spaced, ((0, LANES - feat_span), (0, 0)))
    w_mark = jnp.pad(label_table, ((feat_span, LANES - feat_span - classes), (0, 0)))
    b_enc = row(enc_bias)
    w_embed = jnp.concatenate([w_feat, w_mark], 1)
    terms, left = [], enc_bias
    for _ in range(3):
        terms.append(rounded(left))
        left = left - terms[-1]
    ones = feat_span + classes
    w_all = (w_feat + w_mark).at[ones:ones + 3].set(jnp.stack(terms).astype(bf16))
    marks = jnp.pad(labels, ((0, 0), (0, pad - ctx_len)), constant_values=-1)
    cut = lambda w: w.reshape(model, HEADS, 1, width)
    w_qkv = jnp.concatenate([cut(w_query), cut(w_key), cut(w_value)], 2).reshape(model, 3 * model)
    edge = lambda b: b.reshape(1, HEADS, 1, width)
    b_qkv = jnp.concatenate([edge(b_query), edge(jnp.zeros_like(b_query)), edge(b_value)], 2).reshape(1, 3 * model)
    w_heads = w_qkv.T.reshape(HEADS, 3 * width, model)
    w_feat_t = w_feat.T
    w_rows = jnp.einsum("hkd,df->hkf", w_heads, w_feat_t, preferred_element_type=f32)
    high = rounded(w_rows)
    w_rows = jnp.concatenate([high, w_rows - high], 2).astype(bf16)
    tiles = model // LANES
    flat = cotangent.transpose(1, 0, 2).reshape(span, blocks, tiles, LANES).transpose(0, 2, 1, 3).reshape(-1, LANES)

    feats, stats = fetch(ids, near.astype(f32), far.astype(f32), marks, feat_count, classes)
    stats = lax.dynamic_slice_in_dim(stats, feat_index * (col_width + 1), col_width, 1)
    col_mean, factor = stats[0], stats[1]
    w_out_t = jnp.concatenate([w_out.T, w_feat_t], 1)
    weights = (w_embed, b_enc, w_qkv, b_qkv, w_out, row(b_out), row(gain_one), row(shift_one), w_in, row(b_in),
               w_back, row(b_back), row(gain_two), row(shift_two), w_out_t)
    qkv, expo, layer_out, d_rows, back, keep, give, first = forward(place, queries, feats, flat, weights, ctx_len)
    layer_out = layer_out.reshape(span, tiles, blocks, LANES).transpose(0, 2, 1, 3).reshape(span, blocks, model).transpose(1, 0, 2)

    steps = reduce_chunks(keep, give, 48)
    early = []
    for start, count in CALLS:
        held, back = lax.optimization_barrier((next(steps), back))
        *made, d_rows = score_grads(place, start, count, expo, qkv, back, feats, w_rows, d_rows, early, first)
        early.append(made[0])
    held, d_rows = lax.optimization_barrier((next(steps), d_rows))
    near, far = spread(ids, d_rows, row_count, feat_count, col_width, own_rows)
    own, (keep, give) = next(steps), tail_first(*made)
    give, near, far = lax.optimization_barrier((give, near, far))
    total = added(keep, swap(give, "feat", 2)).astype(bf16)
    d_table = added(near, swap(far, "rows", 1))
    total = added(total, swap(total, "rows", 1)).astype(bf16)
    total, d_table = lax.optimization_barrier((total, d_table))
    for bit in range(row_count.bit_length() - 2, 2, -1):
        half = d_table.shape[0] // 2
        d_table = added(d_table[:half], swap(d_table[half:].astype(bf16), "rows", 1 << bit))
        total = added(total, swap(total, "rows", 1 << bit)).astype(bf16)
    d_low = d_table.astype(bf16)
    d_own = added(d_table[0], *[swap(d_low[at], "rows", 2 * at) for at in range(1, 4)]).astype(bf16)
    for bit in (2, 4):
        total = added(total, swap(total, "rows", bit)).astype(bf16)
    t_near = jnp.concatenate([total, swap(total, "feat", 2)], 0)
    t_far = swap(t_near, "feat", 1)
    d_columns = exchange(d_own, "feat").astype(f32)
    d_columns = d_columns.transpose(1, 0, 2).reshape(col_width, local_rows)
    (g_query, g_key, g_value, g_enc, g_enc_bias, g_table, g_b_query, g_b_value, g_b_in, g_b_out, g_gain_one, g_shift_one,
     g_b_back, g_gain_two, g_shift_two) = finish_tail(place, t_near, t_far, w_heads, w_all, feat_total, col_width, classes)
    ends = gather_chunks(own, 48)
    g_out, g_in, g_back = finish(place, *ends)

    at = feat_index * col_width
    weight = lax.dynamic_slice_in_dim(enc_weight, at, col_width, 0).astype(f32)
    stat_one = jnp.sum(weight * g_enc_bias, 1)
    stat_two = jnp.sum(weight * lax.dynamic_slice_in_dim(g_enc, at, col_width, 0), 1)
    d_spread = -0.5 * stat_two * factor * factor
    d_mean = -factor * stat_one - 2.0 * d_spread * col_mean
    raw_grad = factor[:, None] * d_columns + (d_mean[:, None] + 2.0 * d_spread[:, None] * columns) / row_total
    flatten = lambda a: a.reshape(-1)
    return (
        layer_out, raw_grad.T, g_enc, flatten(g_enc_bias), g_table, g_query, flatten(g_b_query), g_key, g_value,
        flatten(g_b_value), g_out, flatten(g_b_out), flatten(g_gain_one), flatten(g_shift_one), g_in, flatten(g_b_in), g_back,
        flatten(g_b_back), flatten(g_gain_two), flatten(g_shift_two),
    )


def solution(mesh):
    both = ("rows", "feat")
    placed = (P("rows", "feat"),) + (P(),) * 18 + (P(both, None), P(both, None), P(both), P(both, None, None))
    results = (P(both, None, None), P("rows", "feat")) + (P(),) * 18
    return jax.shard_map(body, mesh=mesh, in_specs=placed, out_specs=results, check_vma=False)
```

```python
import functools
import math

import jax
import jax.numpy as jnp
from jax import lax
from jax.experimental import pallas as pl
from jax.experimental.pallas import tpu as pltpu
from jax.sharding import PartitionSpec as P

HEADS = 4
LANES = 128
epsilon = 1e-05
CHUNKS = 32
SMALLS = 120
SPAN = 64.0
VMEM_LIMIT = 54 * 1024 * 1024
f32 = jnp.float32
bf16 = jnp.bfloat16


def dot(left, right):
    return jnp.dot(left, right, preferred_element_type=f32)


def dot_nt(left, right):
    return lax.dot_general(left, right, (((1,), (1,)), ((), ())), preferred_element_type=f32)


def dot_tn(left, right):
    return lax.dot_general(left, right, (((0,), (0,)), ((), ())), preferred_element_type=f32)


def round_up(value, unit):
    return -(-value // unit) * unit


def row_chunks(span):
    for parts in (3, 2, 1):
        if span % (16 * parts) == 0:
            return parts
    return 1


def cost(gigaflops, megabytes):
    return pl.CostEstimate(flops=int(gigaflops * 1e9), bytes_accessed=int(megabytes * 1e6), transcendentals=0)


def params(*names, room=VMEM_LIMIT):
    room = min(room, VMEM_LIMIT)
    return pltpu.CompilerParams(vmem_limit_bytes=room, dimension_semantics=("arbitrary",) * len(names))


def fetch_kernel(span, feats, classes, ids, near, far, labels, feats_o, stats_o, table, rows_f, notes, origins):
    count, deep, own = near.shape
    each = deep // feats
    blocks, pad, _ = feats_o.shape
    unit = next(u for u in (50, 20, 10, 5, 2, 1) if span % u == 0)
    total = 2 * count
    lane = lax.broadcasted_iota(jnp.int32, (total, LANES), 1)
    mean_row, factor_row, origin_rows = 0.0, 0.0, 0.0
    for f in range(feats):
        for half, ref in enumerate((near, far)):
            def collect(g, _):
                notes[pl.ds(half * count + g, 1), :] = ref[g, (f + 1) * each - 1:(f + 1) * each, :2 * LANES]
                return 0

            lax.fori_loop(0, count, collect, 0)
        start, other = notes[:, :LANES], notes[:, LANES:]
        back = lambda v, by: pltpu.roll(v, LANES - by, 1)
        place = lambda v: pltpu.roll(jnp.where(lane < each - 1, v, 0.0), f * each, 1) if f else jnp.where(lane < each - 1, v, 0.0)
        first = back(start, 32) + back(start, 64) * (1.0 / 1024.0) + back(start, 96) * (1.0 / 1048576.0)
        square = other * 16.0 + back(other, 32) * (1.0 / 64.0) + back(other, 64) * (1.0 / 65536.0)
        middle_of = jnp.sum(start + first, 0, keepdims=True) * (1.0 / total)
        apart = start - middle_of
        spread_of = jnp.sum(square + apart * (2.0 * first + apart), 0, keepdims=True) * (1.0 / total)
        spread_of = jnp.where(lane[:1] < each - 1, spread_of, 1.0)
        full = lambda v: jnp.broadcast_to(v, (total, LANES))
        mean_row = mean_row + place(full(middle_of))
        factor_row = factor_row + place(full(lax.rsqrt(spread_of + epsilon)))
        origin_rows = origin_rows + place(start)
    origins[...] = origin_rows
    stats_o[0:1, :] = mean_row[0:1]
    stats_o[1:2, :] = factor_row[0:1]

    for half, ref in enumerate((near, far)):
        def unfold(g, _):
            piece = jnp.concatenate([ref[g], jnp.zeros((LANES - deep, own), f32)], 0).T
            at = half * count + g
            table[pl.ds(pl.multiple_of(at * own, own), own), :] = piece * (1.0 / SPAN) + origins[pl.ds(at, 1), :]
            return 0

        lax.fori_loop(0, count, unfold, 0)
    rows_f[pad - 16:, :] = jnp.zeros((16, LANES), f32)
    kind = lax.broadcasted_iota(jnp.int32, (16, pad), 0)
    pick = (lax.broadcasted_iota(jnp.int32, (16, LANES), 0) + deep == lax.broadcasted_iota(jnp.int32, (16, LANES), 1))
    pick = pick.astype(f32).astype(bf16)
    lane = lax.broadcasted_iota(jnp.int32, (pad, LANES), 1)
    for block in range(blocks):
        def fetch(i, _):
            for u in range(unit):
                at = i * unit + u
                rows_f[pl.ds(at, 1), :] = table[pl.ds(ids[block * span + at], 1), :]
            return 0

        lax.fori_loop(0, span // unit, fetch, 0)
        hot = ((kind == labels[block:block + 1, :]) | (kind == classes)).astype(f32).astype(bf16)
        scaled = (rows_f[...] - mean_row[0:1]) * factor_row[0:1]
        feats_o[block] = jnp.where(lane < deep, scaled, dot_tn(hot, pick)).astype(bf16)


def fetch(ids, near, far, labels, feats, classes):
    blocks, pad = labels.shape
    whole = lambda *s: pl.BlockSpec(s, lambda *_: (0,) * len(s), pipeline_mode=pl.Buffered(1))
    full = lambda *s: pl.BlockSpec(s, lambda *_: (0,) * len(s))
    total = 2 * near.shape[0]
    return pl.pallas_call(
        functools.partial(fetch_kernel, ids.shape[0] // blocks, feats, classes),
        grid_spec=pltpu.PrefetchScalarGridSpec(
            num_scalar_prefetch=1,
            grid=(1,),
            in_specs=[whole(*near.shape), whole(*far.shape), whole(*labels.shape)],
            out_specs=[full(blocks, pad, LANES), full(8, LANES)],
            scratch_shapes=[pltpu.VMEM((total * near.shape[2], LANES), f32), pltpu.VMEM((pad, LANES), f32),
                            pltpu.VMEM((total, 2 * LANES), f32), pltpu.VMEM((total, LANES), f32)],
        ),
        out_shape=[jax.ShapeDtypeStruct((blocks, pad, LANES), bf16), jax.ShapeDtypeStruct((8, LANES), f32)],
        compiler_params=params(0, room=(12 << 20) + 16 * total * near.shape[2] * LANES),
        cost_estimate=cost(6, 1),
        name="fetch",
    )(ids, near, far, labels)


def embed(feats, w_embed, b_enc):
    both = dot(feats, w_embed[...])
    model = both.shape[1] // 2
    slots = (both[:, :model] + b_enc[...]).astype(bf16)
    return slots.astype(f32) + both[:, model:]


def norm_parts(values):
    centre = jnp.mean(values, -1, keepdims=True)
    offset = values - centre
    second = jnp.mean(offset * offset, -1, keepdims=True)
    root = lax.rsqrt(second + epsilon)
    return offset * root, root


def norm_back(grad, unit, root):
    return root * (grad - jnp.mean(grad, -1, keepdims=True) - unit * jnp.mean(grad * unit, -1, keepdims=True))


def forward_kernel(blocks, ctx_len, ctx_pad, parts,
                   place, queries, feats, cot, w_embed, b_enc, w_qkv, b_qkv, w_out, b_out, gain_one, shift_one,
                   w_in, b_in, w_back, b_back, gain_two, shift_two, w_out_t,
                   qkv_o, e_o, out_o, rows_o, back_o, keep_o, give_o, aug_o,
                   mixed, inv, out_f, act_s, norm_s, d_hid_s, d_bra_s, d_att_s, g_out, g_in, g_back, wide, narrow):
    tick = pl.program_id(0)
    pad = qkv_o.shape[2]
    model = back_o.shape[2]
    step = pad // parts
    width = model // HEADS

    @pl.when(tick < blocks * HEADS)
    def _():
        block = tick // HEADS
        head = tick % HEADS

        @pl.when(head == 0)
        def _():
            def project(c):
                rows = slice(c * step, (c + 1) * step)
                low = embed(feats[block, rows, :], w_embed, b_enc).astype(bf16)
                made = (dot(low, w_qkv[...]) + b_qkv[...]).astype(bf16)
                for h in range(HEADS):
                    qkv_o[0, h, rows, :] = made[:, h * 3 * width:(h + 1) * 3 * width]

            for c in range(parts):
                project(c)

        factor = math.log2(math.e) / math.sqrt(width)
        keys = qkv_o[0, head, :ctx_pad, width:2 * width]
        vals = jnp.concatenate([qkv_o[0, head, :ctx_pad, 2 * width:], jnp.ones((ctx_pad, width), bf16)], 1)
        edge = ctx_len // LANES * LANES
        cols = pl.ds(pl.multiple_of(head * width, LANES), width)
        spans = [slice(c * step, (c + 1) * step) for c in range(parts)]

        def score(c):
            return dot_nt(qkv_o[0, head, spans[c], :width], keys)

        def weigh(c, scores):
            front = scores[:, :edge]
            most = jnp.max(front, 1, keepdims=True)
            if edge < ctx_pad:
                lane = lax.broadcasted_iota(jnp.int32, (step, ctx_pad - edge), 1)
                rear = jnp.where(lane < ctx_len - edge, scores[:, edge:], -1e30)
                most = jnp.maximum(most, jnp.max(rear, 1, keepdims=True))
                e_o[0, 0, spans[c], edge:] = jnp.exp2((rear - most) * factor).astype(bf16)
            e_o[0, 0, spans[c], :edge] = jnp.exp2((front - most) * factor).astype(bf16)

        ready = score(0)
        for c in range(parts):
            coming = score(c + 1) if c + 1 < parts else None
            weigh(c, ready)
            ready = coming
        summed = dot(e_o[0, 0], vals)
        inverse = 1.0 / summed[:, width:]
        lane = lax.broadcasted_iota(jnp.int32, (pad, LANES), 1)
        inv[block] = jnp.where(lane == head, inverse[:, :LANES], inv[block])
        mixed[block, :, cols] = (summed[:, :width] * inverse).astype(bf16)

    @pl.when(tick >= blocks * HEADS)
    def _():
        part = tick - blocks * HEADS

        @pl.when(part == 0)
        def _():
            for ref in (g_out, g_in, g_back, wide, narrow):
                ref[...] = jnp.zeros_like(ref)

        tiles = model // LANES
        rows = pl.ds(pl.multiple_of(part * step, 16), step)
        total = lambda v: jnp.sum(v, 0, keepdims=True)
        wide_t, narrow_t = [], [[] for _ in range(6)]

        def flow(block):
            here = slice(block * step, (block + 1) * step)
            mixed_low = mixed[block, rows, :]
            reached = embed(feats[block, rows, :], w_embed, b_enc) + dot(mixed_low, w_out[...])
            yield
            unit_one, root_one = norm_parts(reached + b_out[...])
            normed = unit_one * gain_one[...] + shift_one[...]
            norm_s[here, :] = normed.astype(bf16)
            yield
            hidden = dot(norm_s[here, :], w_in[...])
            yield
            hidden = hidden + b_in[...]
            slant = math.sqrt(2.0 / math.pi)
            square = hidden * hidden
            half = 0.5 * jnp.tanh(hidden * (slant + (slant * 0.044715) * square)) + 0.5
            active = hidden * half
            act_s[here, :] = active.astype(bf16)
            slope = half + active * (1.0 - half) * (2.0 * slant + (6.0 * slant * 0.044715) * square)
            yield
            branch = dot(act_s[here, :], w_back[...])
            yield
            unit_two, root_two = norm_parts(normed + (branch + b_back[...]))
            row = part * step + lax.broadcasted_iota(jnp.int32, (step, 1), 0)
            alive = row < ctx_len + queries[block]
            result = jnp.where(alive, unit_two * gain_two[...] + shift_two[...], 0.0)
            given = []
            for j in range(tiles):
                lanes = pl.ds(j * blocks + block, step, stride=tiles * blocks)
                out_f[lanes, :] = result[:, j * LANES:(j + 1) * LANES]
                given.append(cot[lanes, :])
            grad = jnp.where(alive, jnp.concatenate(given, 1), 0.0)
            second = norm_back(grad * gain_two[...], unit_two, root_two)
            d_bra_s[here, :] = second.astype(bf16)
            narrow_t[3].append(total(d_bra_s[here, :].astype(f32)))
            narrow_t[4].append(total(grad * unit_two))
            narrow_t[5].append(total(grad))
            yield
            d_act = dot_nt(d_bra_s[here, :], w_back[...])
            yield
            d_hid = (slope * d_act).astype(bf16)
            d_hid_s[here, :] = d_hid
            wide_t.append(total(d_hid.astype(f32)))
            yield
            d_norm = dot_nt(d_hid_s[here, :], w_in[...])
            yield
            grad_one = second + d_norm
            narrow_t[1].append(total(grad_one * unit_one))
            narrow_t[2].append(total(grad_one))
            first = norm_back(grad_one * gain_one[...], unit_one, root_one)
            d_att_s[here, :] = first.astype(bf16)
            narrow_t[0].append(total(d_att_s[here, :].astype(f32)))
            yield
            both = dot(d_att_s[here, :], w_out_t[...])
            yield
            row_part = both[:, model:]
            back = both[:, :model].astype(bf16).astype(f32)
            lane = lax.broadcasted_iota(jnp.int32, (step, LANES), 1)
            shifts = jnp.zeros((step, LANES), f32)
            for h in range(HEADS):
                cols = slice(h * width, (h + 1) * width)
                scaled = (back[:, cols] * inv[block, rows, h:h + 1]).astype(bf16)
                back_o[block, :, cols] = scaled
                moved = jnp.sum(scaled.astype(f32) * mixed_low[:, cols].astype(f32), 1, keepdims=True)
                shifts = jnp.where(lane == SMALLS + h, -moved, shifts)
            rows_o[block] = row_part + shifts
            yield

        flows = [flow(block) for block in range(blocks)]
        for item in flows:
            next(item)
        for turn in range(6):
            for item in flows:
                next(item)
                next(item, None)
            if turn == 2:
                g_back[...] += dot_tn(act_s[...], d_bra_s[...])
            if turn == 3:
                g_in[...] += dot_tn(norm_s[...], d_hid_s[...])
            if turn == 4:
                both = jnp.concatenate([jnp.concatenate([mixed[block, rows, :], feats[block, rows, :]], 1) for block in range(blocks)], 0)
                g_out[...] += dot_tn(both, d_att_s[...])
        out_o[...] = out_f[...].astype(bf16)
        wide[0:1, :] += sum(wide_t[1:], wide_t[0])
        for at in range(6):
            narrow[at:at + 1, :] += sum(narrow_t[at][1:], narrow_t[at][0])

        @pl.when(part == parts - 1)
        def _():
            def lay(start, ref, p, _):
                at = pl.multiple_of((p ^ place[0]) * 16, 16)
                other = pl.multiple_of((p ^ place[1]) * 32, 32)
                ref[p - start, 0:16, :] = g_out[pl.ds(at, 16), :].astype(bf16)
                for j in range(2):
                    ref[p - start, 16 + 16 * j:32 + 16 * j, :] = g_in[pl.ds(at, 16), j * model:(j + 1) * model].astype(bf16)
                ref[p - start, 48:80, :] = g_back[pl.ds(other, 32), :].astype(bf16)
                return 0

            for start, ref in ((0, keep_o), (CHUNKS // 2, give_o)):
                lax.fori_loop(start, start + CHUNKS // 2, functools.partial(lay, start, ref), 0)
            aug_o[...] = g_out[model:, :]
            aug_o[SMALLS:SMALLS + 6, :] = narrow[0:6, :]
            for j in range(2):
                aug_o[SMALLS + 6 + j:SMALLS + 7 + j, :] = wide[0:1, j * model:(j + 1) * model]


def forward(place, queries, feats, cot, weights, ctx_len):
    blocks, pad, _ = feats.shape
    model = weights[2].shape[0]
    inner = weights[8].shape[1]
    width = model // HEADS
    ctx_pad = round_up(ctx_len, LANES)
    parts = row_chunks(pad)
    step = pad // parts
    early = blocks * HEADS
    flat = blocks * model // LANES
    attending = lambda t: jnp.minimum(t, early - 1)
    later = lambda t: jnp.maximum(t - early, 0)
    once = lambda a: pl.BlockSpec(a.shape, lambda *_: (0,) * a.ndim, pipeline_mode=pl.Buffered(1))
    full = lambda *s: pl.BlockSpec(s, lambda *_: (0,) * len(s))
    rowed = lambda w: pl.BlockSpec((blocks, step, w), lambda t, *_: (0, later(t), 0))
    shape = jax.ShapeDtypeStruct
    return pl.pallas_call(
        functools.partial(forward_kernel, blocks, ctx_len, ctx_pad, parts),
        grid_spec=pltpu.PrefetchScalarGridSpec(
            num_scalar_prefetch=2,
            grid=(early + parts,),
            in_specs=[once(feats), pl.BlockSpec((step * flat, LANES), lambda t, *_: (later(t), 0))] + [once(a) for a in weights],
            out_specs=[
                pl.BlockSpec((1, HEADS, pad, 3 * width), lambda t, *_: (attending(t) // HEADS, 0, 0, 0)),
                pl.BlockSpec((1, 1, pad, ctx_pad), lambda t, *_: (attending(t) // HEADS, attending(t) % HEADS, 0, 0)),
                pl.BlockSpec((step * flat, LANES), lambda t, *_: (later(t), 0)),
                rowed(LANES), rowed(model),
                full(CHUNKS // 2, 80, model), full(CHUNKS // 2, 80, model), full(LANES, model)],
            scratch_shapes=[
                pltpu.VMEM((blocks, pad, model), bf16), pltpu.VMEM((blocks, pad, LANES), f32), pltpu.VMEM((step * flat, LANES), f32),
                pltpu.VMEM((blocks * step, inner), bf16), pltpu.VMEM((blocks * step, model), bf16),
                pltpu.VMEM((blocks * step, inner), bf16), pltpu.VMEM((blocks * step, model), bf16),
                pltpu.VMEM((blocks * step, model), bf16), pltpu.VMEM((model + LANES, model), f32), pltpu.VMEM((model, inner), f32),
                pltpu.VMEM((inner, model), f32), pltpu.VMEM((8, inner), f32), pltpu.VMEM((8, model), f32)],
        ),
        out_shape=[
            shape((blocks, HEADS, pad, 3 * width), bf16),
            shape((blocks, HEADS, pad, ctx_pad), bf16), shape(cot.shape, bf16), shape((blocks, pad, LANES), f32),
            shape((blocks, pad, model), bf16), shape((CHUNKS // 2, 80, model), bf16),
            shape((CHUNKS // 2, 80, model), bf16), shape((LANES, model), f32)],
        compiler_params=params(0),
        cost_estimate=cost(60, 1),
        name="forward",
    )(place, queries, feats, cot, *weights)


def scores_kernel(start, last, ctx_pad, parts, place, e, qkv, back, feats, w_rows, d_rows, *refs):
    block = pl.program_id(0)
    at = pl.program_id(1)
    count = pl.num_programs(1)
    base = start if last else 0
    if last:
        early, (first, keep_o, give_o, rows_o, ds, dox, d_all, fit) = refs[:-8], refs[-8:]
    else:
        early_o, rows_o, ds, dox, d_all, fit = refs
    pad = back.shape[1]
    step = pad // parts
    width = back.shape[2]
    root = 1.0 / math.sqrt(width)
    keys = qkv[0, 0, :ctx_pad, width:2 * width]
    vals = jnp.concatenate([qkv[0, 0, :ctx_pad, 2 * width:], jnp.ones((ctx_pad, width), bf16)], 1)
    lane = lax.broadcasted_iota(jnp.int32, (pad, width), 1)
    moved = jnp.sum(jnp.where(lane == SMALLS + start + at, d_rows[0], 0.0), 1, keepdims=True)
    top = moved.astype(bf16).astype(f32)
    dox[:, :width] = back[0]
    dox[:, width:] = jnp.where(lane == 0, top, jnp.where(lane == 1, moved - top, 0.0)).astype(bf16)
    spans = [slice(c * step, (c + 1) * step) for c in range(parts)]

    def score(c):
        return dot_nt(dox[spans[c], :], vals)

    ready = score(0)
    for c in range(parts):
        coming = score(c + 1) if c + 1 < parts else None
        ds[spans[c], :] = e[0, 0, spans[c], :] * ready.astype(bf16)
        d_all[spans[c], :width] = (dot(ds[spans[c], :], keys) * root).astype(bf16)
        ready = coming
    d_all[:ctx_pad, 2 * width:] = dot_tn(back[0], e[0, 0]).T.astype(bf16)
    d_all[:ctx_pad, width:2 * width] = (dot_tn(qkv[0, 0, :, :width], ds[...]) * root).T.astype(bf16)
    d_all[ctx_pad:, width:] = jnp.zeros((pad - ctx_pad, 2 * width), bf16)
    fitted = dot_tn(feats[0], d_all[...])
    pair = dot(d_all[...], w_rows[0])
    made = pair[:, :LANES] + pair[:, LANES:]

    @pl.when(at == 0)
    def _():
        rows_o[0] = d_rows[0] + made

    @pl.when(at > 0)
    def _():
        rows_o[0] += made

    @pl.when(block == 0)
    def _():
        fit[base + at] = fitted

    @pl.when(block > 0)
    def _():
        fit[base + at] += fitted

    @pl.when((block == pl.num_programs(0) - 1) & (at == count - 1))
    def _():
        if not last:
            early_o[...] = fit[...]
        else:
            filled = 0
            for ref in early:
                fit[filled:filled + ref.shape[0]] = ref[...]
                filled += ref.shape[0]
            for turn, ref in enumerate((keep_o, give_o)):
                def lay(p, _):
                    chunk = (turn * (CHUNKS // 2) + p) ^ place[2]
                    rows = pl.ds(pl.multiple_of(chunk // HEADS * 16, 16), 16)
                    head = chunk % HEADS
                    ref[p, :, :3 * width] = fit[head, rows, :].astype(bf16)
                    ref[p, :, 3 * width:] = first[rows, pl.ds(pl.multiple_of(head * width, LANES), width)].astype(bf16)
                    return 0

                lax.fori_loop(0, CHUNKS // 2, lay, 0)


def score_grads(place, start, count, e, qkv, back, feats, w_rows, d_rows, early, first):
    blocks, pad, model = back.shape
    ctx_pad = e.shape[3]
    width = model // HEADS
    parts = row_chunks(pad)
    full = lambda *s: pl.BlockSpec(s, lambda *_: (0,) * len(s))
    rowed = pl.BlockSpec((1, pad, LANES), lambda b, h, *_: (b, 0, 0))
    shape = jax.ShapeDtypeStruct
    last = start + count == HEADS
    late = (*early, first) if last else ()
    ends = [shape((CHUNKS // 2, 16, 4 * width), bf16)] * 2 if last else [shape((count, LANES, 3 * width), f32)]
    return pl.pallas_call(
        functools.partial(scores_kernel, start, last, ctx_pad, parts),
        grid_spec=pltpu.PrefetchScalarGridSpec(
            num_scalar_prefetch=1,
            grid=(blocks, count),
            in_specs=[pl.BlockSpec((1, 1, pad, ctx_pad), lambda b, h, *_: (b, start + h, 0, 0)),
                      pl.BlockSpec((1, 1, pad, 3 * width), lambda b, h, *_: (b, start + h, 0, 0)),
                      pl.BlockSpec((1, pad, width), lambda b, h, *_: (b, 0, start + h)),
                      rowed,
                      pl.BlockSpec((1, 3 * width, 2 * LANES), lambda b, h, *_: (start + h, 0, 0)),
                      rowed] + [full(*a.shape) for a in late],
            out_specs=[full(*end.shape) for end in ends] + [rowed],
            scratch_shapes=[pltpu.VMEM((pad, ctx_pad), bf16), pltpu.VMEM((pad, 2 * width), bf16), pltpu.VMEM((pad, 3 * width), bf16),
                            pltpu.VMEM((HEADS if last else count, LANES, 3 * width), f32)],
        ),
        out_shape=ends + [shape((blocks, pad, LANES), f32)],
        compiler_params=params(0, 0, room=36 << 20),
        cost_estimate=cost(8 * count, 1),
        name="score_grads",
    )(place, e, qkv, back, feats, w_rows, d_rows, *late)


def spread_kernel(span, own, ids, rows, near_o, far_o, *tables):
    blocks = rows.shape[0]
    count, feats, col_width, _ = near_o.shape
    for table in tables:
        table[...] = jnp.zeros_like(table)
    each = len(tables) // blocks if len(tables) > 1 else 1
    run = span // each
    unit = next(u for u in (10, 5, 2, 1) if run % u == 0)

    def add(i, _):
        for u in range(unit):
            for t in range(blocks * each):
                block, at = t // each, t % each * run + i * unit + u
                table = tables[t % len(tables)]
                spot = pl.ds(ids[block * span + at], 1)
                table[spot, :] += rows[block, pl.ds(at, 1), :]
        return 0

    lax.fori_loop(0, run // unit, add, 0)

    def fold(start, out_o, g, _):
        spot = pl.ds(pl.multiple_of((start + g) * own, own), own)
        total = tables[0][spot, :]
        for table in tables[1:]:
            total = total + table[spot, :]
        total = total.T
        for f in range(feats):
            at = f * (col_width + 1)
            out_o[g, f] = total[at:at + col_width].astype(bf16)
        return 0

    for start, out_o in ((0, near_o), (count, far_o)):
        lax.fori_loop(0, count, functools.partial(fold, start, out_o), 0)


def spread(ids, rows, count, feats, col_width, own):
    span = ids.shape[0] // rows.shape[0]
    tables = 4 if count <= 8 and span % 2 == 0 else 1
    return pl.pallas_call(
        functools.partial(spread_kernel, span, own),
        grid_spec=pltpu.PrefetchScalarGridSpec(
            num_scalar_prefetch=1,
            grid=(1,),
            in_specs=[pl.BlockSpec(rows.shape, lambda *_: (0, 0, 0))],
            out_specs=[pl.BlockSpec((count // 2, feats, col_width, own), lambda *_: (0, 0, 0, 0))] * 2,
            scratch_shapes=[pltpu.VMEM((count * own, LANES), f32)] * tables,
        ),
        out_shape=[jax.ShapeDtypeStruct((count // 2, feats, col_width, own), bf16)] * 2,
        compiler_params=params(0, room=(12 << 20) + 16 * count * own * LANES),
        cost_estimate=cost(7, 1),
        name="spread",
    )(ids, rows)


def chosen(p, near, far):
    half = CHUNKS // 2
    at = p % half
    return lambda *spot: jnp.where(p < half, near[(at, *spot)].astype(f32), far[(at, *spot)].astype(f32))


def finish_kernel(place, near, far, near_q, far_q, out_o, in_o, back_o):
    step = pl.program_id(0)
    model = out_o.shape[1]
    each = out_o.shape[0] // 16
    for u in range(each):
        take = chosen((step * each + u) ^ place[0], near, far)
        rows = slice(u * 16, (u + 1) * 16)
        out_o[rows, :] = take(slice(0, 16))
        for j in range(2):
            in_o[rows, j * model:(j + 1) * model] = take(slice(16 + 16 * j, 32 + 16 * j))
        take = chosen((step * each + u) ^ place[1], near_q, far_q)
        back_o[u * 32:(u + 1) * 32, :] = take(slice(None))


def finish(place, *ends):
    model = ends[0].shape[2]
    steps = 4
    shapes = [(model, model), (model, 2 * model), (2 * model, model)]
    return pl.pallas_call(
        finish_kernel,
        grid_spec=pltpu.PrefetchScalarGridSpec(
            num_scalar_prefetch=1,
            grid=(steps,),
            in_specs=[pl.BlockSpec(a.shape, lambda *_: (0, 0, 0)) for a in ends],
            out_specs=[pl.BlockSpec((s[0] // steps, s[1]), lambda i, *_: (i, 0)) for s in shapes],
        ),
        out_shape=[jax.ShapeDtypeStruct(s, f32) for s in shapes],
        compiler_params=params(0, room=16 << 20),
        cost_estimate=cost(5, 1),
        name="finish",
    )(place, *ends)


def finish_tail_kernel(col_width, classes, place, near, far, w_heads, w_all, q_o, k_o, v_o, enc_o, bias_o, mark_o, b_query_o, b_value_o,
                       wide_o, *refs):
    lines, (fit, aug) = refs[:-2], refs[-2:]
    model = q_o.shape[1]
    width = model // HEADS
    for c in range(CHUNKS):
        rows = slice(c // HEADS * 16, c // HEADS * 16 + 16)
        head = c % HEADS
        take = chosen(c ^ place[2], near, far)
        fit[head, rows, :] = take(slice(None), slice(0, 3 * width)).astype(bf16)
        aug[rows, head * width:(head + 1) * width] = take(slice(None), slice(3 * width, None))
    feats = enc_o.shape[0] // col_width
    ones = feats * (col_width + 1) + classes
    for row in range(6):
        lines[row][...] = aug[SMALLS + row:SMALLS + row + 1, :]
    for j in range(2):
        wide_o[:, j * model:(j + 1) * model] = aug[SMALLS + 6 + j:SMALLS + 7 + j, :]
    kind = lax.broadcasted_iota(jnp.int32, (LANES, 3 * width), 0)
    total = aug[...]
    for head in range(HEADS):
        cols = slice(head * width, (head + 1) * width)
        part = fit[head]
        total = total + dot(part, w_heads[head])
        line = part[ones:ones + 1, :].astype(f32)
        b_query_o[:, cols] = line[:, :width]
        b_value_o[:, cols] = line[:, 2 * width:]
        spread_line = jnp.where((kind > ones) & (kind < ones + 3), line, part.astype(f32)).astype(bf16)
        made = dot_tn(w_all[...], spread_line)
        for j, ref in enumerate((q_o, k_o, v_o)):
            ref[:, cols] = made[:, j * width:(j + 1) * width]
    aug[...] = total
    for f in range(feats):
        enc_o[f * col_width:(f + 1) * col_width, :] = aug[f * (col_width + 1):f * (col_width + 1) + col_width, :]
    mark_o[...] = aug[ones - classes:ones, :]
    bias_o[...] = aug[ones:ones + 1, :]


def finish_tail(place, near, far, w_heads, w_all, feat_total, col_width, classes):
    model = w_all.shape[1]
    width = model // HEADS
    shapes = [(model, model)] * 3 + [(feat_total, model), (1, model), (classes, model), (1, model), (1, model), (1, 2 * model)]
    shapes = shapes + [(1, model)] * 6
    full = lambda *s: pl.BlockSpec(s, lambda *_: (0,) * len(s))
    return pl.pallas_call(
        functools.partial(finish_tail_kernel, col_width, classes),
        grid_spec=pltpu.PrefetchScalarGridSpec(
            num_scalar_prefetch=1,
            grid=(1,),
            in_specs=[full(*a.shape) for a in (near, far, w_heads, w_all)],
            out_specs=[full(*s) for s in shapes],
            scratch_shapes=[pltpu.VMEM((HEADS, LANES, 3 * width), bf16), pltpu.VMEM((LANES, model), f32)],
        ),
        out_shape=[jax.ShapeDtypeStruct(s, f32) for s in shapes],
        compiler_params=params(0, room=20 << 20),
        cost_estimate=cost(5, 1),
        name="finish_tail",
    )(place, near, far, w_heads, w_all)


CALLS = ((0, 2), (2, 2))


def swap(value, axis, bit):
    size = lax.axis_size(axis)
    return lax.ppermute(value, axis, [(i, i ^ bit) for i in range(size)])


def rounded(value):
    return lax.reduce_precision(value, 8, 7)


def exchange(value, axis):
    return lax.all_to_all(value, axis, split_axis=0, concat_axis=0, tiled=True)


def added(*values):
    return sum((value.astype(f32) for value in values[1:]), values[0].astype(f32))


def reduce_chunks(keep, give, cut):
    over_core, over_x, over_y = ("feat", 1), ("feat", 2), ("rows", 1)
    came = swap(give, *over_core)
    half = keep.shape[0] // 2
    both = []
    for rows, first, then in ((slice(None, cut), over_x, over_y), (slice(cut, None), over_y, over_x)):
        mine, theirs = added(keep[:half, rows], came[:half, rows]), added(keep[half:, rows], came[half:, rows]).astype(bf16)
        both.append((mine, theirs, first, then))
    yield both[0][1]
    half = half // 2
    last = []
    for mine, theirs, first, then in both:
        came = swap(theirs, *first)
        last.append((added(mine[:half], came[:half]), added(mine[half:], came[half:]).astype(bf16), then))
    yield last[0][1]
    total = jnp.concatenate([added(mine, swap(theirs, *then)) for mine, theirs, then in last], 1).astype(bf16)
    yield total
    own = added(total[0], *[swap(total[at], "rows", 2 * at) for at in range(1, half)]).astype(bf16)
    for bit in range(3, lax.axis_size("rows").bit_length() - 1):
        own = added(own, swap(own, "rows", 1 << bit)).astype(bf16)
    yield own


def gather_chunks(own, cut):
    over_core, over_x, over_y = ("feat", 1), ("feat", 2), ("rows", 1)
    own = jnp.stack([own] + [swap(own, "rows", 2 * at) for at in range(1, 4)])
    parts = []
    for rows, first, then in ((slice(None, cut), over_x, over_y), (slice(cut, None), over_y, over_x)):
        part = own[:, rows]
        parts.append((jnp.concatenate([part, swap(part, *then)], 0), first))
    near = [jnp.concatenate([part, swap(part, *first)], 0) for part, first in parts]
    return near[0], swap(near[0], *over_core), near[1], swap(near[1], *over_core)


def tail_first(keep, give):
    half = keep.shape[0] // 2
    came = swap(give, "feat", 1)
    return added(keep[:half], came[:half]), added(keep[half:], came[half:]).astype(bf16)


def body(
    raw_rows, enc_weight, enc_bias, label_table, w_query, b_query, w_key, w_value, b_value, w_out, b_out,
    gain_one, shift_one, w_in, b_in, w_back, b_back, gain_two, shift_two, members, labels, queries, cotangent,
):
    row_count = lax.axis_size("rows")
    feat_count = lax.axis_size("feat")
    row_index = lax.axis_index("rows")
    feat_index = lax.axis_index("feat")
    local_rows, col_width = raw_rows.shape
    own_rows = local_rows // feat_count
    feat_total = col_width * feat_count
    feat_span = feat_total + feat_count
    model = enc_weight.shape[1]
    width = model // HEADS
    classes = label_table.shape[0]
    blocks, span = members.shape
    ctx_len = labels.shape[1]
    pad = round_up(span, 16)
    row_total = float(local_rows * row_count)
    core, over, up, along = feat_index % 2, feat_index // 2, row_index % 2, row_index // 2 % 4
    place = jnp.stack([core * 16 + over * 8 + up * 4 + along, core * 16 + up * 8 + over * 4 + along, core * 16 + over * 8])
    place = place.astype(jnp.int32)
    row = lambda a: a.reshape(1, -1)

    columns = raw_rows.T
    origin = rounded(jnp.mean(columns, 1, keepdims=True))
    moved = columns - origin
    sums = [origin[:, 0]]
    for value, scales in ((jnp.mean(moved, 1), (1.0, 1024.0, 1048576.0)), (jnp.mean(moved * moved, 1), (0.0625, 64.0, 65536.0))):
        for scale in scales:
            top = lax.reduce_precision(value * scale, 5, 10)
            sums.append(top)
            value = value - top / scale
    moved = moved * SPAN
    notes = jnp.pad(jnp.stack(sums), ((0, 1), (0, 32 - col_width))).reshape(1, 1, 2 * LANES)
    notes = jnp.broadcast_to(jnp.pad(notes, ((0, 0), (0, 0), (0, own_rows - 2 * LANES))), (feat_count, 1, own_rows))
    moved = moved.reshape(col_width, feat_count, own_rows).transpose(1, 0, 2)
    sent = jnp.concatenate([moved, notes], 1).astype(jnp.float16)
    owned = exchange(sent, "feat").reshape(1, feat_span, own_rows)
    near = jnp.concatenate([owned] + [swap(owned, "rows", bits) for bits in (2, 4, 6)], 0)
    for bit in range(3, row_count.bit_length() - 1):
        near = jnp.concatenate([near, swap(near, "rows", 1 << bit)], 0)
    far = swap(near, "rows", 1)
    source = members // local_rows
    source = source ^ row_index
    source = ((source >> 1) & 3) + 4 * (source >> 3) + (source & 1) * (row_count // 2)
    ids = (source * own_rows + members % own_rows).reshape(-1)

    spaced = jnp.pad(enc_weight.reshape(feat_count, col_width, model), ((0, 0), (0, 1), (0, 0))).reshape(feat_span, model)
    w_feat = jnp.pad(spaced, ((0, LANES - feat_span), (0, 0)))
    w_mark = jnp.pad(label_table, ((feat_span, LANES - feat_span - classes), (0, 0)))
    b_enc = row(enc_bias)
    w_embed = jnp.concatenate([w_feat, w_mark], 1)
    terms, left = [], enc_bias
    for _ in range(3):
        terms.append(rounded(left))
        left = left - terms[-1]
    ones = feat_span + classes
    w_all = (w_feat + w_mark).at[ones:ones + 3].set(jnp.stack(terms).astype(bf16))
    marks = jnp.pad(labels, ((0, 0), (0, pad - ctx_len)), constant_values=-1)
    cut = lambda w: w.reshape(model, HEADS, 1, width)
    w_qkv = jnp.concatenate([cut(w_query), cut(w_key), cut(w_value)], 2).reshape(model, 3 * model)
    edge = lambda b: b.reshape(1, HEADS, 1, width)
    b_qkv = jnp.concatenate([edge(b_query), edge(jnp.zeros_like(b_query)), edge(b_value)], 2).reshape(1, 3 * model)
    w_heads = w_qkv.T.reshape(HEADS, 3 * width, model)
    w_feat_t = w_feat.T
    w_rows = jnp.einsum("hkd,df->hkf", w_heads, w_feat_t, preferred_element_type=f32)
    high = rounded(w_rows)
    w_rows = jnp.concatenate([high, w_rows - high], 2).astype(bf16)
    tiles = model // LANES
    flat = cotangent.transpose(1, 0, 2).reshape(span, blocks, tiles, LANES).transpose(0, 2, 1, 3).reshape(-1, LANES)

    feats, stats = fetch(ids, near.astype(f32), far.astype(f32), marks, feat_count, classes)
    stats = lax.dynamic_slice_in_dim(stats, feat_index * (col_width + 1), col_width, 1)
    col_mean, factor = stats[0], stats[1]
    w_out_t = jnp.concatenate([w_out.T, w_feat_t], 1)
    weights = (w_embed, b_enc, w_qkv, b_qkv, w_out, row(b_out), row(gain_one), row(shift_one), w_in, row(b_in),
               w_back, row(b_back), row(gain_two), row(shift_two), w_out_t)
    qkv, expo, layer_out, d_rows, back, keep, give, first = forward(place, queries, feats, flat, weights, ctx_len)
    layer_out = layer_out.reshape(span, tiles, blocks, LANES).transpose(0, 2, 1, 3).reshape(span, blocks, model).transpose(1, 0, 2)

    steps = reduce_chunks(keep, give, 48)
    early = []
    for start, count in CALLS:
        held, back = lax.optimization_barrier((next(steps), back))
        *made, d_rows = score_grads(place, start, count, expo, qkv, back, feats, w_rows, d_rows, early, first)
        early.append(made[0])
    held, d_rows = lax.optimization_barrier((next(steps), d_rows))
    near, far = spread(ids, d_rows, row_count, feat_count, col_width, own_rows)
    own, (keep, give) = next(steps), tail_first(*made)
    give, near, far = lax.optimization_barrier((give, near, far))
    total = added(keep, swap(give, "feat", 2)).astype(bf16)
    d_table = added(near, swap(far, "rows", 1))
    total = added(total, swap(total, "rows", 2)).astype(bf16)
    total, d_table = lax.optimization_barrier((total, d_table))
    for bit in range(row_count.bit_length() - 2, 2, -1):
        half = d_table.shape[0] // 2
        d_table = added(d_table[:half], swap(d_table[half:].astype(bf16), "rows", 1 << bit))
        total = added(total, swap(total, "rows", 1 << bit)).astype(bf16)
    d_low = d_table.astype(bf16)
    d_own = added(d_table[0], *[swap(d_low[at], "rows", 2 * at) for at in range(1, 4)]).astype(bf16)
    for bit in (4, 1):
        total = added(total, swap(total, "rows", bit)).astype(bf16)
    t_near = jnp.concatenate([total, swap(total, "feat", 2)], 0)
    t_far = swap(t_near, "feat", 1)
    d_columns = exchange(d_own, "feat").astype(f32)
    d_columns = d_columns.transpose(1, 0, 2).reshape(col_width, local_rows)
    (g_query, g_key, g_value, g_enc, g_enc_bias, g_table, g_b_query, g_b_value, g_b_in, g_b_out, g_gain_one, g_shift_one,
     g_b_back, g_gain_two, g_shift_two) = finish_tail(place, t_near, t_far, w_heads, w_all, feat_total, col_width, classes)
    ends = gather_chunks(own, 48)
    g_out, g_in, g_back = finish(place, *ends)

    at = feat_index * col_width
    weight = lax.dynamic_slice_in_dim(enc_weight, at, col_width, 0).astype(f32)
    stat_one = jnp.sum(weight * g_enc_bias, 1)
    stat_two = jnp.sum(weight * lax.dynamic_slice_in_dim(g_enc, at, col_width, 0), 1)
    d_spread = -0.5 * stat_two * factor * factor
    d_mean = -factor * stat_one - 2.0 * d_spread * col_mean
    raw_grad = factor[:, None] * d_columns + (d_mean[:, None] + 2.0 * d_spread[:, None] * columns) / row_total
    flatten = lambda a: a.reshape(-1)
    return (
        layer_out, raw_grad.T, g_enc, flatten(g_enc_bias), g_table, g_query, flatten(g_b_query), g_key, g_value,
        flatten(g_b_value), g_out, flatten(g_b_out), flatten(g_gain_one), flatten(g_shift_one), g_in, flatten(g_b_in), g_back,
        flatten(g_b_back), flatten(g_gain_two), flatten(g_shift_two),
    )


def solution(mesh):
    both = ("rows", "feat")
    placed = (P("rows", "feat"),) + (P(),) * 18 + (P(both, None), P(both, None), P(both), P(both, None, None))
    results = (P(both, None, None), P("rows", "feat")) + (P(),) * 18
    return jax.shard_map(body, mesh=mesh, in_specs=placed, out_specs=results, check_vma=False)
```
